128 devices in a mesh: section: 2 (over y_lo), dp: 64 (over y_hi, z, x, core).
Axes of the slice: x: 4, y: 4 (y_hi: 2, y_lo: 2; y = y_hi * 2 + y_lo), z: 4, core: 2. Of those that a mesh axis runs over, the one named last changes fastest.
Arguments:
- tokens: bfloat16 [32768, 768], P('dp'), may hold values from -6 to 6
- segment_ids: int32 [32768], P('dp'), may hold values from 0 to 255, never falling along the last dimension, each value on 1 to 256 neighbouring positions
- depth: int32 [64], P('dp'), may hold values from 6 to 12, as said below
- input_weight: float32 [2, 768, 2304], P('section', 'dp'), may hold values from -0.21875 to 0.21875
- input_bias: float32 [2, 1536], P('section', 'dp'), may hold values from -3 to 3
- output_weight: float32 [2, 768, 768], P('section', 'dp'), may hold values from -0.625 to 0.625
- output_bias: float32 [2, 768], P('section', 'dp'), may hold values from -3 to 3
- first_gain: float32 [2, 768], P('section', 'dp'), may hold values from 0.5 to 1.5
- first_shift: float32 [2, 768], P('section', 'dp'), may hold values from -3 to 3
- expand_weight: float32 [2, 768, 3072], P('section', 'dp'), may hold values from -0.21875 to 0.21875
- expand_bias: float32 [2, 3072], P('section', 'dp'), may hold values from -3 to 3
- contract_weight: float32 [2, 3072, 768], P('section', 'dp'), may hold values from -0.15625 to 0.15625
- contract_bias: float32 [2, 768], P('section', 'dp'), may hold values from -3 to 3
- second_gain: float32 [2, 768], P('section', 'dp'), may hold values from 0.5 to 1.5
- second_shift: float32 [2, 768], P('section', 'dp'), may hold values from -3 to 3
- cotangent: bfloat16 [32768, 768], P('dp'), may hold values from -6 to 6
Outputs:
- layer_outputs: bfloat16 [2, 32768, 768], P('section', 'dp')
- input_grads: bfloat16 [2, 32768, 768], P('section', 'dp')
- input_weight_grad: float32 [2, 768, 2304], P('section', 'dp')
- input_bias_grad: float32 [2, 1536], P('section', 'dp')
- output_weight_grad: float32 [2, 768, 768], P('section', 'dp')
- output_bias_grad: float32 [2, 768], P('section', 'dp')
- first_gain_grad: float32 [2, 768], P('section', 'dp')
- first_shift_grad: float32 [2, 768], P('section', 'dp')
- expand_weight_grad: float32 [2, 768, 3072], P('section', 'dp')
- expand_bias_grad: float32 [2, 3072], P('section', 'dp')
- contract_weight_grad: float32 [2, 3072, 768], P('section', 'dp')
- contract_bias_grad: float32 [2, 768], P('section', 'dp')
- second_gain_grad: float32 [2, 768], P('section', 'dp')
- second_shift_grad: float32 [2, 768], P('section', 'dp')
The draws below stay inside these ranges and needn't reach their ends.
Inputs may be any that keep to these rules, and one draw needn't show every extreme that they name: Each group's depth is 6, 9 or 12; some group has 12 and some has 6.
All inputs are finite; a program needn't handle non-finite values.
Results may differ from the reference program's by a relative error of at most 0.014.
Values may be sent and summed in bfloat16 or wider, within the bound.
No kernel may reach another device: no remote copies, remote signals or barrier semaphores. Data moves between devices by JAX's collectives and lax.ppermute only.
A program may use at most 384 MiB of HBM per device.

```python
import math
import jax
import jax.numpy as jnp
import numpy as np
from jax import lax

D = 768
HEADS = 12
HD = 64
FF = 3072
MICRO = 2
MB_ROWS = 256
GROUPS = 64
TOKENS = 32768
DOCS = 256


def draw_depth(key, part):
    key = jax.random.fold_in(key, 7)
    level_key, order_key = jax.random.split(key)
    levels = 6 + 3 * jax.random.randint(level_key, (GROUPS,), 0, 3)
    order = jax.random.permutation(order_key, GROUPS)
    levels = levels.at[order[0]].set(12).at[order[1]].set(6)
    return levels.astype(jnp.int32)


def shard_levels(own_key, dims, shards, least, top_value):
    factor_of, own = 1.0, jax.random.fold_in(own_key, 6)
    for position, blocks in shards:
        draws = jnp.exp(jax.random.uniform(jax.random.fold_in(own, position), (blocks,), jnp.float32, least / len(shards), top_value / len(shards)))
        factor_of = factor_of * jnp.repeat(draws, dims[position] // blocks).reshape([-1 if axis == position else 1 for axis in range(len(dims))])
    return factor_of


def length_profile(number_of, total, limit, slope):
    portions = [(1 << 20) // math.isqrt(grade ** slope) + 1 for grade in range(2, number_of + 1)]
    rest, given = total - limit - (number_of - 1), [1] * (number_of - 1)
    while rest > 0:
        free = [i for i in range(number_of - 1) if given[i] < limit]
        mass, remaining = sum([portions[i] for i in free]), rest
        for i in free:
            extra = min(limit - given[i], max(1, remaining * portions[i] // mass), rest)
            given[i] = given[i] + extra
            rest = rest - extra
    return np.array([limit] + given)


def uneven_parts(own_key, count, total, most, skew):
    if count == 2:
        one = jax.random.randint(own_key, (), max(1, total - most), min(most, total - 1) + 1)
        return jnp.stack([one, total - one])
    tallies = jnp.asarray(length_profile(count, total, most, skew), jnp.int32)
    twos = (count - 1) // 2
    giver, taker = tallies[1:1 + 2 * twos:2], tallies[2:2 + 2 * twos:2]
    room = jnp.minimum(giver - 1, most - taker)
    moved = jax.random.randint(jax.random.fold_in(own_key, 1), (twos,), 0, 1 << 20) % (room + 1)
    tallies = tallies.at[1:1 + 2 * twos:2].set(giver - moved).at[2:2 + 2 * twos:2].set(taker + moved)
    return tallies[jax.random.permutation(jax.random.fold_in(own_key, 2), count)]


def scatter_about(rng, extent, width, limit, cuts=(), held_as=jnp.bfloat16):
    level = shard_levels(rng, extent, cuts, -0.22, 0.18) if cuts else 1.0
    values = jax.random.normal(rng, extent, jnp.float32) * width * level
    return jnp.minimum(jnp.maximum(values, -limit), limit).astype(held_as)


def setup_inputs(seed: int = 0) -> dict:
    streams_of = jax.random.split(jax.random.key(seed), 17)
    return {
        "tokens": scatter_about(streams_of[0], (TOKENS, D), 1.0, 6.0, ((0, 64),)),
        "segment_ids": jnp.searchsorted(jnp.cumsum(uneven_parts(streams_of[1], DOCS, TOKENS, MB_ROWS, 2)), jnp.arange(TOKENS), side="right").astype(jnp.int32),
        "depth": draw_depth(jax.random.fold_in(streams_of[16], 71), 0),
        "input_weight": scatter_about(streams_of[3], (2, D, 3 * D), D ** -0.5, 0.21875, ((0, 2), (1, 64)), jnp.float32),
        "input_bias": scatter_about(streams_of[4], (2, 2 * D), 0.5, 3.0, ((0, 2), (1, 64)), jnp.float32),
        "output_weight": scatter_about(streams_of[5], (2, D, D), (D // 8) ** -0.5, 0.625, ((0, 2), (1, 64)), jnp.float32),
        "output_bias": scatter_about(streams_of[6], (2, D), 0.5, 3.0, ((0, 2), (1, 64)), jnp.float32),
        "first_gain": jnp.clip(1.0 + 0.1 * jax.random.normal(streams_of[7], (2, D), jnp.float32), 0.5, 1.5),
        "first_shift": scatter_about(streams_of[8], (2, D), 0.5, 3.0, ((0, 2), (1, 64)), jnp.float32),
        "expand_weight": scatter_about(streams_of[9], (2, D, FF), D ** -0.5, 0.21875, ((0, 2), (1, 64)), jnp.float32),
        "expand_bias": scatter_about(streams_of[10], (2, FF), 0.5, 3.0, ((0, 2), (1, 64)), jnp.float32),
        "contract_weight": scatter_about(streams_of[11], (2, FF, D), (FF // 2) ** -0.5, 0.15625, ((0, 2), (1, 64)), jnp.float32),
        "contract_bias": scatter_about(streams_of[12], (2, D), 0.5, 3.0, ((0, 2), (1, 64)), jnp.float32),
        "second_gain": jnp.clip(1.0 + 0.1 * jax.random.normal(streams_of[13], (2, D), jnp.float32), 0.5, 1.5),
        "second_shift": scatter_about(streams_of[14], (2, D), 0.5, 3.0, ((0, 2), (1, 64)), jnp.float32),
        "cotangent": scatter_about(streams_of[15], (TOKENS, D), 1.0, 6.0, ((0, 64),)),
    }


epsilon = 1e-05

@jax.custom_vjp
def low(v):
    return lax.optimization_barrier(v.astype(jnp.bfloat16)).astype(jnp.float32)

@jax.custom_vjp
def low_back(v):
    return v

def low_keep(v):
    return (low(v), None)

def low_pass(kept, grad):
    return (grad,)

def back_keep(v):
    return (v, None)

def back_low(kept, grad):
    return (low(grad),)
low.defvjp(low_keep, low_pass)
low_back.defvjp(back_keep, back_low)

def mult(left, right):
    return jnp.dot(left, right, precision=lax.Precision.HIGHEST, preferred_element_type=jnp.float32)

def layer_norm(residual, gain_row, offset):
    centre = residual - lax.optimization_barrier(jnp.mean(residual, axis=-1, keepdims=True))
    variance = lax.optimization_barrier(jnp.mean(centre * centre, axis=-1, keepdims=True))
    return centre * lax.rsqrt(variance + epsilon) * gain_row + offset

def encoder_layer(rows_in, segments, weights):
    input_weight, input_bias, output_weight, output_bias, first_gain, first_shift, expand_weight, expand_bias, contract_weight, contract_bias, second_gain, second_shift = weights
    row_count = rows_in.shape[0]
    full_bias = jnp.concatenate([input_bias[:D], jnp.zeros((D,), jnp.float32), input_bias[D:]])
    projected = low_back(low(mult(rows_in, input_weight) + full_bias))
    queries = projected[:, :D].reshape(row_count, HEADS, HD)
    keys_part = projected[:, D:2 * D].reshape(row_count, HEADS, HD)
    values_part = projected[:, 2 * D:].reshape(row_count, HEADS, HD)
    score_scale = HD ** (-0.5)
    scores = low_back(jnp.einsum('qhd,khd->hqk', queries, keys_part, precision=lax.Precision.HIGHEST) * score_scale)
    same_doc = segments[:, None] == segments[None, :]
    scores = jnp.where(same_doc[None], scores, -1e+30)
    row_max = lax.optimization_barrier(jnp.max(scores, axis=2, keepdims=True))
    exponent = jnp.exp(scores - row_max)
    softmax_rows = exponent / lax.optimization_barrier(jnp.sum(exponent, axis=2, keepdims=True))
    attended = jnp.einsum('hqk,khd->qhd', low(softmax_rows), values_part, precision=lax.Precision.HIGHEST).reshape(row_count, D)
    attended = low_back(low(attended))
    branch = low_back(mult(attended, output_weight) + output_bias)
    hidden = low(layer_norm(rows_in + branch, first_gain, first_shift))
    pre_act = low_back(mult(hidden, expand_weight) + expand_bias)
    activated = low(jax.nn.gelu(pre_act, approximate=False))
    ffn_out = low_back(mult(activated, contract_weight) + contract_bias)
    return layer_norm(hidden + ffn_out, second_gain, second_shift)

def reference(tokens, segment_ids, depth, input_weight, input_bias, output_weight, output_bias, first_gain, first_shift, expand_weight, expand_bias, contract_weight, contract_bias, second_gain, second_shift, cotangent):
    masters = (input_weight, input_bias, output_weight, output_bias, first_gain, first_shift, expand_weight, expand_bias, contract_weight, contract_bias, second_gain, second_shift)
    inputs = tokens.astype(jnp.float32).reshape(-1, MB_ROWS, D)
    segment_rows = segment_ids.reshape(-1, MB_ROWS)
    keep_rows = jnp.repeat(depth > 9, MICRO)
    delta_rows = jnp.zeros_like(inputs)

    def forward_all(inputs, delta_rows, masters):
        low_weights = tuple((low(master) for master in masters))
        first_layer = tuple((weight[0] for weight in low_weights))
        second_layer = tuple((weight[1] for weight in low_weights))

        def one_block(operands):
            rows_block, segments, keep_one, delta_one = operands
            middle = encoder_layer(rows_block, segments, first_layer)
            passed = low_back(low(middle)) + delta_one
            last_out = jnp.where(keep_one, encoder_layer(passed, segments, second_layer), passed)
            return (middle, last_out)
        return lax.map(jax.checkpoint(one_block), (inputs, segment_rows, keep_rows, delta_rows))
    (middles, finals), pullback = jax.vjp(forward_all, inputs, delta_rows, masters)
    grad_last = cotangent.astype(jnp.float32).reshape(-1, MB_ROWS, D)
    grad_inputs, grad_delta, grad_masters = pullback((jnp.zeros_like(middles), grad_last))
    layer_outputs = jnp.stack([middles.reshape(-1, D), finals.reshape(-1, D)]).astype(jnp.bfloat16)
    input_grads = jnp.stack([grad_inputs.reshape(-1, D), grad_delta.reshape(-1, D)]).astype(jnp.bfloat16)
    return (layer_outputs, input_grads, grad_masters[0], grad_masters[1], grad_masters[2], grad_masters[3], grad_masters[4], grad_masters[5], grad_masters[6], grad_masters[7], grad_masters[8], grad_masters[9], grad_masters[10], grad_masters[11])
```

```python
import jax
import jax.numpy as jnp
from jax import lax
from jax.experimental import pallas as pl
from jax.experimental.pallas import tpu as pltpu
from jax.sharding import Mesh, PartitionSpec as P

D = 768
HEADS = 12
BLOCK = 256
EPS = 1e-05
Y = ("section", "yh")
ROWS = 96
BF = jnp.bfloat16
F32 = jnp.float32


def position(axis):
    if isinstance(axis, tuple):
        return lax.axis_index("yh") * 2 + lax.axis_index("section")
    return lax.axis_index(axis)


def size_of(axis):
    return 4 if isinstance(axis, tuple) else lax.axis_size(axis)


def ahead(value, axis, steps):
    count = size_of(axis)
    at = [0, 2, 1, 3] if isinstance(axis, tuple) else range(count)
    return lax.ppermute(value, axis, [(at[i], at[(i + steps) % count]) for i in range(count)])


def from_behind(value, axis):
    return [value] + [ahead(value, axis, k) for k in (1, 2, 3)]


def by_position(pieces, here):
    rising = [pieces[0], pieces[3], pieces[2], pieces[1]]
    return lax.dynamic_slice_in_dim(jnp.stack(rising + rising), (4 - here) % 4, 4, 0)


def ahead_crossed(value, steps, first):
    pairs = []
    for y in range(4):
        for z in range(4):
            for c in range(2):
                to_y, to_z = ((y + steps) % 4, z) if c == first else (y, (z + steps) % 4)
                pairs.append(
                    (
                        (((y % 2) * 2 + y // 2) * 4 + z) * 2 + c,
                        (((to_y % 2) * 2 + to_y // 2) * 4 + to_z) * 2 + c,
                    )
                )
    return lax.ppermute(value, ("section", "yh", "z", "core"), pairs)


def swap_core(value):
    return ahead(value, "core", 1)


def behind(axis, k):
    return lax.rem(position(axis) + (4 - k), 4)


class Chunks:
    def __init__(self, to, sems):
        self.to, self.sems, self.here = to, sems, set()

    def bring(self, source, block, z):
        block = block * 4 + z
        rows = pl.ds(pl.multiple_of(block * ROWS, ROWS), ROWS)
        for j in range(4):
            pltpu.make_async_copy(
                source.at[pl.ds(j * ROWS, ROWS), :], self.to.at[j, rows, :], self.sems.at[j, block]
            ).start()

    def get(self, j):
        for block in range(0 if j in self.here else 8):
            here = self.to.at[j, pl.ds(block * ROWS, ROWS), :]
            pltpu.make_async_copy(here, here, self.sems.at[j, block]).wait()
        self.here.add(j)
        return self.to[j]


def attention_chunks(layer, pieces, to, sems, vraw=None, sem_v=None):
    chunks = Chunks(to, sems)
    core = lax.axis_index("core")
    for r in range(2):

        @pl.when(core == r)
        def _():
            for k in range(4):
                z = behind("z", k)
                for yh in range(2):
                    piece = pieces[r * 8 + layer * 4 + k].at[yh]
                    if vraw is not None:
                        pltpu.make_async_copy(
                            piece.at[pl.ds(4 * ROWS, 16), :], vraw.at[yh, z], sem_v.at[yh, z]
                        ).start()
                    chunks.bring(piece, yh, z)

    return chunks


def expand_chunks(layer, pieces, to, sems):
    chunks = Chunks(to, sems)
    core = lax.axis_index("core")
    for k in range(4):
        ys = behind(Y, k)
        for r in range(2):

            @pl.when(jnp.logical_and(lax.rem(ys, 2) == layer, core == 1 - r))
            def _():
                for h in range(2):
                    for zh in range(2):
                        chunks.bring(pieces[r * 8 + h * 4 + k].at[zh], ys // 2, 2 * zh + h)

    return chunks


class Contract:
    def __init__(self, layer, pieces, to, sems):
        self.to, self.sems, self.here = to, sems, set()
        core = lax.axis_index("core")
        for j in range(4):
            yh, z = j // 2, pl.ds((j % 2) * 2, 2)
            for r in range(2):
                for x in range(4):
                    pltpu.make_async_copy(
                        pieces[r].at[x, z, yh * 2 + layer],
                        to.at[yh, z, x, core if r == 0 else 1 - core],
                        sems.at[j, core if r == 0 else 1 - core, x],
                    ).start()

    def get(self, j):
        yh, first = j // 2, (j % 2) * 2
        for r in range(0 if j in self.here else 2):
            for x in range(4):
                here = self.to.at[yh, pl.ds(first, 2), x, r]
                pltpu.make_async_copy(here, here, self.sems.at[j, r, x]).wait()
        self.here.add(j)
        return self.to[yh, first : first + 2].reshape(D, D)


class Out:
    def __init__(self, sems):
        self.sems, self.copies = sems, []

    def put(self, source, to):
        copy = pltpu.make_async_copy(source, to, self.sems.at[len(self.copies)])
        copy.start()
        self.copies.append(copy)

    def drain(self):
        for copy in self.copies:
            copy.wait()


WA = pltpu.VMEM((4, D, D), BF)
WC = pltpu.VMEM((2, 4, 4, 2, 48, D), BF)
FOUR = pltpu.VMEM((4, BLOCK, D), BF)


def dma(*count):
    return pltpu.SemaphoreType.DMA(count)


def dot(left, right):
    return lax.dot_general(left, right, (((1,), (0,)), ((), ())), preferred_element_type=F32)


def dot_nt(left, right):
    return lax.dot_general(left, right, (((1,), (1,)), ((), ())), preferred_element_type=F32)


def dot_tn(left, right):
    return lax.dot_general(left, right, (((0,), (0,)), ((), ())), preferred_element_type=F32)


def norm_of(residual):
    centre = residual - jnp.mean(residual, axis=1, keepdims=True)
    scaled = lax.rsqrt(jnp.mean(centre * centre, axis=1, keepdims=True) + EPS)
    return centre * scaled, scaled


def norm_back(grad_out, normed, scaled, gain):
    grad_normed = grad_out * gain
    inner = (
        grad_normed
        - jnp.mean(grad_normed, axis=1, keepdims=True)
        - normed * jnp.mean(grad_normed * normed, axis=1, keepdims=True)
    )
    return (
        scaled * inner,
        jnp.sum(grad_out * normed, axis=0, keepdims=True),
        jnp.sum(grad_out, axis=0, keepdims=True),
    )


def head_masks():
    lane = lax.broadcasted_iota(jnp.int32, (BLOCK, 128), 1)
    return lane < 64


def vector_rows(vraw, out):
    groups = [vraw[yh, z][0:8, :256].astype(F32) for yh in range(2) for z in range(4)]
    values = jnp.concatenate(groups, axis=0).astype(BF)
    lane = lax.broadcasted_iota(jnp.int32, (64, D), 1)
    device = lax.broadcasted_iota(jnp.int32, (64, D), 0)

    def rows(start, width, count):
        found = []
        for r in range(count):
            spread = jnp.where(device == (lane + r * D) // width, 1.0, 0.0).astype(BF)
            wide = dot_tn(values[:, start : start + width], spread)
            entry = lax.broadcasted_iota(jnp.int32, wide.shape, 0)
            at = lax.broadcasted_iota(jnp.int32, wide.shape, 1) + r * D
            found.append(
                jnp.sum(jnp.where(entry == at % width, wide, 0.0), axis=0, keepdims=True)
            )
        return found

    found = rows(0, 24, 2)
    for start in (24, 36, 48):
        found += rows(start, 12, 1)
    found += rows(60, 48, 4)
    for start in (108, 120, 132):
        found += rows(start, 12, 1)
    out[...] = jnp.concatenate(found + [jnp.zeros((4, D), F32)], axis=0)


def column_sum(values):
    return jnp.sum(values.astype(F32), axis=0, keepdims=True)


def attention_forward(u, joined, vec, weights, qkv, probs, both, normed, scaled):
    q = ((dot(u, weights.get(0)) + vec[0:1]) * 0.125).astype(BF)
    k = dot(u, weights.get(1)).astype(BF)
    v = (dot(u, weights.get(2)) + vec[1:2]).astype(BF)
    qkv[0] = q
    qkv[1] = k
    qkv[2] = v
    low_half = head_masks()
    for pair in range(HEADS // 2):
        lanes = slice(pair * 128, pair * 128 + 128)
        q2, k2, v2 = q[:, lanes], k[:, lanes], v[:, lanes]
        outs = []
        for h in range(2):
            mine = low_half if h == 0 else jnp.logical_not(low_half)
            scores = dot_nt(jnp.where(mine, q2, jnp.zeros_like(q2)), k2)
            scores = jnp.where(joined, scores, -1e30)
            top = jnp.max(scores, axis=1, keepdims=True)
            exponent = jnp.exp(scores - top)
            total = jnp.sum(exponent, axis=1, keepdims=True)
            rows = (exponent / total).astype(BF)
            probs[2 * pair + h] = rows
            outs.append(dot(rows, v2))
        both[1, :, lanes] = jnp.where(low_half, outs[0], outs[1]).astype(BF)
    branch = dot(both[1], weights.get(3)) + vec[2:3]
    n1, s1 = norm_of(u.astype(F32) + branch)
    normed[...] = n1
    scaled[...] = jnp.broadcast_to(s1, (BLOCK, 128))
    return (n1 * vec[3:4] + vec[4:5]).astype(BF)


def ffn_forward(hidden, vec, expand, contract, act, slope, normed, scaled):
    for j in range(4):
        pre = dot(hidden, expand.get(j)) + vec[5 + j : 6 + j]
        half = 0.5 * (1.0 + lax.erf(pre * 0.7071067811865476))
        act[j] = (pre * half).astype(BF)
        slope[j] = (half + pre * jnp.exp(-0.5 * pre * pre) * 0.3989422804014327).astype(BF)
    total = hidden.astype(F32) + vec[9:10]
    for j in range(4):
        total = total + dot(act[j], contract.get(j))
    n2, s2 = norm_of(total)
    normed[...] = n2
    scaled[...] = jnp.broadcast_to(s2, (BLOCK, 128))
    return n2 * vec[10:11] + vec[11:12]


def ffn_backward(grad, vec, n2, s2, slope, expand, contract, vecs, dffn_ref, dpre_ref):
    dr2, dgain, dshift = norm_back(grad, n2[...], s2[:, 0:1], vec[10:11])
    dffn = dr2.astype(BF)
    dffn_ref[...] = dffn
    vecs[...] = jnp.zeros((16, D), F32)
    vecs[9:10] = column_sum(dffn)
    vecs[10:11] = dgain
    vecs[11:12] = dshift
    for j in range(4):
        dact = dot_nt(dffn, contract.get(j))
        dpre = (dact * slope[j].astype(F32)).astype(BF)
        dpre_ref[j] = dpre
        vecs[5 + j : 6 + j] = column_sum(dpre)
    total = dr2
    for j in range(4):
        total = total + dot_nt(dpre_ref[j], expand.get(j))
    return total


def attention_backward(dhidden, vec, n1, s1, qkv, probs, weights, vecs, parts, head):
    dr1, dgain, dshift = norm_back(dhidden, n1[...], s1[:, 0:1], vec[3:4])
    parts[3] = dr1.astype(BF)
    dattended = dot_nt(parts[3], weights.get(3)).astype(BF)
    low_half = head_masks()
    for pair in range(HEADS // 2):
        lanes = slice(pair * 128, pair * 128 + 128)
        q2, k2, v2 = qkv[0, :, lanes], qkv[1, :, lanes], qkv[2, :, lanes]
        do2 = dattended[:, lanes]
        dqs = []
        dk2 = jnp.zeros((BLOCK, 128), F32)
        dv2 = jnp.zeros((BLOCK, 128), F32)
        for h in range(2):
            mine = low_half if h == 0 else jnp.logical_not(low_half)
            do_h = jnp.where(mine, do2, jnp.zeros_like(do2))
            rows_low = probs[2 * pair + h]
            rows = rows_low.astype(F32)
            dprobs = dot_nt(do_h, v2)
            dscores = (
                rows * (dprobs - jnp.sum(rows * dprobs, axis=1, keepdims=True))
            ).astype(BF)
            dqs.append(dot(dscores, k2))
            dk2 = dk2 + dot_tn(dscores, jnp.where(mine, q2, jnp.zeros_like(q2)))
            dv2 = dv2 + dot_tn(rows_low, do_h)
        parts[0, :, lanes] = (jnp.where(low_half, dqs[0], dqs[1]) * 0.125).astype(BF)
        parts[1, :, lanes] = dk2.astype(BF)
        parts[2, :, lanes] = dv2.astype(BF)
    total = dr1
    for j in range(3):
        total = total + dot_nt(parts[j], weights.get(j))
    head[...] = jnp.concatenate(
        [column_sum(parts[0]), column_sum(parts[2]), column_sum(parts[3]), dgain, dshift, vecs[5:16]],
        axis=0,
    ).astype(BF)
    return total


def put_attention_inputs(out, both, xk, xs):
    core = lax.axis_index("core")
    for to, second in ((xk, core), (xs, 1 - core)):
        out.put(both.at[0], to.at[0])
        out.put(both.at[second], to.at[1])


def put_halves(out, four, one, keep, send):
    core = lax.axis_index("core")
    for to, half in ((keep, core), (send, 1 - core)):
        out.put(four.at[pl.ds(2 * half, 2)], to.at[pl.ds(0, 2)])
        out.put(one, to.at[2])


def wait_vectors(vraw, sems):
    for yh in range(2):
        for z in range(4):
            here = vraw.at[yh, z]
            pltpu.make_async_copy(here, here, sems.at[yh, z]).wait()


def fa_kernel(layer, u, sc, sr, *rest):
    pieces = rest[:16]
    hidden_o, n1_o, s1_o, qkv_o, probs_o, xk_o, xs_o, vec_o = rest[16:24]
    wa, vraw, hidden, n1, s1, qkv, probs, both, vec, sem_w, sem_v, sem_o = rest[24:]
    out = Out(sem_o)
    weights = attention_chunks(layer, pieces, wa, sem_w, vraw, sem_v)
    both[0] = u[...]
    wait_vectors(vraw, sem_v)
    vector_rows(vraw, vec)
    out.put(vec, vec_o)
    joined = sc[...] == sr[...]
    hidden[...] = attention_forward(u[...], joined, vec, weights, qkv, probs, both, n1, s1)
    for source, to in ((hidden, hidden_o), (n1, n1_o), (s1, s1_o), (qkv, qkv_o), (probs, probs_o)):
        out.put(source, to)
    put_attention_inputs(out, both, xk_o, xs_o)
    out.drain()


def ff_kernel(layer, hidden, vec, *rest):
    pieces, pieces_c = rest[:16], rest[16:18]
    result_o, n2_o, s2_o, slope_o, xk_o, xs_o = rest[18:24]
    we, wc, act, slope, n2, s2, result, sem_e, sem_c, sem_o = rest[24:]
    out = Out(sem_o)
    expand = expand_chunks(layer, pieces, we, sem_e)
    contract = Contract(layer, pieces_c, wc, sem_c)
    values = ffn_forward(hidden[...], vec, expand, contract, act, slope, n2, s2)
    put_halves(out, act, hidden, xk_o, xs_o)
    out.put(slope, slope_o)
    result[...] = values.astype(BF)
    for source, to in ((result, result_o), (n2, n2_o), (s2, s2_o)):
        out.put(source, to)
    out.drain()


def second_kernel(layer, keep, u, sc, sr, cot, *rest):
    pieces, pieces_c = rest[:16], rest[16:18]
    last_o, passed_o, xk_o, xs_o, dk_o, ds_o, xka_o, xsa_o, dka_o, dsa_o = rest[18:28]
    wa, we, wc, vraw, hidden, n1, s1, qkv, probs, both, vec = rest[28:39]
    act, slope, n2, s2, last, dpre, dffn, vecs, parts, head, passed = rest[39:50]
    sem_w, sem_v, sem_e, sem_c, sem_o = rest[50:]
    out = Out(sem_o)
    weights = attention_chunks(layer, pieces, wa, sem_w, vraw, sem_v)
    expand = expand_chunks(layer, pieces, we, sem_e)
    contract = Contract(layer, pieces_c, wc, sem_c)
    both[0] = u[...]
    wait_vectors(vraw, sem_v)
    vector_rows(vraw, vec)
    joined = sc[...] == sr[...]
    hidden[...] = attention_forward(u[...], joined, vec, weights, qkv, probs, both, n1, s1)
    put_attention_inputs(out, both, xka_o, xsa_o)
    values = ffn_forward(hidden[...], vec, expand, contract, act, slope, n2, s2)
    put_halves(out, act, hidden, xk_o, xs_o)
    kept = keep[0] > 9
    last[...] = jnp.where(kept, values.astype(BF), u[...])
    out.put(last, last_o)
    grad = jnp.where(kept, cot[...].astype(F32), 0.0)
    dhidden = ffn_backward(grad, vec, n2, s2, slope, expand, contract, vecs, dffn, dpre)
    put_halves(out, dpre, dffn, dk_o, ds_o)
    du = attention_backward(dhidden, vec, n1, s1, qkv, probs, weights, vecs, parts, head)
    put_attention_grads(out, parts, head, dka_o, dsa_o)
    passed[...] = jnp.where(kept, du.astype(BF), cot[...])
    out.put(passed, passed_o)
    out.drain()


def bf_kernel(layer, grad, vec, n2, s2, slope, *rest):
    pieces, pieces_c = rest[:16], rest[16:18]
    dhidden_o, vecs_o, dk_o, ds_o = rest[18:22]
    we, wc, dpre, dffn, dhidden, vecs, sem_e, sem_c, sem_o = rest[22:]
    out = Out(sem_o)
    contract = Contract(layer, pieces_c, wc, sem_c)
    expand = expand_chunks(layer, pieces, we, sem_e)
    dhidden[...] = ffn_backward(
        grad[...].astype(F32), vec, n2, s2, slope, expand, contract, vecs, dffn, dpre
    )
    put_halves(out, dpre, dffn, dk_o, ds_o)
    out.put(dhidden, dhidden_o)
    out.put(vecs, vecs_o)
    out.drain()


def put_attention_grads(out, parts, head, dk, ds):
    core = lax.axis_index("core")
    for to, half in ((dk, core), (ds, 1 - core)):
        for j in range(2):
            out.put(parts.at[2 * half + j], to.at[pl.ds(j * BLOCK, BLOCK), :])
        out.put(head, to.at[pl.ds(2 * BLOCK, 16), :])


def ba_kernel(layer, dhidden, vecs, vec, n1, s1, qkv, probs, *rest):
    pieces = rest[:16]
    du_o, dk_o, ds_o = rest[16:19]
    wa, parts, head, du, sem_w, sem_o = rest[19:]
    out = Out(sem_o)
    weights = attention_chunks(layer, pieces, wa, sem_w)
    du[...] = attention_backward(
        dhidden[...], vec, n1, s1, qkv, probs, weights, vecs, parts, head
    ).astype(BF)
    put_attention_grads(out, parts, head, dk_o, ds_o)
    out.put(du, du_o)
    out.drain()


def bring_rows(own, other, parts, to, sems, first):
    copies = []
    for i in range(parts):
        for r, ref in enumerate((own, other)):
            copies.append(
                pltpu.make_async_copy(
                    ref.at[i],
                    to.at[i, pl.ds(r * BLOCK, BLOCK), :],
                    sems.at[first + 2 * i + r],
                )
            )
    return copies


def bring_grads(own, other, to, head, sems, first):
    copies = []
    for i in range(2):
        for r, ref in enumerate((own, other)):
            copies.append(
                pltpu.make_async_copy(
                    ref.at[pl.ds(i * BLOCK, BLOCK), :],
                    to.at[i, pl.ds(r * BLOCK, BLOCK), :],
                    sems.at[first + 2 * i + r],
                )
            )
    for r, ref in enumerate((own, other)):
        copies.append(
            pltpu.make_async_copy(
                ref.at[pl.ds(2 * BLOCK, 16), :], head.at[r], sems.at[first + 4 + r]
            )
        )
    return copies


def wait_all(copies):
    for copy in copies:
        copy.wait()


def slab_rows(scratch, which, blocks):
    rows = [scratch[pl.ds(pl.multiple_of(b * ROWS + which * 24, 8), 24), :] for b in blocks]
    return jnp.concatenate(rows, axis=0).astype(BF)


def w1_kernel(xk, xr, dk, dr, xka, xra, dka, dra, result, x, d, xa, da, head, grad, staged, sem_i, sem_o):
    d_in, x_in = bring_rows(dk, dr, 3, d, sem_i, 0), bring_rows(xk, xr, 3, x, sem_i, 6)
    xa_in, da_in = bring_rows(xka, xra, 2, xa, sem_i, 12), bring_grads(dka, dra, da, head, sem_i, 16)
    for copy in d_in[4:6] + x_in + d_in[:4] + xa_in + da_in:
        copy.start()
    out = Out(sem_o)
    wait_all(d_in[4:6])
    for a in range(2):
        wait_all(x_in[2 * a : 2 * a + 2])
        values = dot_tn(x[a], d[2]).astype(BF)
        for b in range(8):
            staged[a * 8 + b, 0:96] = values[b * ROWS : (b + 1) * ROWS]
    out.put(staged.at[:, pl.ds(0, 96), :], result.at[:, pl.ds(0, 96), :])

    def both_yh(first):
        for z in range(4):
            for xs in range(4):
                staged[z * 4 + xs, first : first + 48] = slab_rows(grad, xs, (z, 4 + z))

    wait_all(x_in[4:6] + d_in[:4])
    for a in range(2):
        grad[...] = dot_tn(x[2], d[a])
        both_yh(96 + 48 * a)
    out.put(staged.at[:, pl.ds(96, 96), :], result.at[:, pl.ds(96, 96), :])
    wait_all(xa_in + da_in)
    for a in range(2):
        grad[...] = dot_tn(xa[a], da[a])
        both_yh(192 + 48 * a)
    vec = (head[0].astype(F32) + head[1].astype(F32)).astype(BF)
    for b in range(16):
        staged[b, 288:304] = vec
    out.put(staged.at[:, pl.ds(192, 112), :], result.at[:, pl.ds(192, 112), :])
    out.drain()


def wf_kernel(xk, xr, dk, dr, *rest):
    outs_c, outs_b = rest[:4], rest[4:8]
    x, d, grad, staged, sem_i, sem_o = rest[8:]
    d_in, x_in = bring_rows(dk, dr, 3, d, sem_i, 0), bring_rows(xk, xr, 3, x, sem_i, 6)
    for copy in d_in[4:6] + x_in + d_in[:4]:
        copy.start()
    out = Out(sem_o)
    wait_all(d_in[4:6])
    for a in range(2):
        here = slice(a * 192, (a + 1) * 192)
        wait_all(x_in[2 * a : 2 * a + 2])
        grad[...] = dot_tn(x[a], d[2])
        for k in range(4):
            staged[k, here] = slab_rows(grad, lax.rem(position(Y) + k, 4), range(8))
    for k in range(4):
        out.put(staged.at[k], outs_c[k])
    wait_all(x_in[4:6] + d_in[:4])
    for a in range(2):
        here = slice(a * 192, (a + 1) * 192)
        grad[...] = dot_tn(x[2], d[a])
        for k in range(4):
            staged[4 + k, here] = slab_rows(grad, lax.rem(position("x") + k, 4), range(8))
    for k in range(4):
        out.put(staged.at[4 + k], outs_b[k])
    out.drain()


def wa_kernel(xka, xra, dka, dra, *rest):
    outs = rest[:4]
    xa, da, head, grad, staged, sem_i, sem_o = rest[4:]
    xa_in, da_in = bring_rows(xka, xra, 2, xa, sem_i, 0), bring_grads(dka, dra, da, head, sem_i, 4)
    for copy in xa_in + da_in:
        copy.start()
    out = Out(sem_o)
    wait_all(xa_in + da_in)
    vec = (head[0].astype(F32) + head[1].astype(F32)).astype(BF)
    for a in range(2):
        grad[a] = dot_tn(xa[a], da[a]).astype(BF)
    for k in range(4):
        zs = lax.rem(position("z") + k, 4)
        for a in range(2):
            for yh in range(2):
                row = pl.multiple_of((yh * 4 + zs) * ROWS, ROWS)
                staged[k, (a * 2 + yh) * ROWS : (a * 2 + yh + 1) * ROWS] = grad[a, pl.ds(row, ROWS), :]
        staged[k, 384:400] = vec
        out.put(staged.at[k], outs[k])
    out.drain()


def pack_kernel(iw, ib, ow, ob, fg, fs, ew, eb, cw, cb, sg, ss, own, contract, scratch):
    scratch[96:104] = jnp.zeros((8, D), F32)
    for j in range(8):
        rows = iw[0, :, j * D : (j + 1) * D] if j < 3 else ow[0]
        if j > 3:
            rows = ew[0, :, (j - 4) * D : (j - 3) * D]
        scratch[j * 12 : (j + 1) * 12] = rows
    start = 0
    for ref in (ib, ob, fg, fs, eb, cb, sg, ss):
        width = ref.shape[1]
        scratch[96:97, start : start + width] = ref[...]
        start += width
    own[...] = scratch[...].astype(BF)
    contract[...] = cw[0].astype(BF)


def shape(*dims, dtype=F32):
    return jax.ShapeDtypeStruct(dims, dtype)


def call(kernel, outs, args, in_hbm=0, scratch=(), name="kernel", outs_hbm=True, smem=0, flops=1000):
    here = len(args) - in_hbm - smem
    in_specs = [pl.BlockSpec(memory_space=pltpu.SMEM)] * smem
    in_specs += [pl.BlockSpec(memory_space=pltpu.VMEM)] * here
    in_specs += [pl.BlockSpec(memory_space=pl.ANY)] * in_hbm
    out_space = pl.ANY if outs_hbm else pltpu.VMEM
    return pl.pallas_call(
        kernel,
        out_shape=outs,
        in_specs=in_specs,
        out_specs=[pl.BlockSpec(memory_space=out_space)] * len(outs),
        scratch_shapes=list(scratch),
        compiler_params=pltpu.CompilerParams(vmem_limit_bytes=56 * 1024 * 1024),
        cost_estimate=pl.CostEstimate(flops=flops, bytes_accessed=1024, transcendentals=0),
        name=name,
    )(*args)


ROWS_BF = shape(BLOCK, D, dtype=BF)
ROWS_F32 = shape(BLOCK, D)
SCALE = shape(BLOCK, 128)
QKV = shape(3, BLOCK, D, dtype=BF)
PROBS = shape(HEADS, BLOCK, BLOCK, dtype=BF)
SLOPE = shape(4, BLOCK, D, dtype=BF)
TWO = shape(2, BLOCK, D, dtype=BF)
THREE = shape(3, BLOCK, D, dtype=BF)
VECS = shape(16, D)
DA = shape(528, D, dtype=BF)


def vmem(*shapes):
    return [pltpu.VMEM(each.shape, each.dtype) for each in shapes]


HEAD_BF = shape(16, D, dtype=BF)
VRAW = shape(2, 4, 16, D, dtype=BF)


def first_attention(u, seg, pieces):
    saved = [ROWS_F32, SCALE, QKV, PROBS]
    return call(
        lambda *refs: fa_kernel(0, *refs),
        [ROWS_BF, *saved, TWO, TWO, VECS],
        [u, seg[:, None], seg[None, :], *pieces],
        16,
        [WA, *vmem(VRAW, ROWS_BF, *saved, TWO, VECS), dma(4, 8), dma(2, 4), dma(16)],
        name="attention_forward_0",
        flops=12_000_000_000,
    )


def first_ffn(hidden, vec, pieces, pieces_c):
    return call(
        lambda *refs: ff_kernel(0, *refs),
        [ROWS_BF, ROWS_F32, SCALE, SLOPE, THREE, THREE],
        [hidden, vec, *pieces, *pieces_c],
        18,
        [WA, WC, FOUR, *vmem(SLOPE, ROWS_F32, SCALE, ROWS_BF), dma(4, 8), dma(4, 2, 4), dma(16)],
        name="ffn_forward_0",
    )


def second_layer(depth, u, seg, cot, pieces, pieces_c):
    return call(
        lambda *refs: second_kernel(1, *refs),
        [ROWS_BF, ROWS_BF, THREE, THREE, THREE, THREE, TWO, TWO, DA, DA],
        [depth, u, seg[:, None], seg[None, :], cot, *pieces, *pieces_c],
        18,
        [WA, WA, WC, *vmem(VRAW, ROWS_BF, ROWS_F32, SCALE, QKV, PROBS, TWO, VECS)]
        + [FOUR, *vmem(SLOPE, ROWS_F32, SCALE, ROWS_BF)]
        + [FOUR, *vmem(ROWS_BF, VECS), FOUR, *vmem(HEAD_BF, ROWS_BF)]
        + [dma(4, 8), dma(2, 4), dma(4, 8), dma(4, 2, 4), dma(24)],
        name="second_layer",
        smem=1,
    )


def first_ffn_backward(grad, vec, n2, s2, slope, pieces, pieces_c):
    return call(
        lambda *refs: bf_kernel(0, *refs),
        [ROWS_F32, VECS, THREE, THREE],
        [grad, vec, n2, s2, slope, *pieces, *pieces_c],
        18,
        [WA, WC, FOUR, *vmem(ROWS_BF, ROWS_F32, VECS), dma(4, 8), dma(4, 2, 4), dma(16)],
        name="ffn_backward_0",
    )


def first_attention_backward(dhidden, vecs, vec, n1, s1, qkv, probs, pieces):
    return call(
        lambda *refs: ba_kernel(0, *refs),
        [ROWS_BF, DA, DA],
        [dhidden, vecs, vec, n1, s1, qkv, probs, *pieces],
        16,
        [WA, FOUR, *vmem(HEAD_BF, ROWS_BF), dma(4, 8), dma(16)],
        name="attention_backward_0",
    )


def both_cores(parts):
    return pltpu.VMEM((parts, 2 * BLOCK, D), BF)


def second_weights(args):
    return call(
        w1_kernel,
        [shape(16, 304, D, dtype=BF)],
        args,
        8,
        [both_cores(3), both_cores(3), both_cores(2), both_cores(2), pltpu.VMEM((2, 16, D), BF)]
        + [pltpu.VMEM((D, D), F32), pltpu.VMEM((16, 304, D), BF), dma(24), dma(4)],
        name="weights_1",
    )[0]


def first_ffn_weights(args):
    outs = call(
        wf_kernel,
        [shape(384, D, dtype=BF)] * 8,
        args,
        4,
        [both_cores(3), both_cores(3), pltpu.VMEM((D, D), F32)]
        + [pltpu.VMEM((8, 384, D), BF), dma(12), dma(8)],
        name="ffn_weights_0",
    )
    return outs[:4], outs[4:]


def first_attention_weights(args):
    return call(
        wa_kernel,
        [shape(400, D, dtype=BF)] * 4,
        args,
        4,
        [both_cores(2), both_cores(2), pltpu.VMEM((2, 16, D), BF), pltpu.VMEM((2, D, D), BF)]
        + [pltpu.VMEM((4, 400, D), BF), dma(10), dma(4)],
        name="attention_weights_0",
    )


def gather_first(masters):
    core = lax.axis_index("core")
    own, contract = call(
        pack_kernel,
        [shape(104, D, dtype=BF), shape(48, D, dtype=BF)],
        list(masters),
        0,
        [pltpu.VMEM((104, D), F32)],
        name="pack",
        outs_hbm=False,
    )
    own, contract = from_behind(own, "x"), from_behind(contract, Y)
    contract, own = lax.optimization_barrier((contract, own))
    contract, along_x = by_position(contract, position(Y)), by_position(own, position("x"))
    contract = lax.all_gather(contract, "z", axis=0)
    other = swap_core(along_x)
    first, second = jnp.where(core == 0, along_x, other), jnp.where(core == 0, other, along_x)
    both = jnp.stack([first, second])
    chunks = both[:, :, :96].reshape(2, 4, 8, 12, D).transpose(2, 1, 0, 3, 4).reshape(8, ROWS, D)
    vector = both[:, :, 96].transpose(1, 0, 2).reshape(8, D)
    chunks = lax.dynamic_slice_in_dim(chunks, 4 * core, 4, 0).reshape(384, D)
    load = jnp.concatenate([chunks, vector, jnp.zeros((8, D), BF)], axis=0)
    load = [load] + [ahead_crossed(load, k, 0) for k in (1, 2, 3)]
    load, contract = lax.optimization_barrier((load, contract))
    contract = lax.all_gather(contract, "x", axis=0)
    load = by_position(load, jnp.where(core == 0, position(Y), position("z")))
    return load.reshape(2, 2, 400, D), contract


def gather_forward(masters, u, seg):
    load, contract = gather_first(masters)
    own = []
    for half in range(2):
        value = load[:, half]
        own.append([value] + [ahead_crossed(value, k, 1) for k in (1, 2, 3)])
    other = [[swap_core(piece) for piece in own[0]]]
    attended = list(first_attention(u, seg, own[0] + own[1][:1] * 4 + other[0] + own[1][:1] * 4))
    attended[0], contract, own[1][0] = lax.optimization_barrier(
        (attended[0], contract, own[1][0])
    )
    other_c, early = swap_core(contract), swap_core(own[1][0])
    own[1][1:], other_c, early = lax.optimization_barrier((own[1][1:], other_c, early))
    other.append([early] + [swap_core(piece) for piece in own[1][1:]])
    return own[0] + own[1] + other[0] + other[1], [contract, other_c], attended


def summed(pieces):
    total = pieces[0].astype(F32)
    for piece in pieces[1:]:
        total = total + piece.astype(F32)
    return total


def scatter_ahead(pieces, axis):
    return [pieces[0]] + [ahead(pieces[k], axis, k) for k in (1, 2, 3)]


def pieces_ahead(parts, axis):
    here = position(axis)
    return [lax.dynamic_index_in_dim(parts, (here + k) % 4, 0, keepdims=False) for k in range(4)]


def reduce_along(parts, axis):
    return summed(scatter_ahead(pieces_ahead(parts, axis), axis))


def reduce_last(attention, expand, contract, second):
    section, core = lax.axis_index("section"), lax.axis_index("core")
    a, b, c = summed(attention), summed(expand), summed(contract)
    vec = a[384:]
    a, b = a[:384].reshape(2, 2, ROWS, D), b.reshape(2, 2, ROWS, D)
    blocks = []
    for yh in range(2):
        for slot in range(2):
            parts = [a[slot, yh], vec, b[slot, yh]]
            blocks.append(jnp.concatenate([part.astype(BF) for part in parts], axis=0))
    along_y = reduce_along(jnp.stack(blocks), Y)
    c = reduce_along(c.astype(BF).reshape(4, ROWS, D), "z")
    b = reduce_along(along_y[112:].astype(BF).reshape(4, 24, D), "z")

    def by_x(rows):
        return rows.astype(BF).reshape(4, 24, D)

    vec = jnp.broadcast_to(along_y[96:112].astype(BF)[None], (4, 16, D))
    load = reduce_along(jnp.concatenate([by_x(along_y[:96]), by_x(c), vec], axis=1), "x")
    a0, c0 = load[:24], load[24:48]
    second_b, second_a = second[96:192].reshape(2, 2, 24, D), second[192:288].reshape(2, 2, 24, D)
    blocks = []
    for yh in range(2):
        for slot in range(2):
            y = 2 * yh + slot
            parts = [second[24 * y : 24 * y + 24], second_b[slot, yh], second_a[slot, yh]]
            blocks.append(jnp.concatenate(parts + [second[288:]], axis=0))
    along_y = reduce_along(jnp.stack(blocks), Y)
    c1, b1, a1, vec1 = along_y[:24], along_y[24:48], along_y[48:72], along_y[72:]
    vec = jnp.where(section == 0, load[48:], vec1)
    mine = jnp.where(section == 0, jnp.stack([a0, b, c0]), jnp.stack([a1, b1, c1]))
    others = jnp.where(section == 0, jnp.stack([a1, b1, c1]), jnp.stack([a0, b, c0]))
    near, far = crossed_owner(mine[2], False), crossed_owner(others[2], True)
    contract = jnp.concatenate(
        [jnp.where(section == 0, near, far), jnp.where(section == 0, far, near)]
    )
    mine, others = mine[:2].reshape(2, 2, 12, D), others[:2].reshape(2, 2, 12, D)

    def rows_of(value, which):
        return lax.dynamic_index_in_dim(value, which, 1, keepdims=False)

    here = rows_of(mine, core)
    near = to_neighbour(rows_of(mine, 1 - core), False, True)
    far = to_neighbour(rows_of(others, core), True, False)
    far_near = to_neighbour(rows_of(others, 1 - core), True, True)
    own, other = jnp.stack([here, far]), jnp.stack([near, far_near])
    low, high = jnp.where(core == 0, own, other), jnp.where(core == 0, other, own)
    flip = section == 0
    chunks = [jnp.where(flip, low[0], low[1]), jnp.where(flip, low[1], low[0])]
    chunks += [jnp.where(flip, high[0], high[1]), jnp.where(flip, high[1], high[0])]
    input_weight = jnp.concatenate([chunks[j][0] for j in range(3)], axis=1)
    expand_weight = jnp.concatenate([chunks[j][1] for j in range(4)], axis=1)
    return input_weight, chunks[3][0], expand_weight, contract, vec


def to_neighbour(value, other_section, other_core):
    pairs = []
    for s in range(2):
        for c in range(2):
            to = (1 - s if other_section else s) * 2 + (1 - c if other_core else c)
            pairs.append((s * 2 + c, to))
    return lax.ppermute(value, ("section", "core"), pairs)


def crossed_owner(value, other_section):
    pairs = []
    for s in range(2):
        for yh in range(2):
            for c in range(2):
                to = 1 - s if other_section else s
                pairs.append(((s * 2 + yh) * 2 + c, (to * 2 + c) * 2 + yh))
    return lax.ppermute(value, ("section", "yh", "core"), pairs)


def on_device(tokens, segment_ids, depth, *rest):
    masters = rest[:12]
    cotangent = rest[12]
    section = lax.axis_index("section")
    place = (
        lax.axis_index("yh") * 32
        + lax.axis_index("z") * 8
        + lax.axis_index("x") * 2
        + lax.axis_index("core")
    )
    u = lax.dynamic_slice_in_dim(tokens, section * BLOCK, BLOCK, 0)
    seg = lax.dynamic_slice_in_dim(segment_ids, section * BLOCK, BLOCK, 0)
    cot = lax.dynamic_slice_in_dim(cotangent, section * BLOCK, BLOCK, 0)

    def halves(of_first, of_second):
        mine = jnp.where(section == 0, of_first, of_second)
        theirs = ahead(jnp.where(section == 0, of_second, of_first), "section", 1)
        return jnp.concatenate(
            [jnp.where(section == 0, mine, theirs), jnp.where(section == 0, theirs, mine)]
        )[None]

    pieces, pieces_c, attended = gather_forward(masters, u, seg)
    hidden, *saved0, xka0, xsa0, vec0 = attended
    middle, n2_0, s2_0, slope0, xk0, xs0 = first_ffn(hidden, vec0, pieces, pieces_c)
    last, passed, xk1, xs1, dk1, ds1, xka1, xsa1, dka1, dsa1 = second_layer(
        depth, middle, seg, cot, pieces, pieces_c
    )
    dhidden, vecs, dk0, ds0 = first_ffn_backward(
        passed, vec0, n2_0, s2_0, slope0, pieces, pieces_c
    )
    received = [swap_core(each) for each in (xs1, ds1, xsa1, dsa1)]
    dhidden, received = lax.optimization_barrier((dhidden, received))
    weights1 = second_weights(
        [xk1, received[0], dk1, received[1], xka1, received[2], dka1, received[3]]
    )
    dhidden, weights1 = lax.optimization_barrier((dhidden, weights1))
    weights1 = weights1.reshape(16 * 304, D)
    second = lax.psum_scatter(weights1, ("z", "x"), scatter_dimension=0, tiled=True)
    first, dka0, dsa0 = first_attention_backward(dhidden, vecs, vec0, *saved0, pieces)
    received = [swap_core(each) for each in (xs0, ds0, xsa0)]
    first, received = lax.optimization_barrier((first, received))
    contract0, expand0 = first_ffn_weights([xk0, received[0], dk0, received[1]])
    received_a = swap_core(dsa0)
    contract0, expand0, received_a = lax.optimization_barrier((contract0, expand0, received_a))
    attention0 = first_attention_weights([xka0, received[2], dka0, received_a])
    attention0 = scatter_ahead(attention0, "z")
    contract0 = scatter_ahead(contract0, Y)
    expand0 = scatter_ahead(expand0, "x")
    layer_outputs = halves(middle, last)
    input_grads = halves(first, passed)
    iw, ow, ew, cw, vec = reduce_last(attention0, expand0, contract0, second)

    def shard(first_row, rows, width):
        flat = vec[first_row : first_row + rows].reshape(-1)
        return lax.dynamic_slice_in_dim(flat, place * width, width, 0)[None]

    return (
        layer_outputs,
        input_grads,
        iw[None],
        shard(0, 2, 24),
        ow[None],
        shard(2, 1, 12),
        shard(3, 1, 12),
        shard(4, 1, 12),
        ew[None],
        shard(5, 4, 48),
        cw[None],
        shard(9, 1, 12),
        shard(10, 1, 12),
        shard(11, 1, 12),
    )


def solution(mesh):
    wide = Mesh(mesh.devices.reshape(2, 2, 4, 4, 2), ("section", "yh", "z", "x", "core"))
    dp = ("yh", "z", "x", "core")
    matrix, vector = P("section", dp, None), P("section", dp)
    rows = P(dp, None)
    weights = (
        matrix,
        vector,
        matrix,
        vector,
        vector,
        vector,
        matrix,
        vector,
        matrix,
        vector,
        vector,
        vector,
    )
    return jax.shard_map(
        on_device,
        mesh=wide,
        in_specs=(rows, P(dp), P(dp)) + weights + (rows,),
        out_specs=(matrix, matrix) + weights,
        check_vma=False,
    )
```

```python
import jax
import jax.numpy as jnp
from jax import lax
from jax.experimental import pallas as pl
from jax.experimental.pallas import tpu as pltpu
from jax.sharding import Mesh, PartitionSpec as P

D = 768
HEADS = 12
BLOCK = 256
EPS = 1e-05
Y = ("section", "yh")
ROWS = 96
BF = jnp.bfloat16
F32 = jnp.float32


def position(axis):
    if isinstance(axis, tuple):
        return lax.axis_index("yh") * 2 + lax.axis_index("section")
    return lax.axis_index(axis)


def size_of(axis):
    return 4 if isinstance(axis, tuple) else lax.axis_size(axis)


def ahead(value, axis, steps):
    count = size_of(axis)
    at = [0, 2, 1, 3] if isinstance(axis, tuple) else range(count)
    return lax.ppermute(value, axis, [(at[i], at[(i + steps) % count]) for i in range(count)])


def from_behind(value, axis):
    return [value] + [ahead(value, axis, k) for k in (1, 2, 3)]


def by_position(pieces, here):
    rising = [pieces[0], pieces[3], pieces[2], pieces[1]]
    return lax.dynamic_slice_in_dim(jnp.stack(rising + rising), (4 - here) % 4, 4, 0)


def ahead_crossed(value, steps, first):
    pairs = []
    for y in range(4):
        for z in range(4):
            for c in range(2):
                to_y, to_z = ((y + steps) % 4, z) if c == first else (y, (z + steps) % 4)
                pairs.append(
                    (
                        (((y % 2) * 2 + y // 2) * 4 + z) * 2 + c,
                        (((to_y % 2) * 2 + to_y // 2) * 4 + to_z) * 2 + c,
                    )
                )
    return lax.ppermute(value, ("section", "yh", "z", "core"), pairs)


def swap_core(value):
    return ahead(value, "core", 1)


def behind(axis, k):
    return lax.rem(position(axis) + (4 - k), 4)


class Chunks:
    def __init__(self, to, sems):
        self.to, self.sems, self.here = to, sems, set()

    def bring(self, j, source, yh, z):
        block = yh * 4 + z
        rows = pl.ds(pl.multiple_of(block * ROWS, ROWS), ROWS)
        pltpu.make_async_copy(
            source.at[pl.ds(j * ROWS, ROWS), :], self.to.at[j, rows, :], self.sems.at[j, block]
        ).start()

    def wait(self):
        for j in range(4):
            self.get(j)

    def get(self, j):
        for block in range(0 if j in self.here else 8):
            here = self.to.at[j, pl.ds(block * ROWS, ROWS), :]
            pltpu.make_async_copy(here, here, self.sems.at[j, block]).wait()
        self.here.add(j)
        return self.to[j]


def attention_chunks(layer, pieces, to, sems, order, vraw=None, sem_v=None):
    chunks = Chunks(to, sems)
    core = lax.axis_index("core")
    away = jnp.where(lax.axis_index("section") == layer, 0, 1)
    for r in range(2):

        @pl.when(core == r)
        def _():
            def each(act):
                for k in range(4):
                    for e in range(2):
                        steps = 2 * e + away
                        yh = lax.rem(position(Y) + 4 - steps, 4) // 2
                        act(pieces[r * 4 + k].at[steps], yh, behind("z", k))

            if vraw is not None:
                each(
                    lambda piece, yh, z: pltpu.make_async_copy(
                        piece.at[pl.ds(4 * ROWS, 16), :], vraw.at[yh, z], sem_v.at[yh, z]
                    ).start()
                )
            for j in order:
                each(lambda piece, yh, z: chunks.bring(j, piece, yh, z))

    return chunks


def expand_chunks(layer, pieces, to, sems):
    chunks = Chunks(to, sems)
    core = lax.axis_index("core")
    for j in range(4):
        for k in range(4):
            ys = behind(Y, k)
            for r in range(2):

                @pl.when(jnp.logical_and(lax.rem(ys, 2) == layer, core == 1 - r))
                def _():
                    for e in range(4):
                        chunks.bring(j, pieces[r * 4 + k].at[e], ys // 2, behind("z", e))

    return chunks


class Contract:
    def __init__(self, layer, pieces, to, sems_0, sems_1):
        self.to, self.sems_0, self.sems_1, self.here = to, sems_0, sems_1, set()
        core = lax.axis_index("core")
        for r in range(2):
            for yh in range(2):

                @pl.when(core == r)
                def _():
                    for k in range(4):
                        z = behind("z", k)
                        for x in range(4):
                            pltpu.make_async_copy(
                                pieces[r].at[x, k, yh * 2 + layer],
                                to.at[yh, z, x, 0],
                                sems_0.at[yh, z, x],
                            ).start()

            for k in range(4):
                ys = behind(Y, k)

                @pl.when(jnp.logical_and(core == 1 - r, lax.rem(ys, 2) == layer))
                def _():
                    for x in range(4):
                        pltpu.make_async_copy(
                            pieces[r].at[x, k], to.at[ys // 2, :, x, 1], sems_1.at[ys // 2, x]
                        ).start()

    def wait(self):
        for j in range(4):
            self.get(j)

    def get(self, j):
        yh, first = j // 2, (j % 2) * 2
        for x in range(0 if j in self.here else 4):
            for z in (first, first + 1):
                here = self.to.at[yh, z, x, 0]
                pltpu.make_async_copy(here, here, self.sems_0.at[yh, z, x]).wait()
            if first == 0:
                here = self.to.at[yh, :, x, 1]
                pltpu.make_async_copy(here, here, self.sems_1.at[yh, x]).wait()
        self.here.add(j)
        return self.to[yh, first : first + 2].reshape(D, D)


class Out:
    def __init__(self, sems):
        self.sems, self.copies, self.count = sems, [], 0

    def put(self, source, to):
        copy = pltpu.make_async_copy(source, to, self.sems.at[self.count])
        copy.start()
        self.copies.append(copy)
        self.count += 1

    def drain(self):
        for copy in self.copies:
            copy.wait()


WA = pltpu.VMEM((4, D, D), BF)
WC = pltpu.VMEM((2, 4, 4, 2, 48, D), BF)
FOUR = pltpu.VMEM((4, BLOCK, D), BF)


def dma(*count):
    return pltpu.SemaphoreType.DMA(count)


def dot(left, right):
    return lax.dot_general(left, right, (((1,), (0,)), ((), ())), preferred_element_type=F32)


def dot_nt(left, right):
    return lax.dot_general(left, right, (((1,), (1,)), ((), ())), preferred_element_type=F32)


def dot_tn(left, right):
    return lax.dot_general(left, right, (((0,), (0,)), ((), ())), preferred_element_type=F32)


def norm_of(residual):
    centre = residual - jnp.mean(residual, axis=1, keepdims=True)
    scaled = lax.rsqrt(jnp.mean(centre * centre, axis=1, keepdims=True) + EPS)
    return centre * scaled, scaled


def norm_back(grad_out, normed, scaled, gain):
    grad_normed = grad_out * gain
    inner = (
        grad_normed
        - jnp.mean(grad_normed, axis=1, keepdims=True)
        - normed * jnp.mean(grad_normed * normed, axis=1, keepdims=True)
    )
    return (
        scaled * inner,
        jnp.sum(grad_out * normed, axis=0, keepdims=True),
        jnp.sum(grad_out, axis=0, keepdims=True),
    )


def head_masks():
    lane = lax.broadcasted_iota(jnp.int32, (BLOCK, 128), 1)
    return lane < 64


def vector_rows(vraw, out):
    groups = [vraw[yh, z][0:8, :256].astype(F32) for yh in range(2) for z in range(4)]
    values = jnp.concatenate(groups, axis=0).astype(BF)
    lane = lax.broadcasted_iota(jnp.int32, (64, D), 1)
    device = lax.broadcasted_iota(jnp.int32, (64, D), 0)

    def rows(start, width, count):
        found = []
        for r in range(count):
            spread = jnp.where(device == (lane + r * D) // width, 1.0, 0.0).astype(BF)
            wide = dot_tn(values[:, start : start + width], spread)
            entry = lax.broadcasted_iota(jnp.int32, wide.shape, 0)
            at = lax.broadcasted_iota(jnp.int32, wide.shape, 1) + r * D
            found.append(
                jnp.sum(jnp.where(entry == at % width, wide, 0.0), axis=0, keepdims=True)
            )
        return found

    found = rows(0, 24, 2)
    for start in (24, 36, 48):
        found += rows(start, 12, 1)
    found += rows(60, 48, 4)
    for start in (108, 120, 132):
        found += rows(start, 12, 1)
    out[...] = jnp.concatenate(found + [jnp.zeros((4, D), F32)], axis=0)


def column_sum(values):
    return jnp.sum(values.astype(F32), axis=0, keepdims=True)


def attention_forward(u, joined, vec, weights, qkv, probs, both, normed, scaled, attended):
    q = ((dot(u, weights.get(0)) + vec[0:1]) * 0.125).astype(BF)
    k = dot(u, weights.get(1)).astype(BF)
    v = (dot(u, weights.get(2)) + vec[1:2]).astype(BF)
    qkv[0] = q
    qkv[1] = k
    qkv[2] = v
    low_half = head_masks()
    for pair in range(HEADS // 2):
        lanes = slice(pair * 128, pair * 128 + 128)
        q2, k2, v2 = q[:, lanes], k[:, lanes], v[:, lanes]
        outs = []
        for h in range(2):
            mine = low_half if h == 0 else jnp.logical_not(low_half)
            scores = dot_nt(jnp.where(mine, q2, jnp.zeros_like(q2)), k2)
            scores = jnp.where(joined, scores, -1e30)
            top = jnp.max(scores, axis=1, keepdims=True)
            exponent = jnp.exp(scores - top)
            total = jnp.sum(exponent, axis=1, keepdims=True)
            rows = (exponent / total).astype(BF)
            probs[2 * pair + h] = rows
            outs.append(dot(rows, v2))
        both[1, :, lanes] = jnp.where(low_half, outs[0], outs[1]).astype(BF)
    attended()
    branch = dot(both[1], weights.get(3)) + vec[2:3]
    n1, s1 = norm_of(u.astype(F32) + branch)
    normed[...] = n1
    scaled[...] = jnp.broadcast_to(s1, (BLOCK, 128))
    return (n1 * vec[3:4] + vec[4:5]).astype(BF)


def ffn_forward(hidden, vec, expand, contract, act, slope, normed, scaled):
    expand.wait()
    contract.wait()
    for j in range(4):
        pre = dot(hidden, expand.get(j)) + vec[5 + j : 6 + j]
        half = 0.5 * (1.0 + lax.erf(pre * 0.7071067811865476))
        act[j] = (pre * half).astype(BF)
        slope[j] = (half + pre * jnp.exp(-0.5 * pre * pre) * 0.3989422804014327).astype(BF)
    total = hidden.astype(F32) + vec[9:10]
    for j in range(4):
        total = total + dot(act[j], contract.get(j))
    n2, s2 = norm_of(total)
    normed[...] = n2
    scaled[...] = jnp.broadcast_to(s2, (BLOCK, 128))
    return n2 * vec[10:11] + vec[11:12]


def ffn_backward(grad, vec, n2, s2, slope, expand, contract, vecs, dffn_ref, dpre_ref):
    dr2, dgain, dshift = norm_back(grad, n2[...], s2[:, 0:1], vec[10:11])
    dffn = dr2.astype(BF)
    dffn_ref[...] = dffn
    vecs[...] = jnp.zeros((16, D), F32)
    vecs[9:10] = column_sum(dffn)
    vecs[10:11] = dgain
    vecs[11:12] = dshift
    for j in range(4):
        dact = dot_nt(dffn, contract.get(j))
        dpre = (dact * slope[j].astype(F32)).astype(BF)
        dpre_ref[j] = dpre
        vecs[5 + j : 6 + j] = column_sum(dpre)
    total = dr2
    for j in range(4):
        total = total + dot_nt(dpre_ref[j], expand.get(j))
    return total


def attention_backward(dhidden, vec, n1, s1, qkv, probs, weights, vecs, parts, head, ready):
    dr1, dgain, dshift = norm_back(dhidden, n1[...], s1[:, 0:1], vec[3:4])
    parts[3] = dr1.astype(BF)
    dattended = dot_nt(parts[3], weights.get(3)).astype(BF)
    ready()
    low_half = head_masks()
    for pair in range(HEADS // 2):
        lanes = slice(pair * 128, pair * 128 + 128)
        q2, k2, v2 = qkv[0, :, lanes], qkv[1, :, lanes], qkv[2, :, lanes]
        do2 = dattended[:, lanes]
        dqs = []
        dk2 = jnp.zeros((BLOCK, 128), F32)
        dv2 = jnp.zeros((BLOCK, 128), F32)
        for h in range(2):
            mine = low_half if h == 0 else jnp.logical_not(low_half)
            do_h = jnp.where(mine, do2, jnp.zeros_like(do2))
            rows_low = probs[2 * pair + h]
            rows = rows_low.astype(F32)
            dprobs = dot_nt(do_h, v2)
            dscores = (
                rows * (dprobs - jnp.sum(rows * dprobs, axis=1, keepdims=True))
            ).astype(BF)
            dqs.append(dot(dscores, k2))
            dk2 = dk2 + dot_tn(dscores, jnp.where(mine, q2, jnp.zeros_like(q2)))
            dv2 = dv2 + dot_tn(rows_low, do_h)
        parts[0, :, lanes] = (jnp.where(low_half, dqs[0], dqs[1]) * 0.125).astype(BF)
        parts[1, :, lanes] = dk2.astype(BF)
        parts[2, :, lanes] = dv2.astype(BF)
    total = dr1
    for j in range(3):
        total = total + dot_nt(parts[j], weights.get(j))
    head[...] = jnp.concatenate(
        [column_sum(parts[0]), column_sum(parts[2]), column_sum(parts[3]), dgain, dshift, vecs[5:16]],
        axis=0,
    ).astype(BF)
    return total


ACT, HIDDEN, INPUTS, DPRE, DFFN, OUTPUTS, HEAD, ALL = 0, 512, 768, 1280, 1792, 2048, 2560, 2576


def put_rows(out, source, to, first):
    out.put(source, to.at[pl.ds(first, source.shape[0]), :])


def put_attention_inputs(out, both, keep, send):
    core = lax.axis_index("core")
    for to, second in ((keep, core), (send, 1 - core)):
        put_rows(out, both.at[0], to, INPUTS)
        put_rows(out, both.at[second], to, INPUTS + BLOCK)


def put_halves(out, four, one, keep, send, first):
    core = lax.axis_index("core")
    for to, half in ((keep, core), (send, 1 - core)):
        for j in range(2):
            put_rows(out, four.at[2 * half + j], to, first + j * BLOCK)
        put_rows(out, one, to, first + 2 * BLOCK)


def wait_vectors(vraw, sems):
    for yh in range(2):
        for z in range(4):
            here = vraw.at[yh, z]
            pltpu.make_async_copy(here, here, sems.at[yh, z]).wait()


def put_attention_grads(out, parts, head, keep, send, first):
    core = lax.axis_index("core")
    for to, half in ((keep, core), (send, 1 - core)):
        for j in range(2):
            put_rows(out, parts.at[2 * half + j], to, first + j * BLOCK)
        put_rows(out, head, to, first + 2 * BLOCK)


def middle_kernel(keep, u0, sc, sr, cot, *rest):
    pieces, pieces_c = rest[:8], rest[8:10]
    middle_o, last_o, passed_o, dhidden_o, vecs_o = rest[10:15]
    n1_0o, s1_0o, qkv_0o, probs_0o, vec0_o, keep0_o, send0_o, keep_o, send_o = rest[15:24]
    rest = rest[24:]
    vraw0, hidden0, n1_0, s1_0, qkv_0, probs_0, both0, vec0 = rest[:8]
    we0, wc0, act0, slope0, n2_0, s2_0, dffn0, dhidden0, vecs0 = rest[8:17]
    wa, wb, wc, vraw, hidden, n1, s1, qkv, probs, both, vec = rest[17:28]
    act, slope, n2, s2, last, dpre, dffn, vecs, parts, head, passed = rest[28:39]
    sem_w0, sem_v0, sem_e0, sem_c0, sem_d0, sem_w, sem_v, sem_e, sem_c, sem_d, sem_o = rest[39:]
    out = Out(sem_o)
    joined = sc[...] == sr[...]
    weights0 = attention_chunks(0, pieces, wb, sem_w0, (0, 1, 2, 3), vraw0, sem_v0)
    expand0 = expand_chunks(0, pieces, we0, sem_e0)
    contract0 = Contract(0, pieces_c, wc0, sem_c0, sem_d0)
    weights = attention_chunks(1, pieces, wa, sem_w, (0, 1, 2, 3), vraw, sem_v)
    both0[0] = u0[...]
    wait_vectors(vraw0, sem_v0)
    vector_rows(vraw0, vec0)
    out.put(vec0, vec0_o)

    def attended0():
        out.put(qkv_0, qkv_0o)
        out.put(probs_0, probs_0o)
        put_attention_inputs(out, both0, keep0_o, send0_o)

    hidden0[...] = attention_forward(
        u0[...], joined, vec0, weights0, qkv_0, probs_0, both0, n1_0, s1_0, attended0
    )
    out.put(n1_0, n1_0o)
    out.put(s1_0, s1_0o)
    expand = expand_chunks(1, pieces, wb, sem_e)
    contract = Contract(1, pieces_c, wc, sem_c, sem_d)
    values = ffn_forward(hidden0[...], vec0, expand0, contract0, act0, slope0, n2_0, s2_0)
    before = len(out.copies)
    put_halves(out, act0, hidden0, keep0_o, send0_o, ACT)
    act0_copies, out.copies = out.copies[before:], out.copies[:before]
    u = values.astype(BF)
    both[0] = u
    out.put(both.at[0], middle_o)
    wait_vectors(vraw, sem_v)
    vector_rows(vraw, vec)
    hidden[...] = attention_forward(
        u, joined, vec, weights, qkv, probs, both, n1, s1,
        lambda: put_attention_inputs(out, both, keep_o, send_o),
    )
    values = ffn_forward(hidden[...], vec, expand, contract, act, slope, n2, s2)
    put_halves(out, act, hidden, keep_o, send_o, ACT)
    kept = keep[0] > 9
    last[...] = jnp.where(kept, values.astype(BF), both[0])
    out.put(last, last_o)
    grad = jnp.where(kept, cot[...].astype(F32), 0.0)
    grad = ffn_backward(grad, vec, n2, s2, slope, expand, contract, vecs, dffn, dpre)
    put_halves(out, dpre, dffn, keep_o, send_o, DPRE)
    du = attention_backward(
        grad, vec, n1, s1, qkv, probs, weights, vecs, parts, head, lambda: None
    )
    put_attention_grads(out, parts, head, keep_o, send_o, OUTPUTS)
    passed[...] = jnp.where(kept, du.astype(BF), cot[...])
    out.put(passed, passed_o)
    wait_all(act0_copies)
    dhidden0[...] = ffn_backward(
        passed[...].astype(F32), vec0, n2_0, s2_0, slope0, expand0, contract0, vecs0, dffn0, act0
    )
    put_halves(out, act0, dffn0, keep0_o, send0_o, DPRE)
    out.put(dhidden0, dhidden_o)
    out.put(vecs0, vecs_o)
    out.drain()


def ba_kernel(layer, dhidden, vecs, vec, n1, s1, qkv_i, probs_i, *rest):
    pieces = rest[:8]
    du_o, dk_o, ds_o = rest[8:11]
    wa, parts, head, du, qkv, probs, sem_w, sem_i, sem_o = rest[11:]
    out = Out(sem_o)
    saved = [
        pltpu.make_async_copy(qkv_i, qkv, sem_i.at[0]),
        pltpu.make_async_copy(probs_i, probs, sem_i.at[1]),
    ]
    for copy in saved:
        copy.start()
    weights = attention_chunks(layer, pieces, wa, sem_w, (3, 0, 1, 2))
    du[...] = attention_backward(
        dhidden[...], vec, n1, s1, qkv, probs, weights, vecs, parts, head, lambda: wait_all(saved)
    ).astype(BF)
    put_attention_grads(out, parts, head, dk_o, ds_o, 0)
    out.put(du, du_o)
    out.drain()


def wait_all(copies):
    for copy in copies:
        copy.wait()


def slab_rows(scratch, which, blocks):
    rows = [scratch[pl.ds(pl.multiple_of(b * ROWS + which * 24, 8), 24), :] for b in blocks]
    return jnp.concatenate(rows, axis=0).astype(BF)


def bring_both(keep, send, first, to, sems, count):
    return [
        pltpu.make_async_copy(
            ref.at[pl.ds(first, BLOCK), :], to.at[pl.ds(r * BLOCK, BLOCK), :], sems.at[count + r]
        )
        for r, ref in enumerate((keep, send))
    ]


def weights_kernel(layer, before, keep, got, keep_a, got_a, *rest):
    outs_c, result = rest[:4], rest[4]
    x, d, head, grad, grad_a, staged_c, staged, sem_i, sem_o = rest[5:]
    shift = OUTPUTS if keep_a is not keep else 0
    x_in, d_in = [], []
    for i, first in enumerate((ACT, ACT + BLOCK, HIDDEN, INPUTS, INPUTS + BLOCK)):
        x_in.append(bring_both(keep, got, first, x.at[i], sem_i, 2 * i))
    for i, first in enumerate((DPRE, DPRE + BLOCK, DFFN)):
        d_in.append(bring_both(keep, got, first, d.at[i], sem_i, 10 + 2 * i))
    for i, first in enumerate((OUTPUTS, OUTPUTS + BLOCK)):
        d_in.append(bring_both(keep_a, got_a, first - shift, d.at[3 + i], sem_i, 16 + 2 * i))
    head_in = [
        pltpu.make_async_copy(
            ref.at[pl.ds(HEAD - shift, 16), :], head.at[r], sem_i.at[20 + r]
        )
        for r, ref in enumerate((keep_a, got_a))
    ]
    for pair in (d_in[2], x_in[0], x_in[1], x_in[2], d_in[0], x_in[3], d_in[3], d_in[1], x_in[4], d_in[4]):
        for copy in pair:
            copy.start()
    for copy in head_in:
        copy.start()
    out = Out(sem_o)
    wait_all(d_in[2])
    for a in range(2):
        wait_all(x_in[a])
        grad[...] = dot_tn(x[a], d[2])
        for k in range(4):
            staged_c[k, a * 192 : (a + 1) * 192] = slab_rows(
                grad, lax.rem(position(Y) + k, 4), range(8)
            )
    for k in range(4):
        out.put(staged_c.at[k], outs_c[k].at[pl.ds(layer * 384, 384), :])
    wait_all(x_in[2])
    for a in range(2):
        wait_all(d_in[a] + x_in[3 + a] + d_in[3 + a])
        grad[...] = dot_tn(x[2], d[a])
        grad_a[...] = dot_tn(x[3 + a], d[3 + a])
        for yh in range(2):
            first = (2 * yh + a) * 48
            for z in range(4):
                block = (yh * 4 + z) * ROWS
                for xs in range(4):
                    rows = pl.ds(block + xs * 24, 24)
                    staged[z * 4 + xs, first : first + 48] = jnp.concatenate(
                        [grad[rows, :], grad_a[rows, :]], axis=0
                    ).astype(BF)
            to = result.at[:, pl.ds(layer * 208 + first, 48), :]
            out.put(staged.at[:, pl.ds(first, 48), :], to)
    wait_all(head_in)
    vec = (head[0].astype(F32) + head[1].astype(F32)).astype(BF)
    for b in range(16):
        staged[b, 192:208] = vec
    out.put(staged.at[:, pl.ds(192, 16), :], result.at[:, pl.ds(layer * 208 + 192, 16), :])
    out.drain()


def finish_kernel(place, layers, vectors, iw, ib, ow, ob, fg, fs, ew, eb, cb, sg, ss):
    at = place[0]

    def cut(start):
        lane = lax.broadcasted_iota(jnp.int32, (D, 128), 0)
        to = lax.broadcasted_iota(jnp.int32, (D, 128), 1)
        return lax.dot_general(
            vectors[...],
            jnp.where(lane == to + start, 1.0, 0.0),
            (((1,), (0,)), ((), ())),
            precision=lax.Precision.HIGHEST,
            preferred_element_type=F32,
        )

    for ref, which, chunks in ((iw, 0, (0, 1, 2)), (ow, 0, (3,)), (ew, 1, (0, 1, 2, 3))):
        tiles = len(chunks) * 6
        for i, chunk in enumerate(chunks):
            for t in range(6):
                ref[pl.ds(i * 6 + t, 12, stride=tiles), :] = layers[
                    chunk, which, :, t * 128 : t * 128 + 128
                ]
    rows = cut(at * 12)
    for ref, row in ((ob, 2), (fg, 3), (fs, 4), (cb, 9), (sg, 10), (ss, 11)):
        ref[...] = rows[row : row + 1, :12]
    rows = cut(lax.rem(at, 32) * 24)
    ib[...] = jnp.where(at < 32, rows[0:1], rows[1:2])[:, :24]
    rows = cut(lax.rem(at, 16) * 48)
    which = at // 16
    eb[...] = jnp.where(
        which < 2,
        jnp.where(which == 0, rows[5:6], rows[6:7]),
        jnp.where(which == 2, rows[7:8], rows[8:9]),
    )[:, :48]


def pack_kernel(iw, ib, ow, ob, fg, fs, ew, eb, cw, cb, sg, ss, own, contract, scratch):
    scratch[96:104] = jnp.zeros((8, D), F32)
    for j in range(8):
        ref, first, tiles = (iw, j * 6, 18) if j < 3 else (ow, 0, 6)
        if j > 3:
            ref, first, tiles = ew, (j - 4) * 6, 24
        for t in range(6):
            scratch[j * 12 : (j + 1) * 12, t * 128 : t * 128 + 128] = ref[
                pl.ds(first + t, 12, stride=tiles), :
            ]
    start = 0
    for ref in (ib, ob, fg, fs, eb, cb, sg, ss):
        width = ref.shape[1]
        scratch[96:97, start : start + width] = ref[...]
        start += width
    own[...] = scratch[...].astype(BF)
    contract[...] = cw[0].astype(BF)


def shape(*dims, dtype=F32):
    return jax.ShapeDtypeStruct(dims, dtype)


def call(kernel, outs, args, in_hbm=0, scratch=(), name="kernel", outs_hbm=True, smem=0, limit=60, aliases=None):
    here = len(args) - in_hbm - smem
    in_specs = [pl.BlockSpec(memory_space=pltpu.SMEM)] * smem
    in_specs += [pl.BlockSpec(memory_space=pltpu.VMEM)] * here
    in_specs += [pl.BlockSpec(memory_space=pl.ANY)] * in_hbm
    out_space = pl.ANY if outs_hbm else pltpu.VMEM
    return pl.pallas_call(
        kernel,
        out_shape=outs,
        in_specs=in_specs,
        out_specs=[pl.BlockSpec(memory_space=out_space)] * len(outs),
        scratch_shapes=list(scratch),
        compiler_params=pltpu.CompilerParams(vmem_limit_bytes=limit * 1024 * 1024),
        cost_estimate=pl.CostEstimate(flops=1000, bytes_accessed=1024, transcendentals=0),
        input_output_aliases=aliases or {},
        name=name,
    )(*args)


ROWS_BF = shape(BLOCK, D, dtype=BF)
ROWS_F32 = shape(BLOCK, D)
SCALE = shape(BLOCK, 128)
QKV = shape(3, BLOCK, D, dtype=BF)
PROBS = shape(HEADS, BLOCK, BLOCK, dtype=BF)
SLOPE = shape(4, BLOCK, D, dtype=BF)
TWO = shape(2, BLOCK, D, dtype=BF)
THREE = shape(3, BLOCK, D, dtype=BF)
VECS = shape(16, D)
DA = shape(528, D, dtype=BF)


def vmem(*shapes):
    return [pltpu.VMEM(each.shape, each.dtype) for each in shapes]


HEAD_BF = shape(16, D, dtype=BF)
VRAW = shape(2, 4, 16, D, dtype=BF)


def middle_part(depth, u, seg, cot, pieces, pieces_c):
    saved = [ROWS_F32, SCALE, QKV, PROBS]
    gather_sems = [dma(4, 8), dma(2, 4), dma(4, 8), dma(2, 4, 4), dma(2, 4)]
    return call(
        middle_kernel,
        [ROWS_BF, ROWS_BF, ROWS_BF, ROWS_F32, VECS, *saved, VECS]
        + [shape(OUTPUTS, D, dtype=BF)] * 2
        + [shape(ALL, D, dtype=BF)] * 2,
        [depth, u, seg[:, None], seg[None, :], cot, *pieces, *pieces_c],
        10,
        [*vmem(VRAW, ROWS_BF, *saved, TWO, VECS)]
        + [WA, WC, FOUR, *vmem(SLOPE, ROWS_F32, SCALE, ROWS_BF, ROWS_F32, VECS)]
        + [WA, WA, WC, *vmem(VRAW, ROWS_BF, *saved, TWO, VECS)]
        + [FOUR, *vmem(SLOPE, ROWS_F32, SCALE, ROWS_BF)]
        + [FOUR, *vmem(ROWS_BF, VECS), FOUR, *vmem(HEAD_BF, ROWS_BF)]
        + gather_sems
        + gather_sems
        + [dma(56)],
        name="middle",
        smem=1,
    )


def first_attention_backward(dhidden, vecs, vec, n1, s1, qkv, probs, pieces):
    return call(
        lambda *refs: ba_kernel(0, *refs),
        [ROWS_BF, DA, DA],
        [dhidden, vecs, vec, n1, s1, qkv, probs, *pieces],
        10,
        [WA, FOUR, *vmem(HEAD_BF, ROWS_BF, QKV, PROBS), dma(4, 8), dma(2), dma(16)],
        name="attention_backward_0",
    )


def layer_weights(layer, args, before=()):
    count = len(before)

    def kernel(*refs):
        ins = refs[count : count + len(args)]
        ins = ins if len(args) == 4 else (*ins, *ins)
        weights_kernel(layer, refs[:count], *ins, *refs[count + len(args) :])

    both_cores = pltpu.VMEM((5, 2 * BLOCK, D), BF)
    grad = pltpu.VMEM((D, D), F32)
    return call(
        kernel,
        [shape(768, D, dtype=BF)] * 4 + [shape(16, 416, D, dtype=BF)],
        list(before) + args,
        count + len(args),
        [both_cores, both_cores, pltpu.VMEM((2, 16, D), BF), grad, grad]
        + [pltpu.VMEM((4, 384, D), BF), pltpu.VMEM((16, 208, D), BF), dma(22), dma(12)],
        name=f"weights_{layer}",
        aliases={i: i for i in range(count)},
    )


def gather(masters):
    core = lax.axis_index("core")
    own, contract = call(
        pack_kernel,
        [shape(104, D, dtype=BF), shape(48, D, dtype=BF)],
        [each.reshape(-1, 128) if i in (0, 2, 6) else each for i, each in enumerate(masters)],
        0,
        [pltpu.VMEM((104, D), F32)],
        name="pack",
        outs_hbm=False,
    )
    own = from_behind(own, "x")
    contract = [contract] + [ahead_crossed(contract, k, 0) for k in (1, 2, 3)]
    contract, own = lax.optimization_barrier((contract, own))
    contract = by_position(contract, jnp.where(core == 0, position(Y), position("z")))
    along_x = by_position(own, position("x"))
    other = swap_core(along_x)
    first, second = jnp.where(core == 0, along_x, other), jnp.where(core == 0, other, along_x)
    both = jnp.stack([first, second])
    chunks = both[:, :, :96].reshape(2, 4, 8, 12, D).transpose(2, 1, 0, 3, 4).reshape(8, ROWS, D)
    vector = both[:, :, 96].transpose(1, 0, 2).reshape(8, D)
    chunks = lax.dynamic_slice_in_dim(chunks, 4 * core, 4, 0).reshape(384, D)
    load = jnp.concatenate([chunks, vector, jnp.zeros((8, D), BF)], axis=0)
    load = jnp.stack([load] + [ahead_crossed(load, k, 0) for k in (1, 2, 3)])
    contract = lax.optimization_barrier((contract, load))[0]
    contract = jnp.stack([contract] + [ahead_crossed(contract, k, 1) for k in (1, 2, 3)])
    contract = lax.all_gather(contract, "x", axis=0)
    near = [ahead_crossed(load, k, 1) for k in (1, 3)]
    load, near = lax.optimization_barrier((load, near))
    far = ahead_crossed(load, 2, 1)
    other = [swap_core(piece) for piece in (load, *near)]
    far, other = lax.optimization_barrier((far, other))
    other_c, other_far = swap_core(contract), swap_core(far)
    pieces = [load, near[0], far, near[1], other[0], other[1], other_far, other[2]]
    return pieces, [contract, other_c]


def summed(pieces):
    total = pieces[0].astype(F32)
    for piece in pieces[1:]:
        total = total + piece.astype(F32)
    return total


def scatter_ahead(pieces, axis):
    return [pieces[0]] + [ahead(pieces[k], axis, k) for k in (1, 2, 3)]


def pieces_ahead(parts, axis):
    here = position(axis)
    return [lax.dynamic_index_in_dim(parts, (here + k) % 4, 0, keepdims=False) for k in range(4)]


def reduce_along(parts, axis):
    return summed(scatter_ahead(pieces_ahead(parts, axis), axis))


def reduce_contract(parts):
    c = summed(scatter_ahead(parts, Y)).astype(BF).reshape(2, 4, ROWS, D)
    c = reduce_along(c.transpose(1, 0, 2, 3).reshape(4, 2 * ROWS, D), "z")
    c = c.astype(BF).reshape(2, 4, 24, D).transpose(1, 0, 2, 3).reshape(4, 48, D)
    return reduce_along(c, "x").reshape(2, 24, D)


def reduce_last(sums, contract):
    section, core = lax.axis_index("section"), lax.axis_index("core")
    sums = sums.reshape(2, 208, D)
    by_y = sums[:, :192].reshape(2, 4, 48, D).transpose(1, 0, 2, 3)
    vectors = jnp.broadcast_to(sums[None, :, 192:], (4, 2, 16, D))
    by_y = jnp.concatenate([by_y, vectors], axis=2).reshape(4, 128, D)
    both = reduce_along(by_y, Y).reshape(2, 64, D)
    mine = lax.dynamic_index_in_dim(both, section, 0, keepdims=False)
    others = lax.dynamic_index_in_dim(both, 1 - section, 0, keepdims=False)
    vec = mine[48:]
    own_c = lax.dynamic_index_in_dim(contract, section, 0, keepdims=False)
    others_c = lax.dynamic_index_in_dim(contract, 1 - section, 0, keepdims=False)
    mine, others = [mine[24:48], mine[:24], own_c], [others[24:48], others[:24], others_c]
    near, far = crossed_owner(mine[2], False), crossed_owner(others[2], True)
    contract = jnp.concatenate(
        [jnp.where(section == 0, near, far), jnp.where(section == 0, far, near)]
    )
    mine, others = (jnp.stack(each[:2]).reshape(2, 2, 12, D) for each in (mine, others))

    def rows_of(value, which):
        return lax.dynamic_index_in_dim(value, which, 1, keepdims=False)

    here = rows_of(mine, core)
    near = to_neighbour(rows_of(mine, 1 - core), False, True)
    far = to_neighbour(rows_of(others, core), True, False)
    far_near = to_neighbour(rows_of(others, 1 - core), True, True)
    own, other = jnp.stack([here, far]), jnp.stack([near, far_near])
    low, high = jnp.where(core == 0, own, other), jnp.where(core == 0, other, own)
    flip = section == 0
    chunks = [jnp.where(flip, low[0], low[1]), jnp.where(flip, low[1], low[0])]
    chunks += [jnp.where(flip, high[0], high[1]), jnp.where(flip, high[1], high[0])]
    return jnp.stack(chunks), contract, vec


def to_neighbour(value, other_section, other_core):
    pairs = []
    for s in range(2):
        for c in range(2):
            to = (1 - s if other_section else s) * 2 + (1 - c if other_core else c)
            pairs.append((s * 2 + c, to))
    return lax.ppermute(value, ("section", "core"), pairs)


def crossed_owner(value, other_section):
    pairs = []
    for s in range(2):
        for yh in range(2):
            for c in range(2):
                to = 1 - s if other_section else s
                pairs.append(((s * 2 + yh) * 2 + c, (to * 2 + c) * 2 + yh))
    return lax.ppermute(value, ("section", "yh", "core"), pairs)


def on_device(tokens, segment_ids, depth, *rest):
    masters = rest[:12]
    cotangent = rest[12]
    section = lax.axis_index("section")
    place = (
        lax.axis_index("yh") * 32
        + lax.axis_index("z") * 8
        + lax.axis_index("x") * 2
        + lax.axis_index("core")
    )
    u = lax.dynamic_slice_in_dim(tokens, section * BLOCK, BLOCK, 0)
    seg = lax.dynamic_slice_in_dim(segment_ids, section * BLOCK, BLOCK, 0)
    cot = lax.dynamic_slice_in_dim(cotangent, section * BLOCK, BLOCK, 0)

    def halves(of_first, of_second):
        mine = jnp.where(section == 0, of_first, of_second)
        theirs = ahead(jnp.where(section == 0, of_second, of_first), "section", 1)
        return jnp.concatenate(
            [jnp.where(section == 0, mine, theirs), jnp.where(section == 0, theirs, mine)]
        )[None]

    pieces, pieces_c = gather(masters)
    middle, last, passed, dhidden, vecs, *grads = middle_part(depth, u, seg, cot, pieces, pieces_c)
    *saved0, vec0, keep0, send0, keep1, send1 = grads
    first, keep_a, send_a = first_attention_backward(dhidden, vecs, vec0, *saved0, pieces)
    got1 = swap_core(send1)
    first, got1 = lax.optimization_barrier((first, got1))
    *parts, sums = layer_weights(1, [keep1, got1])
    got0, got_a = swap_core(send0), swap_core(send_a)
    sums, got0, got_a = lax.optimization_barrier((sums, got0, got_a))
    *parts, sums = layer_weights(0, [keep0, got0, keep_a, got_a], (*parts, sums))
    sums = lax.psum_scatter(
        sums.reshape(16 * 416, D), ("z", "x"), scatter_dimension=0, tiled=True
    )
    contract = reduce_contract(parts)
    layer_outputs, input_grads = halves(middle, last), halves(first, passed)
    sums, contract, layer_outputs, input_grads = lax.optimization_barrier(
        (sums, contract, layer_outputs, input_grads)
    )
    chunks, cw, vec = reduce_last(sums, contract)
    one, small = shape(1, 12), [shape(1, 24), shape(1, 48)]
    iw, ib, ow, ob, fg, fs, ew, eb, cb, sg, ss = call(
        finish_kernel,
        [shape(216, 128), small[0], shape(72, 128), one, one, one, shape(288, 128), small[1]]
        + [one, one, one],
        [place[None], chunks, vec],
        smem=1,
        name="finish",
        outs_hbm=False,
    )
    return (
        layer_outputs,
        input_grads,
        iw.reshape(1, 12, 3 * D),
        ib,
        ow.reshape(1, 12, D),
        ob,
        fg,
        fs,
        ew.reshape(1, 12, 4 * D),
        eb,
        cw[None],
        cb,
        sg,
        ss,
    )


def solution(mesh):
    wide = Mesh(mesh.devices.reshape(2, 2, 4, 4, 2), ("section", "yh", "z", "x", "core"))
    dp = ("yh", "z", "x", "core")
    matrix, vector = P("section", dp, None), P("section", dp)
    rows = P(dp, None)
    weights = (
        matrix,
        vector,
        matrix,
        vector,
        vector,
        vector,
        matrix,
        vector,
        matrix,
        vector,
        vector,
        vector,
    )
    return jax.shard_map(
        on_device,
        mesh=wide,
        in_specs=(rows, P(dp), P(dp)) + weights + (rows,),
        out_specs=(matrix, matrix) + weights,
        check_vma=False,
    )
```

```python
import jax
import jax.numpy as jnp
from jax import lax
from jax.experimental import pallas as pl
from jax.experimental.pallas import tpu as pltpu
from jax.sharding import Mesh, PartitionSpec as P

D = 768
HEADS = 12
BLOCK = 256
EPS = 1e-05
Y = ("section", "yh")
ROWS = 96
BF = jnp.bfloat16
F32 = jnp.float32


def position(axis):
    if isinstance(axis, tuple):
        return lax.axis_index("yh") * 2 + lax.axis_index("section")
    return lax.axis_index(axis)


def size_of(axis):
    return 4 if isinstance(axis, tuple) else lax.axis_size(axis)


def ahead(value, axis, steps):
    count = size_of(axis)
    at = [0, 2, 1, 3] if isinstance(axis, tuple) else range(count)
    return lax.ppermute(value, axis, [(at[i], at[(i + steps) % count]) for i in range(count)])


def from_behind(value, axis):
    return [value] + [ahead(value, axis, k) for k in (1, 2, 3)]


def by_position(pieces, here):
    rising = [pieces[0], pieces[3], pieces[2], pieces[1]]
    return lax.dynamic_slice_in_dim(jnp.stack(rising + rising), (4 - here) % 4, 4, 0)


def ahead_by_core(value, steps, first, second):
    pairs = []
    for place in range(128):
        at = {"y": place // 32, "z": place // 8 % 4, "x": place // 2 % 4}
        core = place % 2
        to = dict(at)
        axis = second if core else first
        to[axis] = (to[axis] + steps) % 4
        flat = [
            ((((p["y"] % 2) * 2 + p["y"] // 2) * 4 + p["z"]) * 4 + p["x"]) * 2 + core
            for p in (at, to)
        ]
        pairs.append(tuple(flat))
    return lax.ppermute(value, ("section", "yh", "z", "x", "core"), pairs)


def swap_core(value):
    return ahead(value, "core", 1)


def behind(axis, k):
    return lax.rem(position(axis) + (4 - k), 4)


class Chunks:
    def __init__(self, to, sems):
        self.to, self.sems, self.here = to, sems, set()

    def bring(self, j, source, yh, z):
        block = yh * 4 + z
        rows = pl.ds(pl.multiple_of(block * ROWS, ROWS), ROWS)
        pltpu.make_async_copy(
            source.at[pl.ds(j * ROWS, ROWS), :], self.to.at[j, rows, :], self.sems.at[j, block]
        ).start()

    def wait(self):
        for j in range(4):
            self.get(j)

    def get(self, j):
        for block in range(0 if j in self.here else 8):
            here = self.to.at[j, pl.ds(block * ROWS, ROWS), :]
            pltpu.make_async_copy(here, here, self.sems.at[j, block]).wait()
        self.here.add(j)
        return self.to[j]


def entry(pieces, k, i, high):
    if k == 2:
        return pieces[4 if high else 3].at[i - 2 if high else i]
    return pieces[(0, 1, None, 2)[k]].at[i]


def attention_chunks(layer, pieces, to, sems, order, vraw=None, sem_v=None):
    chunks = Chunks(to, sems)
    core = lax.axis_index("core")
    away = jnp.where(lax.axis_index("section") == layer, 0, 1)
    for r in range(2):

        @pl.when(core == r)
        def _():
            def each(act):
                for k in range(4):
                    for e in range(2):
                        steps = 2 * e + away
                        yh = lax.rem(position(Y) + 4 - steps, 4) // 2
                        act(entry(pieces[5 * r : 5 * r + 5], k, steps, e == 1), yh, behind("z", k))

            if vraw is not None:
                each(
                    lambda piece, yh, z: pltpu.make_async_copy(
                        piece.at[pl.ds(4 * ROWS, 16), :], vraw.at[yh, z], sem_v.at[yh, z]
                    ).start()
                )
            for j in order:
                each(lambda piece, yh, z: chunks.bring(j, piece, yh, z))

    return chunks


def expand_chunks(layer, pieces, to, sems):
    chunks = Chunks(to, sems)
    core = lax.axis_index("core")
    for j in range(4):
        for k in range(4):
            ys = behind(Y, k)
            for r in range(2):

                @pl.when(jnp.logical_and(lax.rem(ys, 2) == layer, core == 1 - r))
                def _():
                    for e in range(4):
                        piece = entry(pieces[5 * r : 5 * r + 5], k, e, e > 1)
                        chunks.bring(j, piece, ys // 2, behind("z", e))

    return chunks


class Contract:
    def __init__(self, layer, pieces, to, sems_0, sems_1):
        self.to, self.sems_0, self.sems_1, self.here = to, sems_0, sems_1, set()
        core = lax.axis_index("core")
        for r in range(2):
            mine = pieces[5 * r : 5 * r + 5]
            for yh in range(2):

                @pl.when(core == r)
                def _():
                    for k in range(4):
                        z = behind("z", k)
                        for i in range(4):
                            x = behind("x", i)
                            pltpu.make_async_copy(
                                entry(mine, i, k, k > 1).at[yh * 2 + layer],
                                to.at[yh, z, x, 0],
                                sems_0.at[yh, z, x],
                            ).start()

            for k in range(4):
                ys = behind(Y, k)

                @pl.when(jnp.logical_and(core == 1 - r, lax.rem(ys, 2) == layer))
                def _():
                    for i in range(4):
                        x = behind("x", i)
                        pltpu.make_async_copy(
                            entry(mine, i, k, k > 1), to.at[ys // 2, :, x, 1], sems_1.at[ys // 2, x]
                        ).start()

    def wait(self):
        for j in range(4):
            self.get(j)

    def get(self, j):
        yh, first = j // 2, (j % 2) * 2
        for x in range(0 if j in self.here else 4):
            for z in (first, first + 1):
                here = self.to.at[yh, z, x, 0]
                pltpu.make_async_copy(here, here, self.sems_0.at[yh, z, x]).wait()
            if first == 0:
                here = self.to.at[yh, :, x, 1]
                pltpu.make_async_copy(here, here, self.sems_1.at[yh, x]).wait()
        self.here.add(j)
        return self.to[yh, first : first + 2].reshape(D, D)


class Out:
    def __init__(self, sems):
        self.sems, self.copies, self.count = sems, [], 0

    def put(self, source, to):
        copy = pltpu.make_async_copy(source, to, self.sems.at[self.count])
        copy.start()
        self.copies.append(copy)
        self.count += 1

    def put_either(self, source, of_first, of_second, first):
        sem, rows = self.sems.at[self.count], pl.ds(first, source.shape[0])
        for core, ref in enumerate((of_first, of_second)):

            @pl.when(lax.axis_index("core") == core)
            def _():
                pltpu.make_async_copy(source, ref.at[rows, :], sem).start()

        self.copies.append(pltpu.make_async_copy(source, of_first.at[rows, :], sem))
        self.count += 1

    def drain(self):
        for copy in self.copies:
            copy.wait()


WA = pltpu.VMEM((4, D, D), BF)
WC = pltpu.VMEM((2, 4, 4, 2, 48, D), BF)
FOUR = pltpu.VMEM((4, BLOCK, D), BF)


def dma(*count):
    return pltpu.SemaphoreType.DMA(count)


def dot(left, right):
    return lax.dot_general(left, right, (((1,), (0,)), ((), ())), preferred_element_type=F32)


def dot_nt(left, right):
    return lax.dot_general(left, right, (((1,), (1,)), ((), ())), preferred_element_type=F32)


def dot_tn(left, right):
    return lax.dot_general(left, right, (((0,), (0,)), ((), ())), preferred_element_type=F32)


def norm_of(residual):
    centre = residual - jnp.mean(residual, axis=1, keepdims=True)
    scaled = lax.rsqrt(jnp.mean(centre * centre, axis=1, keepdims=True) + EPS)
    return centre * scaled, scaled


def norm_back(grad_out, normed, scaled, gain):
    grad_normed = grad_out * gain
    inner = (
        grad_normed
        - jnp.mean(grad_normed, axis=1, keepdims=True)
        - normed * jnp.mean(grad_normed * normed, axis=1, keepdims=True)
    )
    return (
        scaled * inner,
        jnp.sum(grad_out * normed, axis=0, keepdims=True),
        jnp.sum(grad_out, axis=0, keepdims=True),
    )


def head_masks():
    lane = lax.broadcasted_iota(jnp.int32, (BLOCK, 128), 1)
    return lane < 64


def vector_rows(vraw, out):
    groups = [vraw[yh, z][0:8, :256].astype(F32) for yh in range(2) for z in range(4)]
    values = jnp.concatenate(groups, axis=0).astype(BF)
    lane = lax.broadcasted_iota(jnp.int32, (64, D), 1)
    device = lax.broadcasted_iota(jnp.int32, (64, D), 0)

    def rows(start, width, count):
        found = []
        for r in range(count):
            spread = jnp.where(device == (lane + r * D) // width, 1.0, 0.0).astype(BF)
            wide = dot_tn(values[:, start : start + width], spread)
            entry = lax.broadcasted_iota(jnp.int32, wide.shape, 0)
            at = lax.broadcasted_iota(jnp.int32, wide.shape, 1) + r * D
            found.append(
                jnp.sum(jnp.where(entry == at % width, wide, 0.0), axis=0, keepdims=True)
            )
        return found

    found = rows(0, 24, 2)
    for start in (24, 36, 48):
        found += rows(start, 12, 1)
    found += rows(60, 48, 4)
    for start in (108, 120, 132):
        found += rows(start, 12, 1)
    out[...] = jnp.concatenate(found + [jnp.zeros((4, D), F32)], axis=0)


def column_sum(values):
    return jnp.sum(values.astype(F32), axis=0, keepdims=True)


def attention_forward(u, joined, vec, weights, qkv, probs, both, normed, scaled, attended):
    q = ((dot(u, weights.get(0)) + vec[0:1]) * 0.125).astype(BF)
    k = dot(u, weights.get(1)).astype(BF)
    v = (dot(u, weights.get(2)) + vec[1:2]).astype(BF)
    qkv[0] = q
    qkv[1] = k
    qkv[2] = v
    low_half = head_masks()
    for pair in range(HEADS // 2):
        lanes = slice(pair * 128, pair * 128 + 128)
        q2, k2, v2 = q[:, lanes], k[:, lanes], v[:, lanes]
        outs = []
        for h in range(2):
            mine = low_half if h == 0 else jnp.logical_not(low_half)
            scores = dot_nt(jnp.where(mine, q2, jnp.zeros_like(q2)), k2)
            scores = jnp.where(joined, scores, -1e30)
            top = jnp.max(scores, axis=1, keepdims=True)
            exponent = jnp.exp(scores - top)
            total = jnp.sum(exponent, axis=1, keepdims=True)
            rows = (exponent / total).astype(BF)
            probs[2 * pair + h] = rows
            outs.append(dot(rows, v2))
        both[1, :, lanes] = jnp.where(low_half, outs[0], outs[1]).astype(BF)
    attended()
    branch = dot(both[1], weights.get(3)) + vec[2:3]
    n1, s1 = norm_of(u.astype(F32) + branch)
    normed[...] = n1
    scaled[...] = jnp.broadcast_to(s1, (BLOCK, 128))
    return (n1 * vec[3:4] + vec[4:5]).astype(BF)


def ffn_forward(hidden, vec, expand, contract, act, slope, normed, scaled):
    expand.wait()
    contract.wait()
    for j in range(4):
        pre = dot(hidden, expand.get(j)) + vec[5 + j : 6 + j]
        half = 0.5 * (1.0 + lax.erf(pre * 0.7071067811865476))
        act[j] = (pre * half).astype(BF)
        slope[j] = (half + pre * jnp.exp(-0.5 * pre * pre) * 0.3989422804014327).astype(BF)
    total = hidden.astype(F32) + vec[9:10]
    for j in range(4):
        total = total + dot(act[j], contract.get(j))
    n2, s2 = norm_of(total)
    normed[...] = n2
    scaled[...] = jnp.broadcast_to(s2, (BLOCK, 128))
    return n2 * vec[10:11] + vec[11:12]


def ffn_backward(grad, vec, n2, s2, slope, expand, contract, vecs, dffn_ref, dpre_ref):
    dr2, dgain, dshift = norm_back(grad, n2[...], s2[:, 0:1], vec[10:11])
    dffn = dr2.astype(BF)
    dffn_ref[...] = dffn
    vecs[...] = jnp.zeros((16, D), F32)
    vecs[9:10] = column_sum(dffn)
    vecs[10:11] = dgain
    vecs[11:12] = dshift
    for j in range(4):
        dact = dot_nt(dffn, contract.get(j))
        dpre = (dact * slope[j].astype(F32)).astype(BF)
        dpre_ref[j] = dpre
        vecs[5 + j : 6 + j] = column_sum(dpre)
    total = dr2
    for j in range(4):
        total = total + dot_nt(dpre_ref[j], expand.get(j))
    return total


def attention_backward(dhidden, vec, n1, s1, qkv, probs, weights, vecs, parts, head, ready):
    dr1, dgain, dshift = norm_back(dhidden, n1[...], s1[:, 0:1], vec[3:4])
    parts[3] = dr1.astype(BF)
    dattended = dot_nt(parts[3], weights.get(3)).astype(BF)
    ready()
    low_half = head_masks()
    for pair in range(HEADS // 2):
        lanes = slice(pair * 128, pair * 128 + 128)
        q2, k2, v2 = qkv[0, :, lanes], qkv[1, :, lanes], qkv[2, :, lanes]
        do2 = dattended[:, lanes]
        dqs = []
        dk2 = jnp.zeros((BLOCK, 128), F32)
        dv2 = jnp.zeros((BLOCK, 128), F32)
        for h in range(2):
            mine = low_half if h == 0 else jnp.logical_not(low_half)
            do_h = jnp.where(mine, do2, jnp.zeros_like(do2))
            rows_low = probs[2 * pair + h]
            rows = rows_low.astype(F32)
            dprobs = dot_nt(do_h, v2)
            dscores = (
                rows * (dprobs - jnp.sum(rows * dprobs, axis=1, keepdims=True))
            ).astype(BF)
            dqs.append(dot(dscores, k2))
            dk2 = dk2 + dot_tn(dscores, jnp.where(mine, q2, jnp.zeros_like(q2)))
            dv2 = dv2 + dot_tn(rows_low, do_h)
        parts[0, :, lanes] = (jnp.where(low_half, dqs[0], dqs[1]) * 0.125).astype(BF)
        parts[1, :, lanes] = dk2.astype(BF)
        parts[2, :, lanes] = dv2.astype(BF)
    total = dr1
    for j in range(3):
        total = total + dot_nt(parts[j], weights.get(j))
    head[...] = jnp.concatenate(
        [column_sum(parts[0]), column_sum(parts[2]), column_sum(parts[3]), dgain, dshift, vecs[5:16]],
        axis=0,
    ).astype(BF)
    return total


INPUTS, OUTPUTS, ACT, DFFN, HEAD, ALL = 0, 512, 1536, 2048, 2304, 2320


def put_act(out, act, keep, send):
    core = lax.axis_index("core")
    for to, half in ((keep, core), (send, 1 - core)):
        for j in range(2):
            out.put(act.at[2 * half + j], to.at[pl.ds(ACT + j * BLOCK, BLOCK), :])


def put_dffn(out, dffn, keep, send):
    for to in (keep, send):
        out.put(dffn, to.at[pl.ds(DFFN, BLOCK), :])


def put_four(out, first, second, rows, four):
    for j in range(4):
        out.put_either(four.at[j], first, second, rows + j * BLOCK)


def wait_vectors(vraw, sems):
    for yh in range(2):
        for z in range(4):
            here = vraw.at[yh, z]
            pltpu.make_async_copy(here, here, sems.at[yh, z]).wait()


def middle_kernel(keep, u0, sc, sr, cot, *rest):
    pieces, pieces_c = rest[:10], rest[10:20]
    middle_o, last_o, passed_o, dhidden_o, vecs_o = rest[20:25]
    n1_0o, s1_0o, qkv_0o, probs_0o, vec0_o, keep0_o, send0_o, keep_o, send_o = rest[25:34]
    rest = rest[34:]
    vraw0, hidden0, n1_0, s1_0, qkv_0, probs_0, both0, vec0 = rest[:8]
    we0, wc0, act0, slope0, n2_0, s2_0, dffn0, dhidden0, vecs0 = rest[8:17]
    wa, wb, wc, vraw, hidden, n1, s1, qkv, probs, both, vec = rest[17:28]
    act, slope, n2, s2, last, dpre, dffn, vecs, parts, head, passed = rest[28:39]
    sem_w0, sem_v0, sem_e0, sem_c0, sem_d0, sem_w, sem_v, sem_e, sem_c, sem_d, sem_o = rest[39:]
    out = Out(sem_o)
    joined = sc[...] == sr[...]
    weights0 = attention_chunks(0, pieces, wb, sem_w0, (0, 1, 2, 3), vraw0, sem_v0)
    expand0 = expand_chunks(0, pieces, we0, sem_e0)
    contract0 = Contract(0, pieces_c, wc0, sem_c0, sem_d0)
    weights = attention_chunks(1, pieces, wa, sem_w, (0, 1, 2, 3), vraw, sem_v)
    both0[0] = u0[...]
    wait_vectors(vraw0, sem_v0)
    vector_rows(vraw0, vec0)
    out.put(vec0, vec0_o)

    def attended0():
        out.put(qkv_0, qkv_0o)
        out.put(probs_0, probs_0o)
        out.put_either(both0.at[0], keep0_o, send0_o, INPUTS)
        out.put_either(both0.at[1], keep0_o, send0_o, INPUTS + BLOCK)

    hidden0[...] = attention_forward(
        u0[...], joined, vec0, weights0, qkv_0, probs_0, both0, n1_0, s1_0, attended0
    )
    out.put(n1_0, n1_0o)
    out.put(s1_0, s1_0o)
    expand = expand_chunks(1, pieces, wb, sem_e)
    contract = Contract(1, pieces_c, wc, sem_c, sem_d)
    values = ffn_forward(hidden0[...], vec0, expand0, contract0, act0, slope0, n2_0, s2_0)
    before = len(out.copies)
    put_act(out, act0, keep0_o, send0_o)
    act0_copies, out.copies = out.copies[before:], out.copies[:before]
    for j in range(2):
        out.put_either(hidden0, send0_o, keep0_o, INPUTS + j * BLOCK)
    u = values.astype(BF)
    both[0] = u
    out.put(both.at[0], middle_o)
    wait_vectors(vraw, sem_v)
    vector_rows(vraw, vec)

    def attended():
        out.put_either(both.at[0], keep_o, send_o, INPUTS)
        out.put_either(both.at[1], keep_o, send_o, INPUTS + BLOCK)

    hidden[...] = attention_forward(u, joined, vec, weights, qkv, probs, both, n1, s1, attended)
    for j in range(2):
        out.put_either(hidden, send_o, keep_o, INPUTS + j * BLOCK)
    values = ffn_forward(hidden[...], vec, expand, contract, act, slope, n2, s2)
    put_act(out, act, keep_o, send_o)
    kept = keep[0] > 9
    last[...] = jnp.where(kept, values.astype(BF), both[0])
    out.put(last, last_o)
    grad = jnp.where(kept, cot[...].astype(F32), 0.0)
    grad = ffn_backward(grad, vec, n2, s2, slope, expand, contract, vecs, dffn, dpre)
    put_four(out, send_o, keep_o, OUTPUTS, dpre)
    put_dffn(out, dffn, keep_o, send_o)
    du = attention_backward(
        grad, vec, n1, s1, qkv, probs, weights, vecs, parts, head, lambda: None
    )
    put_four(out, keep_o, send_o, OUTPUTS, parts)
    out.put_either(head, keep_o, send_o, HEAD)
    passed[...] = jnp.where(kept, du.astype(BF), cot[...])
    out.put(passed, passed_o)
    wait_all(act0_copies)
    dhidden0[...] = ffn_backward(
        passed[...].astype(F32), vec0, n2_0, s2_0, slope0, expand0, contract0, vecs0, dffn0, act0
    )
    put_four(out, send0_o, keep0_o, OUTPUTS, act0)
    put_dffn(out, dffn0, keep0_o, send0_o)
    out.put(dhidden0, dhidden_o)
    out.put(vecs0, vecs_o)
    out.drain()


def ba_kernel(layer, dhidden, vecs, vec, n1, s1, qkv_i, probs_i, *rest):
    pieces = rest[:10]
    du_o, grads_o = rest[10:12]
    wa, parts, head, du, qkv, probs, sem_w, sem_i, sem_o = rest[12:]
    out = Out(sem_o)
    saved = [
        pltpu.make_async_copy(qkv_i, qkv, sem_i.at[0]),
        pltpu.make_async_copy(probs_i, probs, sem_i.at[1]),
    ]
    for copy in saved:
        copy.start()
    weights = attention_chunks(layer, pieces, wa, sem_w, (3, 0, 1, 2))
    du[...] = attention_backward(
        dhidden[...], vec, n1, s1, qkv, probs, weights, vecs, parts, head, lambda: wait_all(saved)
    ).astype(BF)
    for j in range(4):
        out.put(parts.at[j], grads_o.at[pl.ds(j * BLOCK, BLOCK), :])
    out.put(head, grads_o.at[pl.ds(4 * BLOCK, 16), :])
    out.put(du, du_o)
    out.drain()


def wait_all(copies):
    for copy in copies:
        copy.wait()


def slab_rows(scratch, which, blocks):
    rows = [scratch[pl.ds(pl.multiple_of(b * ROWS + which * 24, 8), 24), :] for b in blocks]
    return jnp.concatenate(rows, axis=0).astype(BF)


def wait_all(copies):
    for copy in copies:
        copy.wait()


def slab_rows(scratch, which, blocks):
    rows = [scratch[pl.ds(pl.multiple_of(b * ROWS + which * 24, 8), 24), :] for b in blocks]
    return jnp.concatenate(rows, axis=0).astype(BF)


def bring_both(keep, send, first, to, sems, count):
    return [
        pltpu.make_async_copy(
            ref.at[pl.ds(first, BLOCK), :], to.at[pl.ds(r * BLOCK, BLOCK), :], sems.at[count + r]
        )
        for r, ref in enumerate((keep, send))
    ]


def weights_kernel(layer, ins, *rest):
    outs, outs_c = rest[:4], rest[4:8]
    x, d, act, dffn, head, grad, staged, staged_c, sem_i, sem_o = rest[8:]
    core = lax.axis_index("core")
    keep, got = ins[:2]

    def bring(first, to, count):
        return [
            pltpu.make_async_copy(
                ref.at[pl.ds(first, BLOCK), :], to.at[pl.ds(r * BLOCK, BLOCK), :], sem_i.at[count + r]
            )
            for r, ref in enumerate((keep, got))
        ]

    dffn_in = bring(DFFN, dffn, 0)
    act_in = [bring(ACT + j * BLOCK, act.at[j], 2 + 2 * j) for j in range(2)]
    x_in = [bring(INPUTS + j * BLOCK, x.at[j], 6 + 2 * j) for j in range(2)]
    d_in = [bring(OUTPUTS + j * BLOCK, d.at[j], 10 + 2 * j) for j in range(4)]
    for pair in (dffn_in, *act_in, *x_in):
        for copy in pair:
            copy.start()
    if len(ins) == 2:
        for pair in d_in:
            for copy in pair:
                copy.start()
        heads = [ref.at[pl.ds(HEAD, 16), :] for ref in ins]
    else:
        heads = [ref.at[pl.ds(4 * BLOCK, 16), :] for ref in ins[2:]]

        @pl.when(core == 1)
        def _():
            for pair in d_in:
                for copy in pair:
                    copy.start()

        @pl.when(core == 0)
        def _():
            for j in range(4):
                for r, ref in enumerate(ins[2:]):
                    pltpu.make_async_copy(
                        ref.at[pl.ds(j * BLOCK, BLOCK), :],
                        d.at[j, pl.ds(r * BLOCK, BLOCK), :],
                        sem_i.at[10 + 2 * j + r],
                    ).start()

    head_in = [
        pltpu.make_async_copy(ref, head.at[r], sem_i.at[18 + r]) for r, ref in enumerate(heads)
    ]
    for copy in head_in:
        copy.start()
    out = Out(sem_o)
    wait_all(dffn_in)
    for a in range(2):
        wait_all(act_in[a])
        grad[a] = dot_tn(act[a], dffn[...])
        for k in range(4):
            staged_c[k, a * 192 : (a + 1) * 192] = slab_rows(
                grad.at[a], lax.rem(position(Y) + k, 4), range(8)
            )
    for k in range(4):
        out.put(staged_c.at[k], outs_c[k].at[pl.ds(layer * 384, 384), :])
    wait_all(head_in)
    vec = (head[0].astype(F32) + head[1].astype(F32)).astype(BF)
    wait_all(x_in[0] + x_in[1])
    for j in range(4):
        wait_all(d_in[j])
        here, of_j = slice(j * 192, (j + 1) * 192), grad.at[j % 2]
        of_j[...] = dot_tn(x[j // 3], d[j])

        @pl.when(core == 0)
        def _():
            for k in range(4):
                z = lax.rem(position("z") + k, 4)
                rows = [
                    of_j[pl.ds(pl.multiple_of((yh * 4 + z) * ROWS, 8), ROWS), :] for yh in range(2)
                ]
                staged[k, here] = jnp.concatenate(rows, axis=0).astype(BF)

        @pl.when(core == 1)
        def _():
            for k in range(4):
                staged[k, here] = slab_rows(of_j, lax.rem(position("x") + k, 4), range(8))

        if j % 2:
            for k in range(4):
                rows = (j - 1) * 192
                to = outs[k].at[pl.ds(layer * 768 + rows, 384), :]
                out.put(staged.at[k, pl.ds(rows, 384), :], to)
    for k in range(4):
        staged[k, 768:784] = vec
        to = outs[k].at[pl.ds(1536 + layer * 16, 16), :]
        out.put(staged.at[k, pl.ds(768, 16), :], to)
    out.drain()


def sum_parts(parts, to):
    rows = to.shape[0]
    step = 16 * max(n for n in range(1, 13) if rows % (16 * n) == 0)

    @pl.loop(0, rows // step)
    def _(i):
        here = pl.ds(pl.multiple_of(i * step, 16), step)
        total = parts[0][here, :].astype(F32)
        for part in parts[1:]:
            total = total + part[here, :].astype(F32)
        to[here, :] = total


def pick_rows(total, starts, count):
    rows = [total[pl.ds(pl.multiple_of(start, 8), count), :] for start in starts]
    return jnp.concatenate(rows, axis=0).astype(BF)


def second_cut_kernel(*refs):
    parts, parts_c = refs[:4], refs[4:8]
    outs, outs_c = refs[8:12], refs[12:16]
    total, total_c = refs[16:]
    core = lax.axis_index("core")
    sum_parts(parts_c, total_c)
    for k in range(4):
        x = lax.rem(position("x") + k, 4)
        starts = [layer * 384 + (z * 4 + x) * 24 for layer in range(2) for z in range(4)]
        outs_c[k][...] = pick_rows(total_c, starts, 24)
    sum_parts(parts, total)

    @pl.when(core == 0)
    def _():
        for k in range(4):
            y = lax.rem(position(Y) + k, 4)
            first = lax.rem(y, 2) * 384 + (y // 2) * ROWS
            starts = [layer * 768 + first + j * 192 for layer in range(2) for j in range(2)]
            outs[k][0:384] = pick_rows(total, starts, ROWS)
            outs[k][384:416] = total[1536:1568, :].astype(BF)

    @pl.when(core == 1)
    def _():
        for k in range(4):
            z = lax.rem(position("z") + k, 4)
            starts = [
                layer * 768 + j * 192 + (yh * 4 + z) * 24
                for layer in range(2)
                for j in range(4)
                for yh in range(2)
            ]
            outs[k][0:384] = pick_rows(total, starts, 24)
            outs[k][384:416] = jnp.zeros((32, D), BF)


def third_cut_kernel(*refs):
    parts, parts_c = refs[:4], refs[4:8]
    outs, outs_c = refs[8:12], refs[12:16]
    total, total_c = refs[16:]
    core = lax.axis_index("core")
    sum_parts(parts_c, total_c)
    for k in range(4):
        z = lax.rem(position("z") + k, 4)
        outs_c[k][...] = pick_rows(total_c, [layer * 96 + z * 24 for layer in range(2)], 24)
    sum_parts(parts, total)

    @pl.when(core == 0)
    def _():
        for k in range(4):
            x = lax.rem(position("x") + k, 4)
            starts = [(layer * 2 + j) * ROWS + x * 24 for layer in range(2) for j in range(2)]
            outs[k][0:96] = pick_rows(total, starts, 24)
            outs[k][96:128] = total[384:416, :].astype(BF)

    @pl.when(core == 1)
    def _():
        for k in range(4):
            y = lax.rem(position(Y) + k, 4)
            first = lax.rem(y, 2) * 96 + (y // 2) * 24
            starts = [layer * 192 + first + j * 48 for layer in range(2) for j in range(2)]
            outs[k][0:96] = pick_rows(total, starts, 24)
            outs[k][96:128] = jnp.zeros((32, D), BF)


def finish_kernel(place, layers, vectors, iw, ib, ow, ob, fg, fs, ew, eb, cb, sg, ss):
    at = place[0]

    def cut(start):
        lane = lax.broadcasted_iota(jnp.int32, (D, 128), 0)
        to = lax.broadcasted_iota(jnp.int32, (D, 128), 1)
        return lax.dot_general(
            vectors[...],
            jnp.where(lane == to + start, 1.0, 0.0),
            (((1,), (0,)), ((), ())),
            precision=lax.Precision.HIGHEST,
            preferred_element_type=F32,
        )

    for ref, which, chunks in ((iw, 0, (0, 1, 2)), (ow, 0, (3,)), (ew, 1, (0, 1, 2, 3))):
        tiles = len(chunks) * 6
        for i, chunk in enumerate(chunks):
            for t in range(6):
                ref[pl.ds(i * 6 + t, 12, stride=tiles), :] = layers[
                    chunk, which, :, t * 128 : t * 128 + 128
                ]
    rows = cut(at * 12)
    for ref, row in ((ob, 2), (fg, 3), (fs, 4), (cb, 9), (sg, 10), (ss, 11)):
        ref[...] = rows[row : row + 1, :12]
    rows = cut(lax.rem(at, 32) * 24)
    ib[...] = jnp.where(at < 32, rows[0:1], rows[1:2])[:, :24]
    rows = cut(lax.rem(at, 16) * 48)
    which = at // 16
    eb[...] = jnp.where(
        which < 2,
        jnp.where(which == 0, rows[5:6], rows[6:7]),
        jnp.where(which == 2, rows[7:8], rows[8:9]),
    )[:, :48]


def pack_kernel(iw, ib, ow, ob, fg, fs, ew, eb, cw, cb, sg, ss, own, contract, scratch):
    scratch[96:104] = jnp.zeros((8, D), F32)
    for j in range(8):
        ref, first, tiles = (iw, j * 6, 18) if j < 3 else (ow, 0, 6)
        if j > 3:
            ref, first, tiles = ew, (j - 4) * 6, 24
        for t in range(6):
            scratch[j * 12 : (j + 1) * 12, t * 128 : t * 128 + 128] = ref[
                pl.ds(first + t, 12, stride=tiles), :
            ]
    start = 0
    for ref in (ib, ob, fg, fs, eb, cb, sg, ss):
        width = ref.shape[1]
        scratch[96:97, start : start + width] = ref[...]
        start += width
    own[...] = scratch[...].astype(BF)
    contract[...] = cw[0].astype(BF)


def shape(*dims, dtype=F32):
    return jax.ShapeDtypeStruct(dims, dtype)


def call(kernel, outs, args, in_hbm=0, scratch=(), name="kernel", outs_hbm=True, smem=0, limit=60, aliases=None):
    here = len(args) - in_hbm - smem
    in_specs = [pl.BlockSpec(memory_space=pltpu.SMEM)] * smem
    in_specs += [pl.BlockSpec(memory_space=pltpu.VMEM)] * here
    in_specs += [pl.BlockSpec(memory_space=pl.ANY)] * in_hbm
    out_space = pl.ANY if outs_hbm else pltpu.VMEM
    return pl.pallas_call(
        kernel,
        out_shape=outs,
        in_specs=in_specs,
        out_specs=[pl.BlockSpec(memory_space=out_space)] * len(outs),
        scratch_shapes=list(scratch),
        compiler_params=pltpu.CompilerParams(vmem_limit_bytes=limit * 1024 * 1024),
        cost_estimate=pl.CostEstimate(flops=1000, bytes_accessed=1024, transcendentals=0),
        input_output_aliases=aliases or {},
        name=name,
    )(*args)


ROWS_BF = shape(BLOCK, D, dtype=BF)
ROWS_F32 = shape(BLOCK, D)
SCALE = shape(BLOCK, 128)
QKV = shape(3, BLOCK, D, dtype=BF)
PROBS = shape(HEADS, BLOCK, BLOCK, dtype=BF)
SLOPE = shape(4, BLOCK, D, dtype=BF)
TWO = shape(2, BLOCK, D, dtype=BF)
THREE = shape(3, BLOCK, D, dtype=BF)
VECS = shape(16, D)
DA = shape(528, D, dtype=BF)


def vmem(*shapes):
    return [pltpu.VMEM(each.shape, each.dtype) for each in shapes]


HEAD_BF = shape(16, D, dtype=BF)
VRAW = shape(2, 4, 16, D, dtype=BF)


def middle_part(depth, u, seg, cot, pieces, pieces_c):
    saved = [ROWS_F32, SCALE, QKV, PROBS]
    gather_sems = [dma(4, 8), dma(2, 4), dma(4, 8), dma(2, 4, 4), dma(2, 4)]
    return call(
        middle_kernel,
        [ROWS_BF, ROWS_BF, ROWS_BF, ROWS_F32, VECS, *saved, VECS]
        + [shape(HEAD, D, dtype=BF)] * 2
        + [shape(ALL, D, dtype=BF)] * 2,
        [depth, u, seg[:, None], seg[None, :], cot, *pieces, *pieces_c],
        20,
        [*vmem(VRAW, ROWS_BF, *saved, TWO, VECS)]
        + [WA, WC, FOUR, *vmem(SLOPE, ROWS_F32, SCALE, ROWS_BF, ROWS_F32, VECS)]
        + [WA, WA, WC, *vmem(VRAW, ROWS_BF, *saved, TWO, VECS)]
        + [FOUR, *vmem(SLOPE, ROWS_F32, SCALE, ROWS_BF)]
        + [FOUR, *vmem(ROWS_BF, VECS), FOUR, *vmem(HEAD_BF, ROWS_BF)]
        + gather_sems
        + gather_sems
        + [dma(56)],
        name="middle",
        smem=1,
    )


def first_attention_backward(dhidden, vecs, vec, n1, s1, qkv, probs, pieces):
    return call(
        lambda *refs: ba_kernel(0, *refs),
        [ROWS_BF, shape(4 * BLOCK + 16, D, dtype=BF)],
        [dhidden, vecs, vec, n1, s1, qkv, probs, *pieces],
        12,
        [WA, FOUR, *vmem(HEAD_BF, ROWS_BF, QKV, PROBS), dma(4, 8), dma(2), dma(16)],
        name="attention_backward_0",
    )


def layer_weights(layer, args, before=()):
    count = len(before)

    def kernel(*refs):
        weights_kernel(layer, refs[count : count + len(args)], *refs[count + len(args) :])

    def both_cores(parts):
        return pltpu.VMEM((parts, 2 * BLOCK, D), BF)

    return call(
        kernel,
        [shape(1568, D, dtype=BF)] * 4 + [shape(768, D, dtype=BF)] * 4,
        list(before) + args,
        count + len(args),
        [both_cores(2), both_cores(4), both_cores(2), pltpu.VMEM((2 * BLOCK, D), BF)]
        + [pltpu.VMEM((2, 16, D), BF), pltpu.VMEM((2, D, D), F32)]
        + [pltpu.VMEM((4, 784, D), BF), pltpu.VMEM((4, 384, D), BF), dma(20), dma(16)],
        name=f"weights_{layer}",
        aliases={i: i for i in range(count)},
    )


def cut_again(kernel, parts, parts_c, rows, rows_c, name, limit):
    outs = call(
        kernel,
        [shape(rows, D, dtype=BF)] * 4 + [shape(rows_c, D, dtype=BF)] * 4,
        [*parts, *parts_c],
        0,
        [pltpu.VMEM(parts[0].shape, F32), pltpu.VMEM(parts_c[0].shape, F32)],
        name=name,
        outs_hbm=False,
        limit=limit,
    )
    return outs[:4], outs[4:]


def gather(masters):
    core = lax.axis_index("core")
    own, contract = call(
        pack_kernel,
        [shape(104, D, dtype=BF), shape(48, D, dtype=BF)],
        [each.reshape(-1, 128) if i in (0, 2, 6) else each for i, each in enumerate(masters)],
        0,
        [pltpu.VMEM((104, D), F32)],
        name="pack",
        outs_hbm=False,
    )
    own = from_behind(own, "x")
    contract = [contract] + [ahead_by_core(contract, k, "y", "z") for k in (1, 2, 3)]
    contract, own = lax.optimization_barrier((contract, own))
    contract = by_position(contract, jnp.where(core == 0, position(Y), position("z")))
    along_x = by_position(own, position("x"))
    other = swap_core(along_x)
    contract = lax.optimization_barrier((contract, other))[0]
    first, second = jnp.where(core == 0, along_x, other), jnp.where(core == 0, other, along_x)
    both = jnp.stack([first, second])
    chunks = both[:, :, :96].reshape(2, 4, 8, 12, D).transpose(2, 1, 0, 3, 4).reshape(8, ROWS, D)
    vector = both[:, :, 96].transpose(1, 0, 2).reshape(8, D)
    chunks = lax.dynamic_slice_in_dim(chunks, 4 * core, 4, 0).reshape(384, D)
    load = jnp.concatenate([chunks, vector, jnp.zeros((8, D), BF)], axis=0)
    load = jnp.stack([load] + [ahead_by_core(load, k, "y", "z") for k in (1, 2, 3)])
    contract = jnp.stack([contract] + [ahead_by_core(contract, k, "z", "y") for k in (1, 2, 3)])
    load, contract = lax.optimization_barrier((load, contract))
    near = [ahead_by_core(load, k, "z", "y") for k in (1, 3)]
    near_c = [ahead(contract, "x", k) for k in (1, 3)]
    other = [swap_core(load)]
    near, near_c, other = lax.optimization_barrier((near, near_c, other))
    far = [ahead_by_core(near[0][:2], 1, "z", "y"), ahead_by_core(near[1][2:], 3, "z", "y")]
    far_c = [ahead(near_c[0][:2], "x", 1), ahead(near_c[1][2:], "x", 3)]
    swaps = [other[0]]
    for piece in (*near, contract, *near_c):
        piece = lax.optimization_barrier((piece, swaps[-1]))[0]
        swaps.append(swap_core(piece))
    far, far_c, swaps = lax.optimization_barrier((far, far_c, swaps))
    other = swaps[:3] + [swap_core(piece) for piece in far]
    other_c = swaps[3:] + [swap_core(piece) for piece in far_c]
    return [load, *near, *far, *other], [contract, *near_c, *far_c, *other_c]


def summed(pieces):
    total = pieces[0].astype(F32)
    for piece in pieces[1:]:
        total = total + piece.astype(F32)
    return total


def scatter_ahead(pieces, axis):
    return [pieces[0]] + [ahead(pieces[k], axis, k) for k in (1, 2, 3)]


def crossed_ahead(pieces, first, second):
    return [pieces[0]] + [ahead_by_core(pieces[k], k, first, second) for k in (1, 2, 3)]


def reduce_gradients(parts, parts_c):
    section, core = lax.axis_index("section"), lax.axis_index("core")
    near = [ahead_by_core(parts[k], k, "z", "x") for k in (1, 3)]
    near_c = [ahead(parts_c[k], Y, k) for k in (1, 3)]
    parts, parts_c, near, near_c = lax.optimization_barrier((parts, parts_c, near, near_c))
    far, far_c = ahead_by_core(parts[2], 2, "z", "x"), ahead(parts_c[2], Y, 2)
    parts, parts_c = [parts[0], *near, far], [parts_c[0], *near_c, far_c]
    parts, parts_c = cut_again(second_cut_kernel, parts, parts_c, 416, 192, "second_cut", 20)
    parts, parts_c = crossed_ahead(parts, "y", "z"), scatter_ahead(parts_c, "x")
    parts, parts_c = cut_again(third_cut_kernel, parts, parts_c, 128, 48, "third_cut", 20)
    parts, parts_c = crossed_ahead(parts, "x", "y"), scatter_ahead(parts_c, "z")
    total, total_c = summed(parts), summed(parts_c).reshape(2, 24, D)

    def of_layer(value, which):
        return lax.dynamic_index_in_dim(value, which, 0, keepdims=False)

    vectors = of_layer(total[96:].reshape(2, 16, D), section)
    total = total[:96].reshape(2, 2, 24, D)
    mine, others = [
        [of_layer(total, which), of_layer(total_c, which)] for which in (section, 1 - section)
    ]
    near, far = crossed_owner(mine[1], False), crossed_owner(others[1], True)
    contract = jnp.concatenate(
        [jnp.where(section == 0, near, far), jnp.where(section == 0, far, near)]
    )
    mine, others = mine[0].reshape(2, 2, 12, D), others[0].reshape(2, 2, 12, D)

    def rows_of(value, which):
        return lax.dynamic_index_in_dim(value, which, 1, keepdims=False)

    here = rows_of(mine, core)
    near = rows_of(mine, 1 - core).reshape(24, D)
    near = to_neighbour(jnp.concatenate([near, vectors], axis=0), False, True)
    vectors = jnp.where(core == 0, vectors, near[24:])
    near = near[:24].reshape(2, 12, D)
    far = to_neighbour(rows_of(others, core), True, False)
    far_near = to_neighbour(rows_of(others, 1 - core), True, True)
    own, other = jnp.stack([here, far]), jnp.stack([near, far_near])
    attention, expand = jnp.where(core == 0, own, other), jnp.where(core == 0, other, own)
    flip = section == 0
    chunks = [
        jnp.where(flip, each, jnp.flip(each, 0)).reshape(4, 12, D) for each in (attention, expand)
    ]
    return jnp.stack(chunks, axis=1), contract, vectors


def to_neighbour(value, other_section, other_core):
    pairs = []
    for s in range(2):
        for c in range(2):
            to = (1 - s if other_section else s) * 2 + (1 - c if other_core else c)
            pairs.append((s * 2 + c, to))
    return lax.ppermute(value, ("section", "core"), pairs)


def crossed_owner(value, other_section):
    pairs = []
    for s in range(2):
        for yh in range(2):
            for c in range(2):
                to = 1 - s if other_section else s
                pairs.append(((s * 2 + yh) * 2 + c, (to * 2 + c) * 2 + yh))
    return lax.ppermute(value, ("section", "yh", "core"), pairs)


def on_device(tokens, segment_ids, depth, *rest):
    masters = rest[:12]
    cotangent = rest[12]
    section = lax.axis_index("section")
    place = (
        lax.axis_index("yh") * 32
        + lax.axis_index("z") * 8
        + lax.axis_index("x") * 2
        + lax.axis_index("core")
    )
    u = lax.dynamic_slice_in_dim(tokens, section * BLOCK, BLOCK, 0)
    seg = lax.dynamic_slice_in_dim(segment_ids, section * BLOCK, BLOCK, 0)
    cot = lax.dynamic_slice_in_dim(cotangent, section * BLOCK, BLOCK, 0)

    def exchange(middle, last, first, passed):
        mine = jnp.where(section == 0, jnp.stack([middle, first]), jnp.stack([last, passed]))
        theirs = jnp.where(section == 0, jnp.stack([last, passed]), jnp.stack([middle, first]))
        theirs = ahead(theirs, "section", 1)
        low, high = jnp.where(section == 0, mine, theirs), jnp.where(section == 0, theirs, mine)
        both = jnp.concatenate([low, high], axis=1)
        return both[0][None], both[1][None]

    pieces, pieces_c = gather(masters)
    middle, last, passed, dhidden, vecs, *grads = middle_part(depth, u, seg, cot, pieces, pieces_c)
    *saved0, vec0, keep0, send0, keep1, send1 = grads
    first, grads0 = first_attention_backward(dhidden, vecs, vec0, *saved0, pieces)
    got1 = swap_core(send1)
    first, got1 = lax.optimization_barrier((first, got1))
    outputs = exchange(middle, last, first, passed)
    sums = layer_weights(1, [keep1, got1])
    got0, got_a = swap_core(send0), lax.ppermute(grads0, "core", [(1, 0)])
    sums, got0, got_a = lax.optimization_barrier((sums, got0, got_a))
    sums = layer_weights(0, [keep0, got0, grads0, got_a], sums)
    layer_outputs, input_grads, sums = lax.optimization_barrier((*outputs, sums))
    chunks, cw, vec = reduce_gradients(sums[:4], sums[4:])
    one, small = shape(1, 12), [shape(1, 24), shape(1, 48)]
    iw, ib, ow, ob, fg, fs, ew, eb, cb, sg, ss = call(
        finish_kernel,
        [shape(216, 128), small[0], shape(72, 128), one, one, one, shape(288, 128), small[1]]
        + [one, one, one],
        [place[None], chunks, vec],
        smem=1,
        name="finish",
        outs_hbm=False,
    )
    return (
        layer_outputs,
        input_grads,
        iw.reshape(1, 12, 3 * D),
        ib,
        ow.reshape(1, 12, D),
        ob,
        fg,
        fs,
        ew.reshape(1, 12, 4 * D),
        eb,
        cw[None],
        cb,
        sg,
        ss,
    )


def solution(mesh):
    wide = Mesh(mesh.devices.reshape(2, 2, 4, 4, 2), ("section", "yh", "z", "x", "core"))
    dp = ("yh", "z", "x", "core")
    matrix, vector = P("section", dp, None), P("section", dp)
    rows = P(dp, None)
    weights = (
        matrix,
        vector,
        matrix,
        vector,
        vector,
        vector,
        matrix,
        vector,
        matrix,
        vector,
        vector,
        vector,
    )
    return jax.shard_map(
        on_device,
        mesh=wide,
        in_specs=(rows, P(dp), P(dp)) + weights + (rows,),
        out_specs=(matrix, matrix) + weights,
        check_vma=False,
    )
```

```python
import jax
import jax.numpy as jnp
from jax import lax
from jax.experimental import pallas as pl
from jax.experimental.pallas import tpu as pltpu
from jax.sharding import Mesh, PartitionSpec as P

D = 768
HEADS = 12
BLOCK = 256
EPS = 1e-05
Y = ("section", "yh")
ROWS = 96
BF = jnp.bfloat16
F32 = jnp.float32


def position(axis):
    if isinstance(axis, tuple):
        return lax.axis_index("yh") * 2 + lax.axis_index("section")
    return lax.axis_index(axis)


def size_of(axis):
    return 4 if isinstance(axis, tuple) else lax.axis_size(axis)


def ahead(value, axis, steps):
    count = size_of(axis)
    at = [0, 2, 1, 3] if isinstance(axis, tuple) else range(count)
    return lax.ppermute(value, axis, [(at[i], at[(i + steps) % count]) for i in range(count)])


def from_behind(value, axis):
    return [value] + [ahead(value, axis, k) for k in (1, 2, 3)]


def by_position(pieces, here):
    rising = [pieces[0], pieces[3], pieces[2], pieces[1]]
    return lax.dynamic_slice_in_dim(jnp.stack(rising + rising), (4 - here) % 4, 4, 0)


def ahead_by_core(value, steps, first, second):
    pairs = []
    for place in range(128):
        at = {"y": place // 32, "z": place // 8 % 4, "x": place // 2 % 4}
        core = place % 2
        to = dict(at)
        axis = second if core else first
        to[axis] = (to[axis] + steps) % 4
        flat = [
            ((((p["y"] % 2) * 2 + p["y"] // 2) * 4 + p["z"]) * 4 + p["x"]) * 2 + core
            for p in (at, to)
        ]
        pairs.append(tuple(flat))
    return lax.ppermute(value, ("section", "yh", "z", "x", "core"), pairs)


def swap_core(value):
    return ahead(value, "core", 1)


def behind(axis, k):
    return lax.rem(position(axis) + (4 - k), 4)


class Chunks:
    def __init__(self, to, sems):
        self.to, self.sems, self.here = to, sems, set()

    def bring(self, j, source, yh, z):
        block = yh * 4 + z
        rows = pl.ds(pl.multiple_of(block * ROWS, ROWS), ROWS)
        pltpu.make_async_copy(
            source.at[pl.ds(j * ROWS, ROWS), :], self.to.at[j, rows, :], self.sems.at[j, block]
        ).start()

    def wait(self):
        for j in range(4):
            self.get(j)

    def get(self, j):
        for block in range(0 if j in self.here else 8):
            here = self.to.at[j, pl.ds(block * ROWS, ROWS), :]
            pltpu.make_async_copy(here, here, self.sems.at[j, block]).wait()
        self.here.add(j)
        return self.to[j]


def entry(pieces, k, i, high):
    if k == 2:
        return pieces[4 if high else 3].at[i - 2 if high else i]
    return pieces[(0, 1, None, 2)[k]].at[i]


def attention_chunks(layer, pieces, to, sems, order, vraw=None, sem_v=None):
    chunks = Chunks(to, sems)
    core = lax.axis_index("core")
    away = jnp.where(lax.axis_index("section") == layer, 0, 1)
    for r in range(2):

        @pl.when(core == r)
        def _():
            def each(act):
                for k in range(4):
                    for e in range(2):
                        steps = 2 * e + away
                        yh = lax.rem(position(Y) + 4 - steps, 4) // 2
                        act(entry(pieces[5 * r : 5 * r + 5], k, steps, e == 1), yh, behind("z", k))

            if vraw is not None:
                each(
                    lambda piece, yh, z: pltpu.make_async_copy(
                        piece.at[pl.ds(4 * ROWS, 16), :], vraw.at[yh, z], sem_v.at[yh, z]
                    ).start()
                )
            for j in order:
                each(lambda piece, yh, z: chunks.bring(j, piece, yh, z))

    return chunks


def expand_chunks(layer, pieces, to, sems):
    chunks = Chunks(to, sems)
    core = lax.axis_index("core")
    for j in range(4):
        for k in range(4):
            ys = behind(Y, k)
            for r in range(2):

                @pl.when(jnp.logical_and(lax.rem(ys, 2) == layer, core == 1 - r))
                def _():
                    for e in range(4):
                        piece = entry(pieces[5 * r : 5 * r + 5], k, e, e > 1)
                        chunks.bring(j, piece, ys // 2, behind("z", e))

    return chunks


class Contract:
    def __init__(self, layer, pieces, to, sems_0, sems_1):
        self.to, self.sems_0, self.sems_1, self.here = to, sems_0, sems_1, set()
        core = lax.axis_index("core")
        for r in range(2):
            mine = pieces[5 * r : 5 * r + 5]
            for yh in range(2):

                @pl.when(core == r)
                def _():
                    for k in range(4):
                        z = behind("z", k)
                        for i in range(4):
                            x = behind("x", i)
                            pltpu.make_async_copy(
                                entry(mine, i, k, k > 1).at[yh * 2 + layer],
                                to.at[yh, z, x, 0],
                                sems_0.at[yh, z, x],
                            ).start()

            for k in range(4):
                ys = behind(Y, k)

                @pl.when(jnp.logical_and(core == 1 - r, lax.rem(ys, 2) == layer))
                def _():
                    for i in range(4):
                        x = behind("x", i)
                        pltpu.make_async_copy(
                            entry(mine, i, k, k > 1), to.at[ys // 2, :, x, 1], sems_1.at[ys // 2, x]
                        ).start()

    def wait(self):
        for j in range(4):
            self.get(j)

    def get(self, j):
        yh, first = j // 2, (j % 2) * 2
        for x in range(0 if j in self.here else 4):
            for z in (first, first + 1):
                here = self.to.at[yh, z, x, 0]
                pltpu.make_async_copy(here, here, self.sems_0.at[yh, z, x]).wait()
            if first == 0:
                here = self.to.at[yh, :, x, 1]
                pltpu.make_async_copy(here, here, self.sems_1.at[yh, x]).wait()
        self.here.add(j)
        return self.to[yh, first : first + 2].reshape(D, D)


class Out:
    def __init__(self, sems):
        self.sems, self.copies, self.count = sems, [], 0

    def put(self, source, to):
        copy = pltpu.make_async_copy(source, to, self.sems.at[self.count])
        copy.start()
        self.copies.append(copy)
        self.count += 1

    def put_either(self, source, of_first, of_second, first):
        sem, rows = self.sems.at[self.count], pl.ds(first, source.shape[0])
        for core, ref in enumerate((of_first, of_second)):

            @pl.when(lax.axis_index("core") == core)
            def _():
                pltpu.make_async_copy(source, ref.at[rows, :], sem).start()

        self.copies.append(pltpu.make_async_copy(source, of_first.at[rows, :], sem))
        self.count += 1

    def drain(self):
        for copy in self.copies:
            copy.wait()


WA = pltpu.VMEM((4, D, D), BF)
WC = pltpu.VMEM((2, 4, 4, 2, 48, D), BF)
FOUR = pltpu.VMEM((4, BLOCK, D), BF)


def dma(*count):
    return pltpu.SemaphoreType.DMA(count)


def dot(left, right):
    return lax.dot_general(left, right, (((1,), (0,)), ((), ())), preferred_element_type=F32)


def dot_nt(left, right):
    return lax.dot_general(left, right, (((1,), (1,)), ((), ())), preferred_element_type=F32)


def dot_tn(left, right):
    return lax.dot_general(left, right, (((0,), (0,)), ((), ())), preferred_element_type=F32)


def norm_of(residual):
    centre = residual - jnp.mean(residual, axis=1, keepdims=True)
    scaled = lax.rsqrt(jnp.mean(centre * centre, axis=1, keepdims=True) + EPS)
    return centre * scaled, scaled


def norm_back(grad_out, normed, scaled, gain):
    grad_normed = grad_out * gain
    inner = (
        grad_normed
        - jnp.mean(grad_normed, axis=1, keepdims=True)
        - normed * jnp.mean(grad_normed * normed, axis=1, keepdims=True)
    )
    return (
        scaled * inner,
        jnp.sum(grad_out * normed, axis=0, keepdims=True),
        jnp.sum(grad_out, axis=0, keepdims=True),
    )


def head_masks():
    lane = lax.broadcasted_iota(jnp.int32, (BLOCK, 128), 1)
    return lane < 64


def vector_rows(vraw, out):
    groups = [vraw[yh, z][0:8, :256].astype(F32) for yh in range(2) for z in range(4)]
    values = jnp.concatenate(groups, axis=0).astype(BF)
    values = values[:, :144]
    device = lax.broadcasted_iota(jnp.int32, (64, D), 0)
    entry = lax.broadcasted_iota(jnp.int32, (144, D), 0)
    lane = lax.broadcasted_iota(jnp.int32, (1, D), 1)

    def rows(width, row, starts):
        at = lane + row * D
        wide = dot_tn(values, jnp.where(device == at // width, 1.0, 0.0).astype(BF))
        return [
            jnp.sum(jnp.where(entry == at % width + start, wide, 0.0), axis=0, keepdims=True)
            for start in starts
        ]

    twelve = rows(12, 0, (24, 36, 48, 108, 120, 132))
    found = rows(24, 0, (0,)) + rows(24, 1, (0,)) + twelve[:3]
    for row in range(4):
        found += rows(48, row, (60,))
    found += twelve[3:]
    out[...] = jnp.concatenate(found + [jnp.zeros((4, D), F32)], axis=0)


def column_sum(values):
    return jnp.sum(values.astype(F32), axis=0, keepdims=True)


def attention_forward(u, joined, vec, weights, qkv, probs, both, normed, scaled, attended):
    q = ((dot(u, weights.get(0)) + vec[0:1]) * 0.125).astype(BF)
    k = dot(u, weights.get(1)).astype(BF)
    v = (dot(u, weights.get(2)) + vec[1:2]).astype(BF)
    qkv[0] = q
    qkv[1] = k
    qkv[2] = v
    low_half = head_masks()
    for pair in range(HEADS // 2):
        lanes = slice(pair * 128, pair * 128 + 128)
        q2, k2, v2 = q[:, lanes], k[:, lanes], v[:, lanes]
        outs = []
        for h in range(2):
            mine = low_half if h == 0 else jnp.logical_not(low_half)
            scores = dot_nt(jnp.where(mine, q2, jnp.zeros_like(q2)), k2)
            scores = jnp.where(joined, scores, -1e30)
            top = jnp.max(scores, axis=1, keepdims=True)
            exponent = jnp.exp(scores - top)
            total = jnp.sum(exponent, axis=1, keepdims=True)
            rows = (exponent / total).astype(BF)
            probs[2 * pair + h] = rows
            outs.append(dot(rows, v2))
        both[1, :, lanes] = jnp.where(low_half, outs[0], outs[1]).astype(BF)
    attended()
    branch = dot(both[1], weights.get(3)) + vec[2:3]
    n1, s1 = norm_of(u.astype(F32) + branch)
    normed[...] = n1
    scaled[...] = jnp.broadcast_to(s1, (BLOCK, 128))
    return (n1 * vec[3:4] + vec[4:5]).astype(BF)


def ffn_forward(hidden, vec, expand, contract, act, slope, normed, scaled):
    expand.wait()
    contract.wait()
    for j in range(4):
        pre = dot(hidden, expand.get(j)) + vec[5 + j : 6 + j]
        half = 0.5 * (1.0 + lax.erf(pre * 0.7071067811865476))
        act[j] = (pre * half).astype(BF)
        slope[j] = (half + pre * jnp.exp(-0.5 * pre * pre) * 0.3989422804014327).astype(BF)
    total = hidden.astype(F32) + vec[9:10]
    for j in range(4):
        total = total + dot(act[j], contract.get(j))
    n2, s2 = norm_of(total)
    normed[...] = n2
    scaled[...] = jnp.broadcast_to(s2, (BLOCK, 128))
    return n2 * vec[10:11] + vec[11:12]


def ffn_backward(grad, vec, n2, s2, slope, expand, contract, vecs, dffn_ref, dpre_ref):
    dr2, dgain, dshift = norm_back(grad, n2[...], s2[:, 0:1], vec[10:11])
    dffn = dr2.astype(BF)
    dffn_ref[...] = dffn
    vecs[...] = jnp.zeros((16, D), F32)
    vecs[9:10] = column_sum(dffn)
    vecs[10:11] = dgain
    vecs[11:12] = dshift
    for j in range(4):
        dact = dot_nt(dffn, contract.get(j))
        dpre = (dact * slope[j].astype(F32)).astype(BF)
        dpre_ref[j] = dpre
        vecs[5 + j : 6 + j] = column_sum(dpre)
    total = dr2
    for j in range(4):
        total = total + dot_nt(dpre_ref[j], expand.get(j))
    return total


def attention_backward(dhidden, vec, n1, s1, qkv, probs, weights, vecs, parts, head, ready):
    dr1, dgain, dshift = norm_back(dhidden, n1[...], s1[:, 0:1], vec[3:4])
    parts[3] = dr1.astype(BF)
    dattended = dot_nt(parts[3], weights.get(3)).astype(BF)
    ready()
    low_half = head_masks()
    for pair in range(HEADS // 2):
        lanes = slice(pair * 128, pair * 128 + 128)
        q2, k2, v2 = qkv[0, :, lanes], qkv[1, :, lanes], qkv[2, :, lanes]
        do2 = dattended[:, lanes]
        dqs = []
        dk2 = jnp.zeros((BLOCK, 128), F32)
        dv2 = jnp.zeros((BLOCK, 128), F32)
        for h in range(2):
            mine = low_half if h == 0 else jnp.logical_not(low_half)
            do_h = jnp.where(mine, do2, jnp.zeros_like(do2))
            rows_low = probs[2 * pair + h]
            rows = rows_low.astype(F32)
            dprobs = dot_nt(do_h, v2)
            dscores = (
                rows * (dprobs - jnp.sum(rows * dprobs, axis=1, keepdims=True))
            ).astype(BF)
            dqs.append(dot(dscores, k2))
            dk2 = dk2 + dot_tn(dscores, jnp.where(mine, q2, jnp.zeros_like(q2)))
            dv2 = dv2 + dot_tn(rows_low, do_h)
        parts[0, :, lanes] = (jnp.where(low_half, dqs[0], dqs[1]) * 0.125).astype(BF)
        parts[1, :, lanes] = dk2.astype(BF)
        parts[2, :, lanes] = dv2.astype(BF)
    total = dr1
    for j in range(3):
        total = total + dot_nt(parts[j], weights.get(j))
    head[...] = jnp.concatenate(
        [column_sum(parts[0]), column_sum(parts[2]), column_sum(parts[3]), dgain, dshift, vecs[5:16]],
        axis=0,
    ).astype(BF)
    return total


INPUTS, OUTPUTS, ACT, DFFN, HEAD, ALL = 0, 512, 1536, 2048, 2304, 2320


def put_act(out, act, keep, send):
    core = lax.axis_index("core")
    for to, half in ((keep, core), (send, 1 - core)):
        for j in range(2):
            out.put(act.at[2 * half + j], to.at[pl.ds(ACT + j * BLOCK, BLOCK), :])


def put_dffn(out, dffn, keep, send):
    for to in (keep, send):
        out.put(dffn, to.at[pl.ds(DFFN, BLOCK), :])


def put_four(out, first, second, rows, four):
    for j in range(4):
        out.put_either(four.at[j], first, second, rows + j * BLOCK)


def wait_vectors(vraw, sems):
    for yh in range(2):
        for z in range(4):
            here = vraw.at[yh, z]
            pltpu.make_async_copy(here, here, sems.at[yh, z]).wait()


def middle_kernel(keep, seg, tokens, cotangent, *rest):
    pieces, pieces_c = rest[:10], rest[10:20]
    middle_o, last_o, passed_o, dhidden_o, vecs_o = rest[20:25]
    n1_0o, s1_0o, qkv_0o, probs_0o, vec0_o, keep0_o, send0_o, keep_o, send_o = rest[25:34]
    rest = rest[34:]
    u0, cot, sem_i, *rest = rest
    vraw0, hidden0, n1_0, s1_0, qkv_0, probs_0, both0, vec0 = rest[:8]
    we0, wc0, act0, slope0, n2_0, s2_0, dffn0, dhidden0, vecs0 = rest[8:17]
    wa, wb, wc, vraw, hidden, n1, s1, qkv, probs, both, vec = rest[17:28]
    act, slope, n2, s2, last, dpre, dffn, vecs, parts, head, passed = rest[28:39]
    sem_w0, sem_v0, sem_e0, sem_c0, sem_d0, sem_w, sem_v, sem_e, sem_c, sem_d, sem_o = rest[39:]
    out = Out(sem_o)
    rows = pl.ds(pl.multiple_of(lax.axis_index("section") * BLOCK, BLOCK), BLOCK)
    blocks = [
        pltpu.make_async_copy(source.at[rows, :], to, sem_i.at[i])
        for i, (source, to) in enumerate(((tokens, u0), (cotangent, cot)))
    ]
    for copy in blocks:
        copy.start()
    here = jnp.broadcast_to(seg[...].astype(F32), (BLOCK, BLOCK))
    joined = here == here.T
    weights0 = attention_chunks(0, pieces, wb, sem_w0, (0, 1, 2, 3), vraw0, sem_v0)
    expand0 = expand_chunks(0, pieces, we0, sem_e0)
    contract0 = Contract(0, pieces_c, wc0, sem_c0, sem_d0)
    weights = attention_chunks(1, pieces, wa, sem_w, (0, 1, 2, 3), vraw, sem_v)
    wait_all(blocks)
    both0[0] = u0[...]
    wait_vectors(vraw0, sem_v0)
    vector_rows(vraw0, vec0)
    out.put(vec0, vec0_o)

    def attended0():
        out.put(qkv_0, qkv_0o)
        out.put(probs_0, probs_0o)
        out.put_either(both0.at[0], keep0_o, send0_o, INPUTS)
        out.put_either(both0.at[1], keep0_o, send0_o, INPUTS + BLOCK)

    hidden0[...] = attention_forward(
        u0[...], joined, vec0, weights0, qkv_0, probs_0, both0, n1_0, s1_0, attended0
    )
    out.put(n1_0, n1_0o)
    out.put(s1_0, s1_0o)
    expand = expand_chunks(1, pieces, wb, sem_e)
    contract = Contract(1, pieces_c, wc, sem_c, sem_d)
    values = ffn_forward(hidden0[...], vec0, expand0, contract0, act0, slope0, n2_0, s2_0)
    before = len(out.copies)
    put_act(out, act0, keep0_o, send0_o)
    act0_copies, out.copies = out.copies[before:], out.copies[:before]
    for j in range(2):
        out.put_either(hidden0, send0_o, keep0_o, INPUTS + j * BLOCK)
    u = values.astype(BF)
    both[0] = u
    out.put(both.at[0], middle_o)
    wait_vectors(vraw, sem_v)
    vector_rows(vraw, vec)

    def attended():
        out.put_either(both.at[0], keep_o, send_o, INPUTS)
        out.put_either(both.at[1], keep_o, send_o, INPUTS + BLOCK)

    hidden[...] = attention_forward(u, joined, vec, weights, qkv, probs, both, n1, s1, attended)
    for j in range(2):
        out.put_either(hidden, send_o, keep_o, INPUTS + j * BLOCK)
    values = ffn_forward(hidden[...], vec, expand, contract, act, slope, n2, s2)
    put_act(out, act, keep_o, send_o)
    kept = keep[0] > 9
    last[...] = jnp.where(kept, values.astype(BF), both[0])
    out.put(last, last_o)
    grad = jnp.where(kept, cot[...].astype(F32), 0.0)
    grad = ffn_backward(grad, vec, n2, s2, slope, expand, contract, vecs, dffn, dpre)
    put_four(out, send_o, keep_o, OUTPUTS, dpre)
    put_dffn(out, dffn, keep_o, send_o)
    du = attention_backward(
        grad, vec, n1, s1, qkv, probs, weights, vecs, parts, head, lambda: None
    )
    put_four(out, keep_o, send_o, OUTPUTS, parts)
    out.put_either(head, keep_o, send_o, HEAD)
    passed[...] = jnp.where(kept, du.astype(BF), cot[...])
    out.put(passed, passed_o)
    wait_all(act0_copies)
    dhidden0[...] = ffn_backward(
        passed[...].astype(F32), vec0, n2_0, s2_0, slope0, expand0, contract0, vecs0, dffn0, act0
    )
    put_four(out, send0_o, keep0_o, OUTPUTS, act0)
    put_dffn(out, dffn0, keep0_o, send0_o)
    out.put(dhidden0, dhidden_o)
    out.put(vecs0, vecs_o)
    out.drain()


def ba_kernel(layer, dhidden, vecs, vec, n1, s1, qkv_i, probs_i, *rest):
    pieces = rest[:10]
    du_o, grads_o = rest[10:12]
    wa, parts, head, du, qkv, probs, sem_w, sem_i, sem_o = rest[12:]
    out = Out(sem_o)
    saved = [
        pltpu.make_async_copy(qkv_i, qkv, sem_i.at[0]),
        pltpu.make_async_copy(probs_i, probs, sem_i.at[1]),
    ]
    for copy in saved:
        copy.start()
    weights = attention_chunks(layer, pieces, wa, sem_w, (3, 0, 1, 2))
    du[...] = attention_backward(
        dhidden[...], vec, n1, s1, qkv, probs, weights, vecs, parts, head, lambda: wait_all(saved)
    ).astype(BF)
    for j in range(4):
        out.put(parts.at[j], grads_o.at[pl.ds(j * BLOCK, BLOCK), :])
    out.put(head, grads_o.at[pl.ds(4 * BLOCK, 16), :])
    out.put(du, du_o)
    out.drain()


def wait_all(copies):
    for copy in copies:
        copy.wait()


def slab_rows(scratch, which, blocks):
    rows = [scratch[pl.ds(pl.multiple_of(b * ROWS + which * 24, 8), 24), :] for b in blocks]
    return jnp.concatenate(rows, axis=0).astype(BF)


def wait_all(copies):
    for copy in copies:
        copy.wait()


def slab_rows(scratch, which, blocks):
    rows = [scratch[pl.ds(pl.multiple_of(b * ROWS + which * 24, 8), 24), :] for b in blocks]
    return jnp.concatenate(rows, axis=0).astype(BF)


def bring_both(keep, send, first, to, sems, count):
    return [
        pltpu.make_async_copy(
            ref.at[pl.ds(first, BLOCK), :], to.at[pl.ds(r * BLOCK, BLOCK), :], sems.at[count + r]
        )
        for r, ref in enumerate((keep, send))
    ]


def weights_kernel(layer, ins, *rest):
    x, d, act, dffn, head, grad, staged, staged_c, sem_i, sem_o = rest[8:]

    def of_layer(refs, far, rows):
        refs = [ref.at[pl.ds(layer * rows, rows), :] for ref in refs]
        return [refs[0], refs[1], far, refs[2]]

    outs, outs_c = of_layer(rest[:3], rest[6], 784), of_layer(rest[3:6], rest[7], 384)
    core = lax.axis_index("core")
    keep, got = ins[:2]

    def bring(first, to, count):
        return [
            pltpu.make_async_copy(
                ref.at[pl.ds(first, BLOCK), :], to.at[pl.ds(r * BLOCK, BLOCK), :], sem_i.at[count + r]
            )
            for r, ref in enumerate((keep, got))
        ]

    dffn_in = bring(DFFN, dffn, 0)
    act_in = [bring(ACT + j * BLOCK, act.at[j], 2 + 2 * j) for j in range(2)]
    x_in = [bring(INPUTS + j * BLOCK, x.at[j], 6 + 2 * j) for j in range(2)]
    d_in = [bring(OUTPUTS + j * BLOCK, d.at[j], 10 + 2 * j) for j in range(4)]
    for pair in (dffn_in, *act_in, *x_in):
        for copy in pair:
            copy.start()
    if len(ins) == 2:
        for pair in d_in:
            for copy in pair:
                copy.start()
        heads = [ref.at[pl.ds(HEAD, 16), :] for ref in ins]
    else:
        heads = [ref.at[pl.ds(4 * BLOCK, 16), :] for ref in ins[2:]]

        @pl.when(core == 1)
        def _():
            for pair in d_in:
                for copy in pair:
                    copy.start()

        @pl.when(core == 0)
        def _():
            for j in range(4):
                for r, ref in enumerate(ins[2:]):
                    pltpu.make_async_copy(
                        ref.at[pl.ds(j * BLOCK, BLOCK), :],
                        d.at[j, pl.ds(r * BLOCK, BLOCK), :],
                        sem_i.at[10 + 2 * j + r],
                    ).start()

    head_in = [
        pltpu.make_async_copy(ref, head.at[r], sem_i.at[18 + r]) for r, ref in enumerate(heads)
    ]
    for copy in head_in:
        copy.start()
    out = Out(sem_o)
    wait_all(dffn_in)
    for a in range(2):
        wait_all(act_in[a])
        grad[a] = dot_tn(act[a], dffn[...])
        for k in range(4):
            staged_c[k, a * 192 : (a + 1) * 192] = slab_rows(
                grad.at[a], lax.rem(position(Y) + k, 4), range(8)
            )
    for k in range(4):
        out.put(staged_c.at[k], outs_c[k])
    wait_all(head_in)
    vec = (head[0].astype(F32) + head[1].astype(F32)).astype(BF)
    wait_all(x_in[0] + x_in[1])
    for j in range(4):
        wait_all(d_in[j])
        here, of_j = slice(j * 192, (j + 1) * 192), grad.at[j % 2]
        of_j[...] = dot_tn(x[j // 3], d[j])

        @pl.when(core == 0)
        def _():
            for k in range(4):
                z = lax.rem(position("z") + k, 4)
                rows = [
                    of_j[pl.ds(pl.multiple_of((yh * 4 + z) * ROWS, 8), ROWS), :] for yh in range(2)
                ]
                staged[k, here] = jnp.concatenate(rows, axis=0).astype(BF)

        @pl.when(core == 1)
        def _():
            for k in range(4):
                staged[k, here] = slab_rows(of_j, lax.rem(position("x") + k, 4), range(8))

        if j % 2:
            for k in range(4):
                rows = pl.ds((j - 1) * 192, 384)
                out.put(staged.at[k, rows, :], outs[k].at[rows, :])
    for k in range(4):
        staged[k, 768:784] = vec
        rows = pl.ds(768, 16)
        out.put(staged.at[k, rows, :], outs[k].at[rows, :])
    out.drain()


def sum_parts(parts, to):
    rows = to.shape[0]
    step = 16 * max(n for n in range(1, 13) if rows % (16 * n) == 0)

    @pl.loop(0, rows // step)
    def _(i):
        here = pl.ds(pl.multiple_of(i * step, 16), step)
        total = parts[0][here, :].astype(F32)
        for part in parts[1:]:
            total = total + part[here, :].astype(F32)
        to[here, :] = total


def pick_rows(total, starts, count):
    rows = [total[pl.ds(pl.multiple_of(start, 8), count), :] for start in starts]
    return jnp.concatenate(rows, axis=0).astype(BF)


def pass_on_kernel(*refs):
    got, sums, semaphores = refs[4:8], refs[8:12], refs[16]
    rows = [pl.ds(0 if i % 2 == 0 else got[i].shape[0], got[i].shape[0]) for i in range(4)]
    held = refs[12:16]
    copies = [
        pltpu.make_async_copy(sums[i].at[rows[i], :], held[i], semaphores.at[i]) for i in range(4)
    ]
    for copy in copies:
        copy.start()
    out = Out(semaphores)
    out.count = 4
    for i in range(4):
        copies[i].wait()
        held[i][...] = (held[i][...].astype(F32) + got[i][...].astype(F32)).astype(BF)
        out.put(held[i], sums[i].at[rows[i], :])
    out.drain()


def second_cut_kernel(*refs):
    parts, parts_c = refs[:3], refs[3:6]
    outs, outs_c = refs[6:10], refs[10:14]
    total, total_c = refs[14:]
    core = lax.axis_index("core")
    sum_parts(parts_c, total_c)
    for k in range(4):
        x = lax.rem(position("x") + k, 4)
        starts = [layer * 384 + (z * 4 + x) * 24 for layer in range(2) for z in range(4)]
        outs_c[k][...] = pick_rows(total_c, starts, 24)
    sum_parts(parts, total)

    @pl.when(core == 0)
    def _():
        for k in range(4):
            y = lax.rem(position(Y) + k, 4)
            first = lax.rem(y, 2) * 384 + (y // 2) * ROWS
            starts = [layer * 784 + first + j * 192 for layer in range(2) for j in range(2)]
            outs[k][0:384] = pick_rows(total, starts, ROWS)
            outs[k][384:416] = pick_rows(total, (768, 784 + 768), 16)

    @pl.when(core == 1)
    def _():
        for k in range(4):
            z = lax.rem(position("z") + k, 4)
            starts = [
                layer * 784 + j * 192 + (yh * 4 + z) * 24
                for layer in range(2)
                for j in range(4)
                for yh in range(2)
            ]
            outs[k][0:384] = pick_rows(total, starts, 24)
            outs[k][384:416] = jnp.zeros((32, D), BF)


def third_cut_kernel(*refs):
    parts, parts_c = refs[:4], refs[4:8]
    outs, outs_c = refs[8:12], refs[12:16]
    total, total_c = refs[16:]
    core = lax.axis_index("core")
    sum_parts(parts_c, total_c)
    for k in range(4):
        z = lax.rem(position("z") + k, 4)
        outs_c[k][...] = pick_rows(total_c, [layer * 96 + z * 24 for layer in range(2)], 24)
    sum_parts(parts, total)

    @pl.when(core == 0)
    def _():
        for k in range(4):
            x = lax.rem(position("x") + k, 4)
            starts = [(layer * 2 + j) * ROWS + x * 24 for layer in range(2) for j in range(2)]
            outs[k][0:96] = pick_rows(total, starts, 24)
            outs[k][96:128] = total[384:416, :].astype(BF)

    @pl.when(core == 1)
    def _():
        for k in range(4):
            y = lax.rem(position(Y) + k, 4)
            first = lax.rem(y, 2) * 96 + (y // 2) * 24
            starts = [layer * 192 + first + j * 48 for layer in range(2) for j in range(2)]
            outs[k][0:96] = pick_rows(total, starts, 24)
            outs[k][96:128] = jnp.zeros((32, D), BF)


def finish_kernel(place, layers, vectors, iw, ib, ow, ob, fg, fs, ew, eb, cb, sg, ss):
    at = place[0]

    def cut(start):
        lane = lax.broadcasted_iota(jnp.int32, (D, 128), 0)
        to = lax.broadcasted_iota(jnp.int32, (D, 128), 1)
        return lax.dot_general(
            vectors[...],
            jnp.where(lane == to + start, 1.0, 0.0),
            (((1,), (0,)), ((), ())),
            precision=lax.Precision.HIGHEST,
            preferred_element_type=F32,
        )

    for ref, which, chunks in ((iw, 0, (0, 1, 2)), (ow, 0, (3,)), (ew, 1, (0, 1, 2, 3))):
        tiles = len(chunks) * 6
        for i, chunk in enumerate(chunks):
            for t in range(6):
                ref[pl.ds(i * 6 + t, 12, stride=tiles), :] = layers[
                    chunk, which, :, t * 128 : t * 128 + 128
                ]
    rows = cut(at * 12)
    for ref, row in ((ob, 2), (fg, 3), (fs, 4), (cb, 9), (sg, 10), (ss, 11)):
        ref[...] = rows[row : row + 1, :12]
    rows = cut(lax.rem(at, 32) * 24)
    ib[...] = jnp.where(at < 32, rows[0:1], rows[1:2])[:, :24]
    rows = cut(lax.rem(at, 16) * 48)
    which = at // 16
    eb[...] = jnp.where(
        which < 2,
        jnp.where(which == 0, rows[5:6], rows[6:7]),
        jnp.where(which == 2, rows[7:8], rows[8:9]),
    )[:, :48]


def pack_kernel(iw, ib, ow, ob, fg, fs, ew, eb, cw, cb, sg, ss, own, contract, scratch):
    scratch[96:104] = jnp.zeros((8, D), F32)
    for j in range(8):
        ref, first, tiles = (iw, j * 6, 18) if j < 3 else (ow, 0, 6)
        if j > 3:
            ref, first, tiles = ew, (j - 4) * 6, 24
        for t in range(6):
            scratch[j * 12 : (j + 1) * 12, t * 128 : t * 128 + 128] = ref[
                pl.ds(first + t, 12, stride=tiles), :
            ]
    start = 0
    for ref in (ib, ob, fg, fs, eb, cb, sg, ss):
        width = ref.shape[1]
        scratch[96:97, start : start + width] = ref[...]
        start += width
    own[...] = scratch[...].astype(BF)
    contract[...] = cw[0].astype(BF)


def shape(*dims, dtype=F32):
    return jax.ShapeDtypeStruct(dims, dtype)


def call(kernel, outs, args, in_hbm=0, scratch=(), name="kernel", outs_hbm=True, smem=0, limit=60, aliases=None):
    here = len(args) - in_hbm - smem
    in_specs = [pl.BlockSpec(memory_space=pltpu.SMEM)] * smem
    in_specs += [pl.BlockSpec(memory_space=pltpu.VMEM)] * here
    in_specs += [pl.BlockSpec(memory_space=pl.ANY)] * in_hbm
    out_space = pl.ANY if outs_hbm else pltpu.VMEM
    return pl.pallas_call(
        kernel,
        out_shape=outs,
        in_specs=in_specs,
        out_specs=[pl.BlockSpec(memory_space=out_space)] * len(outs),
        scratch_shapes=list(scratch),
        compiler_params=pltpu.CompilerParams(vmem_limit_bytes=limit * 1024 * 1024),
        cost_estimate=pl.CostEstimate(flops=1000, bytes_accessed=1024, transcendentals=0),
        input_output_aliases=aliases or {},
        name=name,
    )(*args)


ROWS_BF = shape(BLOCK, D, dtype=BF)
ROWS_F32 = shape(BLOCK, D)
SCALE = shape(BLOCK, 128)
QKV = shape(3, BLOCK, D, dtype=BF)
PROBS = shape(HEADS, BLOCK, BLOCK, dtype=BF)
SLOPE = shape(4, BLOCK, D, dtype=BF)
TWO = shape(2, BLOCK, D, dtype=BF)
THREE = shape(3, BLOCK, D, dtype=BF)
VECS = shape(16, D)
DA = shape(528, D, dtype=BF)


def vmem(*shapes):
    return [pltpu.VMEM(each.shape, each.dtype) for each in shapes]


HEAD_BF = shape(16, D, dtype=BF)
VRAW = shape(2, 4, 16, D, dtype=BF)


def middle_part(depth, tokens, seg, cotangent, pieces, pieces_c):
    saved = [ROWS_F32, SCALE, QKV, PROBS]
    gather_sems = [dma(4, 8), dma(2, 4), dma(4, 8), dma(2, 4, 4), dma(2, 4)]
    return call(
        middle_kernel,
        [ROWS_BF, ROWS_BF, ROWS_BF, ROWS_F32, VECS, *saved, VECS]
        + [shape(HEAD, D, dtype=BF)] * 2
        + [shape(ALL, D, dtype=BF)] * 2,
        [depth, seg[None, :], tokens, cotangent, *pieces, *pieces_c],
        22,
        [*vmem(ROWS_BF, ROWS_BF), dma(2), *vmem(VRAW, ROWS_BF, *saved, TWO, VECS)]
        + [WA, WC, FOUR, *vmem(SLOPE, ROWS_F32, SCALE, ROWS_BF, ROWS_F32, VECS)]
        + [WA, WA, WC, *vmem(VRAW, ROWS_BF, *saved, TWO, VECS)]
        + [FOUR, *vmem(SLOPE, ROWS_F32, SCALE, ROWS_BF)]
        + [FOUR, *vmem(ROWS_BF, VECS), FOUR, *vmem(HEAD_BF, ROWS_BF)]
        + gather_sems
        + gather_sems
        + [dma(56)],
        name="middle",
        smem=1,
    )


def first_attention_backward(dhidden, vecs, vec, n1, s1, qkv, probs, pieces):
    return call(
        lambda *refs: ba_kernel(0, *refs),
        [ROWS_BF, shape(4 * BLOCK + 16, D, dtype=BF)],
        [dhidden, vecs, vec, n1, s1, qkv, probs, *pieces],
        12,
        [WA, FOUR, *vmem(HEAD_BF, ROWS_BF, QKV, PROBS), dma(4, 8), dma(2), dma(16)],
        name="attention_backward_0",
    )


def layer_weights(layer, args, before=()):
    count = len(before)

    def kernel(*refs):
        weights_kernel(layer, refs[count : count + len(args)], *refs[count + len(args) :])

    def both_cores(parts):
        return pltpu.VMEM((parts, 2 * BLOCK, D), BF)

    return call(
        kernel,
        [shape(1568, D, dtype=BF)] * 3
        + [shape(768, D, dtype=BF)] * 3
        + [shape(784, D, dtype=BF), shape(384, D, dtype=BF)],
        list(before) + args,
        count + len(args),
        [both_cores(2), both_cores(4), both_cores(2), pltpu.VMEM((2 * BLOCK, D), BF)]
        + [pltpu.VMEM((2, 16, D), BF), pltpu.VMEM((2, D, D), F32)]
        + [pltpu.VMEM((4, 784, D), BF), pltpu.VMEM((4, 384, D), BF), dma(20), dma(16)],
        name=f"weights_{layer}",
        aliases={i: i for i in range(count)},
    )


def pass_on(sums, got):
    kept = [pltpu.VMEM(each.shape, BF) for each in got]
    return call(
        lambda *refs: pass_on_kernel(*refs[4:8], *refs[:4], *refs[8:]),
        [shape(*each.shape, dtype=BF) for each in sums],
        [*got, *sums],
        4,
        kept + [dma(8)],
        name="pass_on",
        aliases={4 + i: i for i in range(4)},
    )


def cut_again(kernel, parts, parts_c, rows, rows_c, name, limit):
    outs = call(
        kernel,
        [shape(rows, D, dtype=BF)] * 4 + [shape(rows_c, D, dtype=BF)] * 4,
        [*parts, *parts_c],
        0,
        [pltpu.VMEM(parts[0].shape, F32), pltpu.VMEM(parts_c[0].shape, F32)],
        name=name,
        outs_hbm=False,
        limit=limit,
    )
    return outs[:4], outs[4:]


def gather(masters):
    core = lax.axis_index("core")
    own, contract = call(
        pack_kernel,
        [shape(104, D, dtype=BF), shape(48, D, dtype=BF)],
        [each.reshape(-1, 128) if i in (0, 2, 6) else each for i, each in enumerate(masters)],
        0,
        [pltpu.VMEM((104, D), F32)],
        name="pack",
        outs_hbm=False,
    )
    own = from_behind(own, "x")
    contract, own = lax.optimization_barrier((contract, own))
    contract = [contract] + [ahead_by_core(contract, k, "y", "z") for k in (1, 2, 3)]
    contract = by_position(contract, jnp.where(core == 0, position(Y), position("z")))
    contract = [contract] + [ahead_by_core(contract, k, "z", "y") for k in (1, 2, 3)]
    along_x = by_position(own, position("x"))
    other = swap_core(along_x)
    first, second = jnp.where(core == 0, along_x, other), jnp.where(core == 0, other, along_x)
    both = jnp.stack([first, second])
    chunks = both[:, :, :96].reshape(2, 4, 8, 12, D).transpose(2, 1, 0, 3, 4).reshape(8, ROWS, D)
    vector = both[:, :, 96].transpose(1, 0, 2).reshape(8, D)
    chunks = lax.dynamic_slice_in_dim(chunks, 4 * core, 4, 0).reshape(384, D)
    load = jnp.concatenate([chunks, vector, jnp.zeros((8, D), BF)], axis=0)
    load = jnp.stack([load] + [ahead_by_core(load, k, "y", "z") for k in (1, 2, 3)])
    contract = jnp.stack(contract)
    load, contract = lax.optimization_barrier((load, contract))
    near = [ahead_by_core(load, k, "z", "y") for k in (1, 3)]
    near_c = [ahead(contract, "x", k) for k in (1, 3)]
    other = swap_core(load)
    other_c = swap_core(lax.optimization_barrier((contract, other))[0])
    near, near_c, other, other_c = lax.optimization_barrier((near, near_c, other, other_c))
    far = [ahead_by_core(near[0][:2], 1, "z", "y"), ahead_by_core(near[1][2:], 3, "z", "y")]
    far_c = [ahead(near_c[0][:2], "x", 1), ahead(near_c[1][2:], "x", 3)]
    early = swap_core(near[0])
    far, far_c, early, near, near_c = lax.optimization_barrier((far, far_c, early, near, near_c))
    other = [other, early] + [swap_core(piece) for piece in (near[1], *far)]
    other_c = [other_c] + [swap_core(piece) for piece in (*near_c, *far_c)]
    return [load, *near, *far, *other], [contract, *near_c, *far_c, *other_c]


def summed(pieces):
    total = pieces[0].astype(F32)
    for piece in pieces[1:]:
        total = total + piece.astype(F32)
    return total


def scatter_ahead(pieces, axis):
    return [pieces[0]] + [ahead(pieces[k], axis, k) for k in (1, 2, 3)]


def crossed_ahead(pieces, first, second):
    return [pieces[0]] + [ahead_by_core(pieces[k], k, first, second) for k in (1, 2, 3)]


def reduce_gradients(parts, parts_c, far, far_c):
    section, core = lax.axis_index("section"), lax.axis_index("core")
    got = [ahead_by_core(far[0], 1, "z", "x"), ahead_by_core(far[1], 3, "z", "x")]
    got += [ahead(far_c[0], Y, 1), ahead(far_c[1], Y, 3)]
    sums = pass_on([*parts[1:], *parts_c[1:]], got)
    near = [ahead_by_core(sums[0], 1, "z", "x"), ahead_by_core(sums[1], 3, "z", "x")]
    near_c = [ahead(sums[2], Y, 1), ahead(sums[3], Y, 3)]
    parts, parts_c = [parts[0], *near], [parts_c[0], *near_c]
    parts, parts_c = cut_again(second_cut_kernel, parts, parts_c, 416, 192, "second_cut", 20)
    parts, parts_c = crossed_ahead(parts, "y", "z"), scatter_ahead(parts_c, "x")
    parts, parts_c = cut_again(third_cut_kernel, parts, parts_c, 128, 48, "third_cut", 20)
    parts, parts_c = crossed_ahead(parts, "x", "y"), scatter_ahead(parts_c, "z")
    parts, parts_c = lax.optimization_barrier((parts, parts_c))
    total, total_c = summed(parts), summed(parts_c).reshape(2, 24, D)

    def of_layer(value, which):
        return lax.dynamic_index_in_dim(value, which, 0, keepdims=False)

    vectors = of_layer(total[96:].reshape(2, 16, D), section)
    total = total[:96].reshape(2, 2, 24, D)
    mine, others = [
        [of_layer(total, which), of_layer(total_c, which)] for which in (section, 1 - section)
    ]
    near, far = crossed_owner(mine[1], False), crossed_owner(others[1], True)
    contract = jnp.concatenate(
        [jnp.where(section == 0, near, far), jnp.where(section == 0, far, near)]
    )
    mine, others = mine[0].reshape(2, 2, 12, D), others[0].reshape(2, 2, 12, D)

    def rows_of(value, which):
        return lax.dynamic_index_in_dim(value, which, 1, keepdims=False)

    here = rows_of(mine, core)
    near = rows_of(mine, 1 - core).reshape(24, D)
    near = to_neighbour(jnp.concatenate([near, vectors], axis=0), False, True)
    vectors = jnp.where(core == 0, vectors, near[24:])
    near = near[:24].reshape(2, 12, D)
    far = to_neighbour(rows_of(others, core), True, False)
    far_near = to_neighbour(rows_of(others, 1 - core), True, True)
    own, other = jnp.stack([here, far]), jnp.stack([near, far_near])
    attention, expand = jnp.where(core == 0, own, other), jnp.where(core == 0, other, own)
    flip = section == 0
    chunks = [
        jnp.where(flip, each, jnp.flip(each, 0)).reshape(4, 12, D) for each in (attention, expand)
    ]
    return jnp.stack(chunks, axis=1), contract, vectors


def to_neighbour(value, other_section, other_core):
    pairs = []
    for s in range(2):
        for c in range(2):
            to = (1 - s if other_section else s) * 2 + (1 - c if other_core else c)
            pairs.append((s * 2 + c, to))
    return lax.ppermute(value, ("section", "core"), pairs)


def crossed_owner(value, other_section):
    pairs = []
    for s in range(2):
        for yh in range(2):
            for c in range(2):
                to = 1 - s if other_section else s
                pairs.append(((s * 2 + yh) * 2 + c, (to * 2 + c) * 2 + yh))
    return lax.ppermute(value, ("section", "yh", "core"), pairs)


def on_device(tokens, segment_ids, depth, *rest):
    masters = rest[:12]
    cotangent = rest[12]
    section = lax.axis_index("section")
    place = (
        lax.axis_index("yh") * 32
        + lax.axis_index("z") * 8
        + lax.axis_index("x") * 2
        + lax.axis_index("core")
    )
    seg = lax.dynamic_slice_in_dim(segment_ids, section * BLOCK, BLOCK, 0)

    def chosen(middle, last, first, passed):
        return jnp.where(section == 0, jnp.stack([middle, first]), jnp.stack([last, passed]))

    pieces, pieces_c = gather(masters)
    middle, last, passed, dhidden, vecs, *grads = middle_part(depth, tokens, seg, cotangent, pieces, pieces_c)
    *saved0, vec0, keep0, send0, keep1, send1 = grads
    first, grads0 = first_attention_backward(dhidden, vecs, vec0, *saved0, pieces)
    got1 = swap_core(send1)
    first, got1 = lax.optimization_barrier((first, got1))
    theirs = ahead(chosen(last, middle, passed, first), "section", 1)
    *sums, far1, far1_c = layer_weights(1, [keep1, got1])
    far1 = (far1, far1_c)
    got0, got_a = swap_core(send0), lax.ppermute(grads0, "core", [(1, 0)])
    sums, got0, got_a = lax.optimization_barrier((sums, got0, got_a))
    sums = layer_weights(0, [keep0, got0, grads0, got_a], sums)
    theirs, sums = lax.optimization_barrier((theirs, sums))
    chunks, cw, vec = reduce_gradients(
        sums[:3], sums[3:6], (sums[6], far1[0]), (sums[7], far1[1])
    )
    mine = chosen(middle, last, first, passed)
    low, high = jnp.where(section == 0, mine, theirs), jnp.where(section == 0, theirs, mine)
    layer_outputs, input_grads = jnp.concatenate([low, high], axis=1)[:, None]
    one, small = shape(1, 12), [shape(1, 24), shape(1, 48)]
    iw, ib, ow, ob, fg, fs, ew, eb, cb, sg, ss = call(
        finish_kernel,
        [shape(216, 128), small[0], shape(72, 128), one, one, one, shape(288, 128), small[1]]
        + [one, one, one],
        [place[None], chunks, vec],
        smem=1,
        name="finish",
        outs_hbm=False,
    )
    return (
        layer_outputs,
        input_grads,
        iw.reshape(1, 12, 3 * D),
        ib,
        ow.reshape(1, 12, D),
        ob,
        fg,
        fs,
        ew.reshape(1, 12, 4 * D),
        eb,
        cw[None],
        cb,
        sg,
        ss,
    )


def solution(mesh):
    wide = Mesh(mesh.devices.reshape(2, 2, 4, 4, 2), ("section", "yh", "z", "x", "core"))
    dp = ("yh", "z", "x", "core")
    matrix, vector = P("section", dp, None), P("section", dp)
    rows = P(dp, None)
    weights = (
        matrix,
        vector,
        matrix,
        vector,
        vector,
        vector,
        matrix,
        vector,
        matrix,
        vector,
        vector,
        vector,
    )
    return jax.shard_map(
        on_device,
        mesh=wide,
        in_specs=(rows, P(dp), P(dp)) + weights + (rows,),
        out_specs=(matrix, matrix) + weights,
        check_vma=False,
    )
```

```python
import jax
import jax.numpy as jnp
from jax import lax
from jax.experimental import pallas as pl
from jax.experimental.pallas import tpu as pltpu
from jax.sharding import Mesh, PartitionSpec as P

D = 768
HEADS = 12
BLOCK = 256
EPS = 1e-05
Y = ("section", "yh")
ROWS = 96
BF = jnp.bfloat16
F32 = jnp.float32


def position(axis):
    if isinstance(axis, tuple):
        return lax.axis_index("yh") * 2 + lax.axis_index("section")
    return lax.axis_index(axis)


def size_of(axis):
    return 4 if isinstance(axis, tuple) else lax.axis_size(axis)


def ahead(value, axis, steps):
    count = size_of(axis)
    at = [0, 2, 1, 3] if isinstance(axis, tuple) else range(count)
    return lax.ppermute(value, axis, [(at[i], at[(i + steps) % count]) for i in range(count)])


def from_behind(value, axis):
    return [value] + [ahead(value, axis, k) for k in (1, 2, 3)]


def by_position(pieces, here):
    rising = [pieces[0], pieces[3], pieces[2], pieces[1]]
    return lax.dynamic_slice_in_dim(jnp.stack(rising + rising), (4 - here) % 4, 4, 0)


def ahead_by_core(value, steps, first, second):
    pairs = []
    for place in range(128):
        at = {"y": place // 32, "z": place // 8 % 4, "x": place // 2 % 4}
        core = place % 2
        to = dict(at)
        axis = second if core else first
        to[axis] = (to[axis] + steps) % 4
        flat = [
            ((((p["y"] % 2) * 2 + p["y"] // 2) * 4 + p["z"]) * 4 + p["x"]) * 2 + core
            for p in (at, to)
        ]
        pairs.append(tuple(flat))
    return lax.ppermute(value, ("section", "yh", "z", "x", "core"), pairs)


def swap_core(value):
    return ahead(value, "core", 1)


def behind(axis, k):
    return lax.rem(position(axis) + (4 - k), 4)


class Chunks:
    def __init__(self, to, sems):
        self.to, self.sems, self.here = to, sems, set()

    def bring(self, j, source, yh, z):
        block = yh * 4 + z
        rows = pl.ds(pl.multiple_of(block * ROWS, ROWS), ROWS)
        pltpu.make_async_copy(
            source.at[pl.ds(j * ROWS, ROWS), :], self.to.at[j, rows, :], self.sems.at[j, block]
        ).start()

    def wait(self):
        for j in range(4):
            self.get(j)

    def get(self, j):
        for block in range(0 if j in self.here else 8):
            here = self.to.at[j, pl.ds(block * ROWS, ROWS), :]
            pltpu.make_async_copy(here, here, self.sems.at[j, block]).wait()
        self.here.add(j)
        return self.to[j]


def entry(pieces, k, i, high):
    if k == 2:
        return pieces[4 if high else 3].at[i - 2 if high else i]
    return pieces[(0, 1, None, 2)[k]].at[i]


def attention_chunks(layer, pieces, to, sems, order, vraw=None, sem_v=None):
    chunks = Chunks(to, sems)
    core = lax.axis_index("core")
    away = jnp.where(lax.axis_index("section") == layer, 0, 1)
    for r in range(2):

        @pl.when(core == r)
        def _():
            def each(act):
                for k in range(4):
                    for e in range(2):
                        steps = 2 * e + away
                        yh = lax.rem(position(Y) + 4 - steps, 4) // 2
                        act(entry(pieces[5 * r : 5 * r + 5], k, steps, e == 1), yh, behind("z", k))

            if vraw is not None:
                each(
                    lambda piece, yh, z: pltpu.make_async_copy(
                        piece.at[pl.ds(4 * ROWS, 16), :], vraw.at[yh, z], sem_v.at[yh, z]
                    ).start()
                )
            for j in order:
                each(lambda piece, yh, z: chunks.bring(j, piece, yh, z))

    return chunks


def expand_chunks(layer, pieces, to, sems):
    chunks = Chunks(to, sems)
    core = lax.axis_index("core")
    for j in range(4):
        for k in range(4):
            ys = behind(Y, k)
            for r in range(2):

                @pl.when(jnp.logical_and(lax.rem(ys, 2) == layer, core == 1 - r))
                def _():
                    for e in range(4):
                        piece = entry(pieces[5 * r : 5 * r + 5], k, e, e > 1)
                        chunks.bring(j, piece, ys // 2, behind("z", e))

    return chunks


class Contract:
    def __init__(self, layer, pieces, to, sems_0, sems_1):
        self.to, self.sems_0, self.sems_1, self.here = to, sems_0, sems_1, set()
        core = lax.axis_index("core")
        for r in range(2):
            mine = pieces[5 * r : 5 * r + 5]
            for yh in range(2):

                @pl.when(core == r)
                def _():
                    for k in range(4):
                        z = behind("z", k)
                        for i in range(4):
                            x = behind("x", i)
                            pltpu.make_async_copy(
                                entry(mine, i, k, k > 1).at[yh * 2 + layer],
                                to.at[yh, z, x, 0],
                                sems_0.at[yh, z, x],
                            ).start()

            for k in range(4):
                ys = behind(Y, k)

                @pl.when(jnp.logical_and(core == 1 - r, lax.rem(ys, 2) == layer))
                def _():
                    for i in range(4):
                        x = behind("x", i)
                        pltpu.make_async_copy(
                            entry(mine, i, k, k > 1), to.at[ys // 2, :, x, 1], sems_1.at[ys // 2, x]
                        ).start()

    def wait(self):
        for j in range(4):
            self.get(j)

    def get(self, j):
        yh, first = j // 2, (j % 2) * 2
        for x in range(0 if j in self.here else 4):
            for z in (first, first + 1):
                here = self.to.at[yh, z, x, 0]
                pltpu.make_async_copy(here, here, self.sems_0.at[yh, z, x]).wait()
            if first == 0:
                here = self.to.at[yh, :, x, 1]
                pltpu.make_async_copy(here, here, self.sems_1.at[yh, x]).wait()
        self.here.add(j)
        return self.to[yh, first : first + 2].reshape(D, D)


class Out:
    def __init__(self, sems):
        self.sems, self.copies, self.count = sems, [], 0

    def put(self, source, to):
        copy = pltpu.make_async_copy(source, to, self.sems.at[self.count])
        copy.start()
        self.copies.append(copy)
        self.count += 1

    def put_either(self, source, of_first, of_second, first):
        sem, rows = self.sems.at[self.count], pl.ds(first, source.shape[0])
        for core, ref in enumerate((of_first, of_second)):

            @pl.when(lax.axis_index("core") == core)
            def _():
                pltpu.make_async_copy(source, ref.at[rows, :], sem).start()

        self.copies.append(pltpu.make_async_copy(source, of_first.at[rows, :], sem))
        self.count += 1

    def drain(self):
        for copy in self.copies:
            copy.wait()


WA = pltpu.VMEM((4, D, D), BF)
WC = pltpu.VMEM((2, 4, 4, 2, 48, D), BF)
FOUR = pltpu.VMEM((4, BLOCK, D), BF)


def dma(*count):
    return pltpu.SemaphoreType.DMA(count)


def dot(left, right):
    return lax.dot_general(left, right, (((1,), (0,)), ((), ())), preferred_element_type=F32)


def dot_nt(left, right):
    return lax.dot_general(left, right, (((1,), (1,)), ((), ())), preferred_element_type=F32)


def dot_tn(left, right):
    return lax.dot_general(left, right, (((0,), (0,)), ((), ())), preferred_element_type=F32)


def norm_of(residual):
    centre = residual - jnp.mean(residual, axis=1, keepdims=True)
    scaled = lax.rsqrt(jnp.mean(centre * centre, axis=1, keepdims=True) + EPS)
    return centre * scaled, scaled


def norm_back(grad_out, normed, scaled, gain):
    grad_normed = grad_out * gain
    inner = (
        grad_normed
        - jnp.mean(grad_normed, axis=1, keepdims=True)
        - normed * jnp.mean(grad_normed * normed, axis=1, keepdims=True)
    )
    return (
        scaled * inner,
        jnp.sum(grad_out * normed, axis=0, keepdims=True),
        jnp.sum(grad_out, axis=0, keepdims=True),
    )


def head_masks():
    lane = lax.broadcasted_iota(jnp.int32, (BLOCK, 128), 1)
    return lane < 64


def vector_rows(vraw, out):
    groups = [vraw[yh, z][0:8, :256].astype(F32) for yh in range(2) for z in range(4)]
    values = jnp.concatenate(groups, axis=0).astype(BF)
    lane = lax.broadcasted_iota(jnp.int32, (64, D), 1)
    device = lax.broadcasted_iota(jnp.int32, (64, D), 0)

    def rows(start, width, count):
        found = []
        for r in range(count):
            spread = jnp.where(device == (lane + r * D) // width, 1.0, 0.0).astype(BF)
            wide = dot_tn(values[:, start : start + width], spread)
            entry = lax.broadcasted_iota(jnp.int32, wide.shape, 0)
            at = lax.broadcasted_iota(jnp.int32, wide.shape, 1) + r * D
            found.append(
                jnp.sum(jnp.where(entry == at % width, wide, 0.0), axis=0, keepdims=True)
            )
        return found

    found = rows(0, 24, 2)
    for start in (24, 36, 48):
        found += rows(start, 12, 1)
    found += rows(60, 48, 4)
    for start in (108, 120, 132):
        found += rows(start, 12, 1)
    out[...] = jnp.concatenate(found + [jnp.zeros((4, D), F32)], axis=0)


def column_sum(values):
    return jnp.sum(values.astype(F32), axis=0, keepdims=True)


def attention_forward(u, joined, vec, weights, qkv, probs, both, normed, scaled, attended):
    q = ((dot(u, weights.get(0)) + vec[0:1]) * 0.125).astype(BF)
    k = dot(u, weights.get(1)).astype(BF)
    v = (dot(u, weights.get(2)) + vec[1:2]).astype(BF)
    qkv[0] = q
    qkv[1] = k
    qkv[2] = v
    low_half = head_masks()
    for pair in range(HEADS // 2):
        lanes = slice(pair * 128, pair * 128 + 128)
        q2, k2, v2 = q[:, lanes], k[:, lanes], v[:, lanes]
        outs = []
        for h in range(2):
            mine = low_half if h == 0 else jnp.logical_not(low_half)
            scores = dot_nt(jnp.where(mine, q2, jnp.zeros_like(q2)), k2)
            scores = jnp.where(joined, scores, -1e30)
            top = jnp.max(scores, axis=1, keepdims=True)
            exponent = jnp.exp(scores - top)
            total = jnp.sum(exponent, axis=1, keepdims=True)
            rows = (exponent / total).astype(BF)
            probs[2 * pair + h] = rows
            outs.append(dot(rows, v2))
        both[1, :, lanes] = jnp.where(low_half, outs[0], outs[1]).astype(BF)
    attended()
    branch = dot(both[1], weights.get(3)) + vec[2:3]
    n1, s1 = norm_of(u.astype(F32) + branch)
    normed[...] = n1
    scaled[...] = jnp.broadcast_to(s1, (BLOCK, 128))
    return (n1 * vec[3:4] + vec[4:5]).astype(BF)


def ffn_forward(hidden, vec, expand, contract, act, slope, normed, scaled):
    expand.wait()
    contract.wait()
    for j in range(4):
        pre = dot(hidden, expand.get(j)) + vec[5 + j : 6 + j]
        half = 0.5 * (1.0 + lax.erf(pre * 0.7071067811865476))
        act[j] = (pre * half).astype(BF)
        slope[j] = (half + pre * jnp.exp(-0.5 * pre * pre) * 0.3989422804014327).astype(BF)
    total = hidden.astype(F32) + vec[9:10]
    for j in range(4):
        total = total + dot(act[j], contract.get(j))
    n2, s2 = norm_of(total)
    normed[...] = n2
    scaled[...] = jnp.broadcast_to(s2, (BLOCK, 128))
    return n2 * vec[10:11] + vec[11:12]


def ffn_backward(grad, vec, n2, s2, slope, expand, contract, vecs, dffn_ref, dpre_ref):
    dr2, dgain, dshift = norm_back(grad, n2[...], s2[:, 0:1], vec[10:11])
    dffn = dr2.astype(BF)
    dffn_ref[...] = dffn
    vecs[...] = jnp.zeros((16, D), F32)
    vecs[9:10] = column_sum(dffn)
    vecs[10:11] = dgain
    vecs[11:12] = dshift
    for j in range(4):
        dact = dot_nt(dffn, contract.get(j))
        dpre = (dact * slope[j].astype(F32)).astype(BF)
        dpre_ref[j] = dpre
        vecs[5 + j : 6 + j] = column_sum(dpre)
    total = dr2
    for j in range(4):
        total = total + dot_nt(dpre_ref[j], expand.get(j))
    return total


def attention_backward(dhidden, vec, n1, s1, qkv, probs, weights, vecs, parts, head, ready):
    dr1, dgain, dshift = norm_back(dhidden, n1[...], s1[:, 0:1], vec[3:4])
    parts[3] = dr1.astype(BF)
    dattended = dot_nt(parts[3], weights.get(3)).astype(BF)
    ready()
    low_half = head_masks()
    for pair in range(HEADS // 2):
        lanes = slice(pair * 128, pair * 128 + 128)
        q2, k2, v2 = qkv[0, :, lanes], qkv[1, :, lanes], qkv[2, :, lanes]
        do2 = dattended[:, lanes]
        dqs = []
        dk2 = jnp.zeros((BLOCK, 128), F32)
        dv2 = jnp.zeros((BLOCK, 128), F32)
        for h in range(2):
            mine = low_half if h == 0 else jnp.logical_not(low_half)
            do_h = jnp.where(mine, do2, jnp.zeros_like(do2))
            rows_low = probs[2 * pair + h]
            rows = rows_low.astype(F32)
            dprobs = dot_nt(do_h, v2)
            dscores = (
                rows * (dprobs - jnp.sum(rows * dprobs, axis=1, keepdims=True))
            ).astype(BF)
            dqs.append(dot(dscores, k2))
            dk2 = dk2 + dot_tn(dscores, jnp.where(mine, q2, jnp.zeros_like(q2)))
            dv2 = dv2 + dot_tn(rows_low, do_h)
        parts[0, :, lanes] = (jnp.where(low_half, dqs[0], dqs[1]) * 0.125).astype(BF)
        parts[1, :, lanes] = dk2.astype(BF)
        parts[2, :, lanes] = dv2.astype(BF)
    total = dr1
    for j in range(3):
        total = total + dot_nt(parts[j], weights.get(j))
    head[...] = jnp.concatenate(
        [column_sum(parts[0]), column_sum(parts[2]), column_sum(parts[3]), dgain, dshift, vecs[5:16]],
        axis=0,
    ).astype(BF)
    return total


INPUTS, OUTPUTS, ACT, DFFN, HEAD, ALL = 0, 512, 1536, 2048, 2304, 2320


def put_act(out, act, keep, send):
    core = lax.axis_index("core")
    for to, half in ((keep, core), (send, 1 - core)):
        for j in range(2):
            out.put(act.at[2 * half + j], to.at[pl.ds(ACT + j * BLOCK, BLOCK), :])


def put_dffn(out, dffn, keep, send):
    for to in (keep, send):
        out.put(dffn, to.at[pl.ds(DFFN, BLOCK), :])


def put_four(out, first, second, rows, four):
    for j in range(4):
        out.put_either(four.at[j], first, second, rows + j * BLOCK)


def wait_vectors(vraw, sems):
    for yh in range(2):
        for z in range(4):
            here = vraw.at[yh, z]
            pltpu.make_async_copy(here, here, sems.at[yh, z]).wait()


def middle_kernel(keep, seg, tokens, cotangent, *rest):
    pieces, pieces_c = rest[:10], rest[10:20]
    middle_o, last_o, passed_o, dhidden_o, vecs_o = rest[20:25]
    n1_0o, s1_0o, qkv_0o, probs_0o, vec0_o, keep0_o, send0_o, keep_o, send_o = rest[25:34]
    rest = rest[34:]
    u0, cot, sem_i, *rest = rest
    vraw0, hidden0, n1_0, s1_0, qkv_0, probs_0, both0, vec0 = rest[:8]
    we0, wc0, act0, slope0, n2_0, s2_0, dffn0, dhidden0, vecs0 = rest[8:17]
    wa, wb, wc, vraw, hidden, n1, s1, qkv, probs, both, vec = rest[17:28]
    act, slope, n2, s2, last, dpre, dffn, vecs, parts, head, passed = rest[28:39]
    sem_w0, sem_v0, sem_e0, sem_c0, sem_d0, sem_w, sem_v, sem_e, sem_c, sem_d, sem_o = rest[39:]
    out = Out(sem_o)
    rows = pl.ds(pl.multiple_of(lax.axis_index("section") * BLOCK, BLOCK), BLOCK)
    blocks = [
        pltpu.make_async_copy(source.at[rows, :], to, sem_i.at[i])
        for i, (source, to) in enumerate(((tokens, u0), (cotangent, cot)))
    ]
    for copy in blocks:
        copy.start()
    here = jnp.broadcast_to(seg[...].astype(F32), (BLOCK, BLOCK))
    joined = here == here.T
    weights0 = attention_chunks(0, pieces, wb, sem_w0, (0, 1, 2, 3), vraw0, sem_v0)
    expand0 = expand_chunks(0, pieces, we0, sem_e0)
    contract0 = Contract(0, pieces_c, wc0, sem_c0, sem_d0)
    weights = attention_chunks(1, pieces, wa, sem_w, (0, 1, 2, 3), vraw, sem_v)
    wait_all(blocks)
    both0[0] = u0[...]
    wait_vectors(vraw0, sem_v0)
    vector_rows(vraw0, vec0)
    out.put(vec0, vec0_o)

    def attended0():
        out.put(qkv_0, qkv_0o)
        out.put(probs_0, probs_0o)
        out.put_either(both0.at[0], keep0_o, send0_o, INPUTS)
        out.put_either(both0.at[1], keep0_o, send0_o, INPUTS + BLOCK)

    hidden0[...] = attention_forward(
        u0[...], joined, vec0, weights0, qkv_0, probs_0, both0, n1_0, s1_0, attended0
    )
    out.put(n1_0, n1_0o)
    out.put(s1_0, s1_0o)
    expand = expand_chunks(1, pieces, wb, sem_e)
    contract = Contract(1, pieces_c, wc, sem_c, sem_d)
    values = ffn_forward(hidden0[...], vec0, expand0, contract0, act0, slope0, n2_0, s2_0)
    before = len(out.copies)
    put_act(out, act0, keep0_o, send0_o)
    act0_copies, out.copies = out.copies[before:], out.copies[:before]
    for j in range(2):
        out.put_either(hidden0, send0_o, keep0_o, INPUTS + j * BLOCK)
    u = values.astype(BF)
    both[0] = u
    out.put(both.at[0], middle_o)
    wait_vectors(vraw, sem_v)
    vector_rows(vraw, vec)

    def attended():
        out.put_either(both.at[0], keep_o, send_o, INPUTS)
        out.put_either(both.at[1], keep_o, send_o, INPUTS + BLOCK)

    hidden[...] = attention_forward(u, joined, vec, weights, qkv, probs, both, n1, s1, attended)
    for j in range(2):
        out.put_either(hidden, send_o, keep_o, INPUTS + j * BLOCK)
    values = ffn_forward(hidden[...], vec, expand, contract, act, slope, n2, s2)
    put_act(out, act, keep_o, send_o)
    kept = keep[0] > 9
    last[...] = jnp.where(kept, values.astype(BF), both[0])
    out.put(last, last_o)
    grad = jnp.where(kept, cot[...].astype(F32), 0.0)
    grad = ffn_backward(grad, vec, n2, s2, slope, expand, contract, vecs, dffn, dpre)
    put_four(out, send_o, keep_o, OUTPUTS, dpre)
    put_dffn(out, dffn, keep_o, send_o)
    du = attention_backward(
        grad, vec, n1, s1, qkv, probs, weights, vecs, parts, head, lambda: None
    )
    put_four(out, keep_o, send_o, OUTPUTS, parts)
    out.put_either(head, keep_o, send_o, HEAD)
    passed[...] = jnp.where(kept, du.astype(BF), cot[...])
    out.put(passed, passed_o)
    wait_all(act0_copies)
    dhidden0[...] = ffn_backward(
        passed[...].astype(F32), vec0, n2_0, s2_0, slope0, expand0, contract0, vecs0, dffn0, act0
    )
    put_four(out, send0_o, keep0_o, OUTPUTS, act0)
    put_dffn(out, dffn0, keep0_o, send0_o)
    out.put(dhidden0, dhidden_o)
    out.put(vecs0, vecs_o)
    out.drain()


def ba_kernel(layer, dhidden, vecs, vec, n1, s1, qkv_i, probs_i, *rest):
    pieces = rest[:10]
    du_o, grads_o = rest[10:12]
    wa, parts, head, du, qkv, probs, sem_w, sem_i, sem_o = rest[12:]
    out = Out(sem_o)
    saved = [
        pltpu.make_async_copy(qkv_i, qkv, sem_i.at[0]),
        pltpu.make_async_copy(probs_i, probs, sem_i.at[1]),
    ]
    for copy in saved:
        copy.start()
    weights = attention_chunks(layer, pieces, wa, sem_w, (3, 0, 1, 2))
    du[...] = attention_backward(
        dhidden[...], vec, n1, s1, qkv, probs, weights, vecs, parts, head, lambda: wait_all(saved)
    ).astype(BF)
    for j in range(4):
        out.put(parts.at[j], grads_o.at[pl.ds(j * BLOCK, BLOCK), :])
    out.put(head, grads_o.at[pl.ds(4 * BLOCK, 16), :])
    out.put(du, du_o)
    out.drain()


def wait_all(copies):
    for copy in copies:
        copy.wait()


def slab_rows(scratch, which, blocks):
    rows = [scratch[pl.ds(pl.multiple_of(b * ROWS + which * 24, 8), 24), :] for b in blocks]
    return jnp.concatenate(rows, axis=0).astype(BF)


def wait_all(copies):
    for copy in copies:
        copy.wait()


def slab_rows(scratch, which, blocks):
    rows = [scratch[pl.ds(pl.multiple_of(b * ROWS + which * 24, 8), 24), :] for b in blocks]
    return jnp.concatenate(rows, axis=0).astype(BF)


def bring_both(keep, send, first, to, sems, count):
    return [
        pltpu.make_async_copy(
            ref.at[pl.ds(first, BLOCK), :], to.at[pl.ds(r * BLOCK, BLOCK), :], sems.at[count + r]
        )
        for r, ref in enumerate((keep, send))
    ]


def weights_kernel(layer, ins, *rest):
    x, d, act, dffn, head, grad, staged, staged_c, sem_i, sem_o = rest[8:]

    def of_layer(refs, far, rows):
        refs = [ref.at[pl.ds(layer * rows, rows), :] for ref in refs]
        return [refs[0], refs[1], far, refs[2]]

    outs, outs_c = of_layer(rest[:3], rest[6], 784), of_layer(rest[3:6], rest[7], 384)
    core = lax.axis_index("core")
    keep, got = ins[:2]

    def bring(first, to, count):
        return [
            pltpu.make_async_copy(
                ref.at[pl.ds(first, BLOCK), :], to.at[pl.ds(r * BLOCK, BLOCK), :], sem_i.at[count + r]
            )
            for r, ref in enumerate((keep, got))
        ]

    dffn_in = bring(DFFN, dffn, 0)
    act_in = [bring(ACT + j * BLOCK, act.at[j], 2 + 2 * j) for j in range(2)]
    x_in = [bring(INPUTS + j * BLOCK, x.at[j], 6 + 2 * j) for j in range(2)]
    d_in = [bring(OUTPUTS + j * BLOCK, d.at[j], 10 + 2 * j) for j in range(4)]
    for pair in (dffn_in, *act_in, *x_in):
        for copy in pair:
            copy.start()
    if len(ins) == 2:
        for pair in d_in:
            for copy in pair:
                copy.start()
        heads = [ref.at[pl.ds(HEAD, 16), :] for ref in ins]
    else:
        heads = [ref.at[pl.ds(4 * BLOCK, 16), :] for ref in ins[2:]]

        @pl.when(core == 1)
        def _():
            for pair in d_in:
                for copy in pair:
                    copy.start()

        @pl.when(core == 0)
        def _():
            for j in range(4):
                for r, ref in enumerate(ins[2:]):
                    pltpu.make_async_copy(
                        ref.at[pl.ds(j * BLOCK, BLOCK), :],
                        d.at[j, pl.ds(r * BLOCK, BLOCK), :],
                        sem_i.at[10 + 2 * j + r],
                    ).start()

    head_in = [
        pltpu.make_async_copy(ref, head.at[r], sem_i.at[18 + r]) for r, ref in enumerate(heads)
    ]
    for copy in head_in:
        copy.start()
    out = Out(sem_o)
    wait_all(dffn_in)
    for a in range(2):
        wait_all(act_in[a])
        grad[a] = dot_tn(act[a], dffn[...])
        for k in range(4):
            staged_c[k, a * 192 : (a + 1) * 192] = slab_rows(
                grad.at[a], lax.rem(position(Y) + k, 4), range(8)
            )
    for k in range(4):
        out.put(staged_c.at[k], outs_c[k])
    wait_all(head_in)
    vec = (head[0].astype(F32) + head[1].astype(F32)).astype(BF)
    wait_all(x_in[0] + x_in[1])
    for j in range(4):
        wait_all(d_in[j])
        here, of_j = slice(j * 192, (j + 1) * 192), grad.at[j % 2]
        of_j[...] = dot_tn(x[j // 3], d[j])

        @pl.when(core == 0)
        def _():
            for k in range(4):
                z = lax.rem(position("z") + k, 4)
                rows = [
                    of_j[pl.ds(pl.multiple_of((yh * 4 + z) * ROWS, 8), ROWS), :] for yh in range(2)
                ]
                staged[k, here] = jnp.concatenate(rows, axis=0).astype(BF)

        @pl.when(core == 1)
        def _():
            for k in range(4):
                staged[k, here] = slab_rows(of_j, lax.rem(position("x") + k, 4), range(8))

        if j % 2:
            for k in range(4):
                rows = pl.ds((j - 1) * 192, 384)
                out.put(staged.at[k, rows, :], outs[k].at[rows, :])
    for k in range(4):
        staged[k, 768:784] = vec
        rows = pl.ds(768, 16)
        out.put(staged.at[k, rows, :], outs[k].at[rows, :])
    out.drain()


def sum_parts(parts, to):
    rows = to.shape[0]
    step = 16 * max(n for n in range(1, 13) if rows % (16 * n) == 0)

    @pl.loop(0, rows // step)
    def _(i):
        here = pl.ds(pl.multiple_of(i * step, 16), step)
        total = parts[0][here, :].astype(F32)
        for part in parts[1:]:
            total = total + part[here, :].astype(F32)
        to[here, :] = total


def pick_rows(total, starts, count):
    rows = [total[pl.ds(pl.multiple_of(start, 8), count), :] for start in starts]
    return jnp.concatenate(rows, axis=0).astype(BF)


def pass_on_kernel(*refs):
    got, sums, semaphores = refs[4:8], refs[8:12], refs[16]
    rows = [pl.ds(0 if i % 2 == 0 else got[i].shape[0], got[i].shape[0]) for i in range(4)]
    held = refs[12:16]
    copies = [
        pltpu.make_async_copy(sums[i].at[rows[i], :], held[i], semaphores.at[i]) for i in range(4)
    ]
    for copy in copies:
        copy.start()
    out = Out(semaphores)
    out.count = 4
    for i in range(4):
        copies[i].wait()
        held[i][...] = (held[i][...].astype(F32) + got[i][...].astype(F32)).astype(BF)
        out.put(held[i], sums[i].at[rows[i], :])
    out.drain()


def second_cut_kernel(*refs):
    parts, parts_c = refs[:3], refs[3:6]
    outs, outs_c = refs[6:10], refs[10:14]
    total, total_c = refs[14:]
    core = lax.axis_index("core")
    sum_parts(parts_c, total_c)
    for k in range(4):
        x = lax.rem(position("x") + k, 4)
        starts = [layer * 384 + (z * 4 + x) * 24 for layer in range(2) for z in range(4)]
        outs_c[k][...] = pick_rows(total_c, starts, 24)
    sum_parts(parts, total)

    @pl.when(core == 0)
    def _():
        for k in range(4):
            y = lax.rem(position(Y) + k, 4)
            first = lax.rem(y, 2) * 384 + (y // 2) * ROWS
            starts = [layer * 784 + first + j * 192 for layer in range(2) for j in range(2)]
            outs[k][0:384] = pick_rows(total, starts, ROWS)
            outs[k][384:416] = pick_rows(total, (768, 784 + 768), 16)

    @pl.when(core == 1)
    def _():
        for k in range(4):
            z = lax.rem(position("z") + k, 4)
            starts = [
                layer * 784 + j * 192 + (yh * 4 + z) * 24
                for layer in range(2)
                for j in range(4)
                for yh in range(2)
            ]
            outs[k][0:384] = pick_rows(total, starts, 24)
            outs[k][384:416] = jnp.zeros((32, D), BF)


def third_cut_kernel(*refs):
    parts, parts_c = refs[:4], refs[4:8]
    outs, outs_c = refs[8:12], refs[12:16]
    total, total_c = refs[16:]
    core = lax.axis_index("core")
    sum_parts(parts_c, total_c)
    for k in range(4):
        z = lax.rem(position("z") + k, 4)
        outs_c[k][...] = pick_rows(total_c, [layer * 96 + z * 24 for layer in range(2)], 24)
    sum_parts(parts, total)

    @pl.when(core == 0)
    def _():
        for k in range(4):
            x = lax.rem(position("x") + k, 4)
            starts = [(layer * 2 + j) * ROWS + x * 24 for layer in range(2) for j in range(2)]
            outs[k][0:96] = pick_rows(total, starts, 24)
            outs[k][96:128] = total[384:416, :].astype(BF)

    @pl.when(core == 1)
    def _():
        for k in range(4):
            y = lax.rem(position(Y) + k, 4)
            first = lax.rem(y, 2) * 96 + (y // 2) * 24
            starts = [layer * 192 + first + j * 48 for layer in range(2) for j in range(2)]
            outs[k][0:96] = pick_rows(total, starts, 24)
            outs[k][96:128] = jnp.zeros((32, D), BF)


def finish_kernel(place, here, far, near, far_near, own, iw, ib, ow, ob, fg, fs, ew, eb, cb, sg, ss):
    at, core, section = place[0], lax.axis_index("core"), lax.axis_index("section")
    vectors = jnp.where(core == 0, own[...], near[24:40])
    pairs = []
    for which in range(2):
        for pair in range(2):
            for j in range(2):
                mine = jnp.where(section == pair, here[j], far[j])
                theirs = jnp.where(section == pair, near[j * 12 : j * 12 + 12], far_near[j])
                pairs.append(jnp.where(core == which, mine, theirs))

    def cut(start):
        lane = lax.broadcasted_iota(jnp.int32, (D, 128), 0)
        to = lax.broadcasted_iota(jnp.int32, (D, 128), 1)
        return lax.dot_general(
            vectors,
            jnp.where(lane == to + start, 1.0, 0.0),
            (((1,), (0,)), ((), ())),
            precision=lax.Precision.HIGHEST,
            preferred_element_type=F32,
        )

    for ref, which, chunks in ((iw, 0, (0, 1, 2)), (ow, 0, (3,)), (ew, 1, (0, 1, 2, 3))):
        tiles = len(chunks) * 6
        for i, chunk in enumerate(chunks):
            for t in range(6):
                ref[pl.ds(i * 6 + t, 12, stride=tiles), :] = pairs[which * 4 + chunk][
                    :, t * 128 : t * 128 + 128
                ]
    rows = cut(at * 12)
    for ref, row in ((ob, 2), (fg, 3), (fs, 4), (cb, 9), (sg, 10), (ss, 11)):
        ref[...] = rows[row : row + 1, :12]
    rows = cut(lax.rem(at, 32) * 24)
    ib[...] = jnp.where(at < 32, rows[0:1], rows[1:2])[:, :24]
    rows = cut(lax.rem(at, 16) * 48)
    which = at // 16
    eb[...] = jnp.where(
        which < 2,
        jnp.where(which == 0, rows[5:6], rows[6:7]),
        jnp.where(which == 2, rows[7:8], rows[8:9]),
    )[:, :48]


def pack_kernel(iw, ib, ow, ob, fg, fs, ew, eb, cw, cb, sg, ss, own, contract, scratch):
    scratch[96:104] = jnp.zeros((8, D), F32)
    for j in range(8):
        ref, first, tiles = (iw, j * 6, 18) if j < 3 else (ow, 0, 6)
        if j > 3:
            ref, first, tiles = ew, (j - 4) * 6, 24
        for t in range(6):
            scratch[j * 12 : (j + 1) * 12, t * 128 : t * 128 + 128] = ref[
                pl.ds(first + t, 12, stride=tiles), :
            ]
    start = 0
    for ref in (ib, ob, fg, fs, eb, cb, sg, ss):
        width = ref.shape[1]
        scratch[96:97, start : start + width] = ref[...]
        start += width
    own[...] = scratch[...].astype(BF)
    contract[...] = cw[0].astype(BF)


def shape(*dims, dtype=F32):
    return jax.ShapeDtypeStruct(dims, dtype)


def call(kernel, outs, args, in_hbm=0, scratch=(), name="kernel", outs_hbm=True, smem=0, limit=60, aliases=None):
    here = len(args) - in_hbm - smem
    in_specs = [pl.BlockSpec(memory_space=pltpu.SMEM)] * smem
    in_specs += [pl.BlockSpec(memory_space=pltpu.VMEM)] * here
    in_specs += [pl.BlockSpec(memory_space=pl.ANY)] * in_hbm
    out_space = pl.ANY if outs_hbm else pltpu.VMEM
    return pl.pallas_call(
        kernel,
        out_shape=outs,
        in_specs=in_specs,
        out_specs=[pl.BlockSpec(memory_space=out_space)] * len(outs),
        scratch_shapes=list(scratch),
        compiler_params=pltpu.CompilerParams(vmem_limit_bytes=limit * 1024 * 1024),
        cost_estimate=pl.CostEstimate(flops=1000, bytes_accessed=1024, transcendentals=0),
        input_output_aliases=aliases or {},
        name=name,
    )(*args)


ROWS_BF = shape(BLOCK, D, dtype=BF)
ROWS_F32 = shape(BLOCK, D)
SCALE = shape(BLOCK, 128)
QKV = shape(3, BLOCK, D, dtype=BF)
PROBS = shape(HEADS, BLOCK, BLOCK, dtype=BF)
SLOPE = shape(4, BLOCK, D, dtype=BF)
TWO = shape(2, BLOCK, D, dtype=BF)
THREE = shape(3, BLOCK, D, dtype=BF)
VECS = shape(16, D)
DA = shape(528, D, dtype=BF)


def vmem(*shapes):
    return [pltpu.VMEM(each.shape, each.dtype) for each in shapes]


HEAD_BF = shape(16, D, dtype=BF)
VRAW = shape(2, 4, 16, D, dtype=BF)


def middle_part(depth, tokens, seg, cotangent, pieces, pieces_c):
    saved = [ROWS_F32, SCALE, QKV, PROBS]
    gather_sems = [dma(4, 8), dma(2, 4), dma(4, 8), dma(2, 4, 4), dma(2, 4)]
    return call(
        middle_kernel,
        [ROWS_BF, ROWS_BF, ROWS_BF, ROWS_F32, VECS, *saved, VECS]
        + [shape(HEAD, D, dtype=BF)] * 2
        + [shape(ALL, D, dtype=BF)] * 2,
        [depth, seg[None, :], tokens, cotangent, *pieces, *pieces_c],
        22,
        [*vmem(ROWS_BF, ROWS_BF), dma(2), *vmem(VRAW, ROWS_BF, *saved, TWO, VECS)]
        + [WA, WC, FOUR, *vmem(SLOPE, ROWS_F32, SCALE, ROWS_BF, ROWS_F32, VECS)]
        + [WA, WA, WC, *vmem(VRAW, ROWS_BF, *saved, TWO, VECS)]
        + [FOUR, *vmem(SLOPE, ROWS_F32, SCALE, ROWS_BF)]
        + [FOUR, *vmem(ROWS_BF, VECS), FOUR, *vmem(HEAD_BF, ROWS_BF)]
        + gather_sems
        + gather_sems
        + [dma(56)],
        name="middle",
        smem=1,
    )


def first_attention_backward(dhidden, vecs, vec, n1, s1, qkv, probs, pieces):
    return call(
        lambda *refs: ba_kernel(0, *refs),
        [ROWS_BF, shape(4 * BLOCK + 16, D, dtype=BF)],
        [dhidden, vecs, vec, n1, s1, qkv, probs, *pieces],
        12,
        [WA, FOUR, *vmem(HEAD_BF, ROWS_BF, QKV, PROBS), dma(4, 8), dma(2), dma(16)],
        name="attention_backward_0",
    )


def layer_weights(layer, args, before=()):
    count = len(before)

    def kernel(*refs):
        weights_kernel(layer, refs[count : count + len(args)], *refs[count + len(args) :])

    def both_cores(parts):
        return pltpu.VMEM((parts, 2 * BLOCK, D), BF)

    return call(
        kernel,
        [shape(1568, D, dtype=BF)] * 3
        + [shape(768, D, dtype=BF)] * 3
        + [shape(784, D, dtype=BF), shape(384, D, dtype=BF)],
        list(before) + args,
        count + len(args),
        [both_cores(2), both_cores(4), both_cores(2), pltpu.VMEM((2 * BLOCK, D), BF)]
        + [pltpu.VMEM((2, 16, D), BF), pltpu.VMEM((2, D, D), F32)]
        + [pltpu.VMEM((4, 784, D), BF), pltpu.VMEM((4, 384, D), BF), dma(20), dma(16)],
        name=f"weights_{layer}",
        aliases={i: i for i in range(count)},
    )


def pass_on(sums, got):
    kept = [pltpu.VMEM(each.shape, BF) for each in got]
    return call(
        lambda *refs: pass_on_kernel(*refs[4:8], *refs[:4], *refs[8:]),
        [shape(*each.shape, dtype=BF) for each in sums],
        [*got, *sums],
        4,
        kept + [dma(8)],
        name="pass_on",
        aliases={4 + i: i for i in range(4)},
    )


def cut_again(kernel, parts, parts_c, rows, rows_c, name, limit):
    outs = call(
        kernel,
        [shape(rows, D, dtype=BF)] * 4 + [shape(rows_c, D, dtype=BF)] * 4,
        [*parts, *parts_c],
        0,
        [pltpu.VMEM(parts[0].shape, F32), pltpu.VMEM(parts_c[0].shape, F32)],
        name=name,
        outs_hbm=False,
        limit=limit,
    )
    return outs[:4], outs[4:]


def gather(masters):
    core = lax.axis_index("core")
    own, contract = call(
        pack_kernel,
        [shape(104, D, dtype=BF), shape(48, D, dtype=BF)],
        [each.reshape(-1, 128) if i in (0, 2, 6) else each for i, each in enumerate(masters)],
        0,
        [pltpu.VMEM((104, D), F32)],
        name="pack",
        outs_hbm=False,
    )
    own = from_behind(own, "x")
    contract, own = lax.optimization_barrier((contract, own))
    contract = [contract] + [ahead_by_core(contract, k, "y", "z") for k in (1, 2, 3)]
    contract = by_position(contract, jnp.where(core == 0, position(Y), position("z")))
    contract = [contract] + [ahead_by_core(contract, k, "z", "y") for k in (1, 2, 3)]
    along_x = by_position(own, position("x"))
    other = swap_core(along_x)
    first, second = jnp.where(core == 0, along_x, other), jnp.where(core == 0, other, along_x)
    both = jnp.stack([first, second])
    chunks = both[:, :, :96].reshape(2, 4, 8, 12, D).transpose(2, 1, 0, 3, 4).reshape(8, ROWS, D)
    vector = both[:, :, 96].transpose(1, 0, 2).reshape(8, D)
    chunks = lax.dynamic_slice_in_dim(chunks, 4 * core, 4, 0).reshape(384, D)
    load = jnp.concatenate([chunks, vector, jnp.zeros((8, D), BF)], axis=0)
    load = jnp.stack([load] + [ahead_by_core(load, k, "y", "z") for k in (1, 2, 3)])
    contract = jnp.stack(contract)
    load, contract = lax.optimization_barrier((load, contract))
    near = [ahead_by_core(load, k, "z", "y") for k in (1, 3)]
    near_c = [ahead(contract, "x", k) for k in (1, 3)]
    other = swap_core(load)
    other_c = swap_core(lax.optimization_barrier((contract, other))[0])
    near, near_c, other, other_c = lax.optimization_barrier((near, near_c, other, other_c))
    far = [ahead_by_core(near[0][:2], 1, "z", "y"), ahead_by_core(near[1][2:], 3, "z", "y")]
    far_c = [ahead(near_c[0][:2], "x", 1), ahead(near_c[1][2:], "x", 3)]
    early = swap_core(near[0])
    far, far_c, early, near, near_c = lax.optimization_barrier((far, far_c, early, near, near_c))
    other = [other, early] + [swap_core(piece) for piece in (near[1], *far)]
    other_c = [other_c] + [swap_core(piece) for piece in (*near_c, *far_c)]
    return [load, *near, *far, *other], [contract, *near_c, *far_c, *other_c]


def summed(pieces):
    total = pieces[0].astype(F32)
    for piece in pieces[1:]:
        total = total + piece.astype(F32)
    return total


def scatter_ahead(pieces, axis):
    return [pieces[0]] + [ahead(pieces[k], axis, k) for k in (1, 2, 3)]


def crossed_ahead(pieces, first, second):
    return [pieces[0]] + [ahead_by_core(pieces[k], k, first, second) for k in (1, 2, 3)]


def reduce_gradients(parts, parts_c, far, far_c):
    section, core = lax.axis_index("section"), lax.axis_index("core")
    got = [ahead_by_core(far[0], 1, "z", "x"), ahead_by_core(far[1], 3, "z", "x")]
    got += [ahead(far_c[0], Y, 1), ahead(far_c[1], Y, 3)]
    sums = pass_on([*parts[1:], *parts_c[1:]], got)
    near = [ahead_by_core(sums[0], 1, "z", "x"), ahead_by_core(sums[1], 3, "z", "x")]
    near_c = [ahead(sums[2], Y, 1), ahead(sums[3], Y, 3)]
    parts, parts_c = [parts[0], *near], [parts_c[0], *near_c]
    parts, parts_c = cut_again(second_cut_kernel, parts, parts_c, 416, 192, "second_cut", 20)
    near = [ahead_by_core(parts[k], k, "y", "z") for k in (1, 3)]
    near_c = [ahead(parts_c[k], "x", k) for k in (1, 3)]
    parts, parts_c, near, near_c = lax.optimization_barrier((parts, parts_c, near, near_c))
    far, far_c = ahead_by_core(parts[2], 2, "y", "z"), ahead(parts_c[2], "x", 2)
    parts, parts_c = [parts[0], *near, far], [parts_c[0], *near_c, far_c]
    parts, parts_c = cut_again(third_cut_kernel, parts, parts_c, 128, 48, "third_cut", 20)
    parts, parts_c = crossed_ahead(parts, "x", "y"), scatter_ahead(parts_c, "z")
    parts, parts_c = lax.optimization_barrier((parts, parts_c))
    total, total_c = summed(parts), summed(parts_c).reshape(2, 24, D)

    def of_layer(value, which):
        return lax.dynamic_index_in_dim(value, which, 0, keepdims=False)

    vectors = of_layer(total[96:].reshape(2, 16, D), section)
    total = total[:96].reshape(2, 2, 24, D)
    mine, others = [
        [of_layer(total, which), of_layer(total_c, which)] for which in (section, 1 - section)
    ]
    near, far = crossed_owner(mine[1], False), crossed_owner(others[1], True)
    contract = jnp.concatenate(
        [jnp.where(section == 0, near, far), jnp.where(section == 0, far, near)]
    )
    mine, others = mine[0].reshape(2, 2, 12, D), others[0].reshape(2, 2, 12, D)

    def rows_of(value, which):
        return lax.dynamic_index_in_dim(value, which, 1, keepdims=False)

    here = rows_of(mine, core)
    near = rows_of(mine, 1 - core).reshape(24, D)
    near = to_neighbour(jnp.concatenate([near, vectors], axis=0), False, True)
    far = to_neighbour(rows_of(others, core), True, False)
    far_near = to_neighbour(rows_of(others, 1 - core), True, True)
    return (here, far, near, far_near, vectors), contract


def to_neighbour(value, other_section, other_core):
    pairs = []
    for s in range(2):
        for c in range(2):
            to = (1 - s if other_section else s) * 2 + (1 - c if other_core else c)
            pairs.append((s * 2 + c, to))
    return lax.ppermute(value, ("section", "core"), pairs)


def crossed_owner(value, other_section):
    pairs = []
    for s in range(2):
        for yh in range(2):
            for c in range(2):
                to = 1 - s if other_section else s
                pairs.append(((s * 2 + yh) * 2 + c, (to * 2 + c) * 2 + yh))
    return lax.ppermute(value, ("section", "yh", "core"), pairs)


def on_device(tokens, segment_ids, depth, *rest):
    masters = rest[:12]
    cotangent = rest[12]
    section = lax.axis_index("section")
    place = (
        lax.axis_index("yh") * 32
        + lax.axis_index("z") * 8
        + lax.axis_index("x") * 2
        + lax.axis_index("core")
    )
    seg = lax.dynamic_slice_in_dim(segment_ids, section * BLOCK, BLOCK, 0)

    def chosen(middle, last, first, passed):
        return jnp.where(section == 0, jnp.stack([middle, first]), jnp.stack([last, passed]))

    pieces, pieces_c = gather(masters)
    middle, last, passed, dhidden, vecs, *grads = middle_part(depth, tokens, seg, cotangent, pieces, pieces_c)
    *saved0, vec0, keep0, send0, keep1, send1 = grads
    first, grads0 = first_attention_backward(dhidden, vecs, vec0, *saved0, pieces)
    got1 = swap_core(send1)
    first, got1 = lax.optimization_barrier((first, got1))
    theirs = ahead(chosen(last, middle, passed, first), "section", 1)
    *sums, far1, far1_c = layer_weights(1, [keep1, got1])
    far1 = (far1, far1_c)
    got0, got_a = swap_core(send0), lax.ppermute(grads0, "core", [(1, 0)])
    sums, got0, got_a = lax.optimization_barrier((sums, got0, got_a))
    sums = layer_weights(0, [keep0, got0, grads0, got_a], sums)
    theirs, sums = lax.optimization_barrier((theirs, sums))
    ends, cw = reduce_gradients(
        sums[:3], sums[3:6], (sums[6], far1[0]), (sums[7], far1[1])
    )
    mine = chosen(middle, last, first, passed)
    low, high = jnp.where(section == 0, mine, theirs), jnp.where(section == 0, theirs, mine)
    layer_outputs, input_grads = jnp.concatenate([low, high], axis=1)[:, None]
    one, small = shape(1, 12), [shape(1, 24), shape(1, 48)]
    iw, ib, ow, ob, fg, fs, ew, eb, cb, sg, ss = call(
        finish_kernel,
        [shape(216, 128), small[0], shape(72, 128), one, one, one, shape(288, 128), small[1]]
        + [one, one, one],
        [place[None], *ends],
        smem=1,
        name="finish",
        outs_hbm=False,
    )
    return (
        layer_outputs,
        input_grads,
        iw.reshape(1, 12, 3 * D),
        ib,
        ow.reshape(1, 12, D),
        ob,
        fg,
        fs,
        ew.reshape(1, 12, 4 * D),
        eb,
        cw[None],
        cb,
        sg,
        ss,
    )


def solution(mesh):
    wide = Mesh(mesh.devices.reshape(2, 2, 4, 4, 2), ("section", "yh", "z", "x", "core"))
    dp = ("yh", "z", "x", "core")
    matrix, vector = P("section", dp, None), P("section", dp)
    rows = P(dp, None)
    weights = (
        matrix,
        vector,
        matrix,
        vector,
        vector,
        vector,
        matrix,
        vector,
        matrix,
        vector,
        vector,
        vector,
    )
    return jax.shard_map(
        on_device,
        mesh=wide,
        in_specs=(rows, P(dp), P(dp)) + weights + (rows,),
        out_specs=(matrix, matrix) + weights,
        check_vma=False,
    )
```
